32 devices in a mesh: dp: 16 (over z, y, x), tensor: 2 (over core).
Axes of the slice: x: 2, y: 2, z: 4, core: 2. Of those that a mesh axis runs over, the one named last changes fastest.
Arguments:
- mixer_input: bfloat16 [192, 768, 196], P('dp', 'tensor'), may hold values from -6 to 6
- keep_mask: int32 [192, 196], P('dp'), may hold values from 0 to 1, as said below
- ln_gain: bfloat16 [2, 768], P(None, 'dp'), may hold values from 0.25 to 1.75
- ln_shift: bfloat16 [2, 768], P(None, 'dp'), may hold values from -3 to 3
- token_w1: bfloat16 [196, 384], P(None, 'dp'), may hold values from -0.4375 to 0.4375
- token_b1: bfloat16 [384], P('dp'), may hold values from -3 to 3
- token_w2: bfloat16 [384, 196], P('dp'), may hold values from -0.3125 to 0.3125
- token_b2: bfloat16 [196], replicated, may hold values from -3 to 3
- chan_w1: bfloat16 [768, 3072], P(None, 'tensor'), may hold values from -0.21875 to 0.21875
- chan_b1: bfloat16 [3072], P('tensor'), may hold values from -3 to 3
- chan_w2: bfloat16 [3072, 768], P('tensor'), may hold values from -0.109375 to 0.109375
- chan_b2: bfloat16 [768], P('tensor'), may hold values from -3 to 3
- grad_out: bfloat16 [192, 768, 196], P('dp', 'tensor'), may hold values from -6 to 6
- grad_pooled: float32 [192, 768], P('dp', 'tensor'), may hold values from -18 to 18
Outputs:
- block_out: float32 [192, 768, 196], P('dp', 'tensor')
- pooled: float32 [192, 768], P('dp', 'tensor')
- grad_input: float32 [192, 768, 196], P('dp', 'tensor')
- grad_ln_gain: float32 [2, 768], P(None, 'dp')
- grad_ln_shift: float32 [2, 768], P(None, 'dp')
- grad_token_w1: float32 [196, 384], P(None, 'dp')
- grad_token_b1: float32 [384], P('dp')
- grad_token_w2: float32 [384, 196], P('dp')
- grad_token_b2: float32 [196], replicated
- grad_chan_w1: float32 [768, 3072], P('dp', 'tensor')
- grad_chan_b1: float32 [3072], P(('tensor', 'dp'))
- grad_chan_w2: float32 [3072, 768], P('tensor', 'dp')
- grad_chan_b2: float32 [768], P(('tensor', 'dp'))
- example_sq: float32 [192], P('dp')
The draws below stay inside these ranges and needn't reach their ends.
Inputs may be any that keep to these rules, and one draw needn't show every extreme that they name: `keep_mask`: each image keeps at least 49 of its patches.
All inputs are finite; a program needn't handle non-finite values.
Results may differ from the reference program's by a relative error of at most 0.03.
Values may be sent and summed in bfloat16 or wider, within the bound.
A program may use at most 192 MiB of HBM per device.

```python
import jax
import jax.numpy as jnp
from jax import lax

D = 768
S = 196
DS = 384
DC = 3072
IMG_DEV = 12
IMAGES = 192
N_TENSOR = 2


def draw_keep_mask(key, part):
    key = jax.random.fold_in(key, 11)
    keys = jax.random.split(key, IMAGES + 1)
    kept_count = jax.random.randint(keys[0], (IMAGES,), S // 4, S + 1)
    ranking = jax.vmap(lambda row_key: jax.random.permutation(row_key, S))(keys[1:])
    return (ranking < kept_count[:, None]).astype(jnp.int32)


def shard_levels(key, shape, cuts, low, high):
    def one(position, shards_of):
        heights = jax.random.uniform(jax.random.fold_in(jax.random.fold_in(key, 6), position), (shards_of,), jnp.float32, low / len(cuts), high / len(cuts))
        return jnp.repeat(jnp.exp(heights), shape[position] // shards_of).reshape((-1,) + (1,) * (len(shape) - position - 1))

    gain = one(*cuts[0])
    for cut in cuts[1:]:
        gain = gain * one(*cut)
    return gain


def normal_values(key, extent, width, reach, shards=(), held_as=jnp.bfloat16):
    values = jax.random.normal(key, extent, jnp.float32) * width
    if len(shards) > 0:
        values = shard_levels(key, extent, shards, -0.22, 0.18) * values
    return jnp.clip(values, min=-reach, max=reach).astype(held_as)


def setup_inputs(seed: int = 0) -> dict:
    streams_of = jax.random.split(jax.random.key(seed), 15)
    return {
        "mixer_input": normal_values(streams_of[0], (IMAGES, D, S), 1.0, 6.0, ((0, 16), (1, 2))),
        "keep_mask": draw_keep_mask(jax.random.fold_in(streams_of[14], 71), 0),
        "ln_gain": jnp.clip(1.0 + 0.15 * jax.random.normal(streams_of[2], (2, D), jnp.float32), 0.25, 1.75).astype(jnp.bfloat16),
        "ln_shift": normal_values(streams_of[3], (2, D), 0.5, 3.0, ((1, 16),)),
        "token_w1": normal_values(streams_of[4], (S, DS), S ** -0.5, 0.4375, ((1, 16),)),
        "token_b1": normal_values(streams_of[5], (DS,), 0.5, 3.0, ((0, 16),)),
        "token_w2": normal_values(streams_of[6], (DS, S), DS ** -0.5, 0.3125, ((0, 16),)),
        "token_b2": normal_values(streams_of[7], (S,), 0.5, 3.0),
        "chan_w1": normal_values(streams_of[8], (D, DC), D ** -0.5, 0.21875, ((1, 2),)),
        "chan_b1": normal_values(streams_of[9], (DC,), 0.5, 3.0, ((0, 2),)),
        "chan_w2": normal_values(streams_of[10], (DC, D), DC ** -0.5, 0.109375, ((0, 2),)),
        "chan_b2": normal_values(streams_of[11], (D,), 0.5, 3.0, ((0, 2),)),
        "grad_out": normal_values(streams_of[12], (IMAGES, D, S), 1.0, 6.0, ((0, 16), (1, 2))),
        "grad_pooled": normal_values(streams_of[13], (IMAGES, D), 3.0, 18.0, ((0, 16), (1, 2)), jnp.float32),
    }


@jax.custom_vjp
def low(v):
    return lax.optimization_barrier(v.astype(jnp.bfloat16)).astype(jnp.float32)

@jax.custom_vjp
def low_back(v):
    return v

def low_keep(v):
    return (low(v), None)

def low_pass(kept, grad):
    return (grad,)

def back_keep(v):
    return (v, None)

def back_low(kept, grad):
    return (low(grad),)
low.defvjp(low_keep, low_pass)
low_back.defvjp(back_keep, back_low)
epsilon = 1e-05
highest = lax.Precision.HIGHEST

def layer_norm(values, gains, shifts):
    average = lax.optimization_barrier(jnp.mean(values, axis=0, keepdims=True))
    centred = values - average
    spread = lax.optimization_barrier(jnp.mean(centred * centred, axis=0, keepdims=True))
    return centred * lax.rsqrt(spread + epsilon) * gains[:, None] + shifts[:, None]

def image_forward(weights, picture, kept):
    gains, shifts, token_in, token_bias, token_back, token_shift, chan_in, chan_bias, chan_back, chan_shift = weights
    normed_first = low(layer_norm(picture, gains[0], shifts[0]))
    token_pre = low_back(jnp.dot(normed_first, token_in, precision=highest) + token_bias[None, :])
    token_hid = low(jax.nn.gelu(token_pre, approximate=False))
    token_out = low_back(jnp.dot(token_hid, token_back, precision=highest) + token_shift[None, :])
    mixture = picture + token_out
    second = low(layer_norm(mixture, gains[1], shifts[1]))
    blocks = DC // N_TENSOR
    pieces = []
    for number in range(N_TENSOR):
        copied = low_back(second)
        columns = chan_in[:, number * blocks:(number + 1) * blocks]
        pieces.append(jnp.dot(columns.T, copied, precision=highest))
    chan_pre = low_back(jnp.concatenate(pieces, axis=0) + chan_bias[:, None])
    chan_hid = low(jax.nn.gelu(chan_pre, approximate=False))
    summed = jnp.zeros_like(mixture)
    for number in range(N_TENSOR):
        row_block = chan_back[number * blocks:(number + 1) * blocks]
        hid_block = chan_hid[number * blocks:(number + 1) * blocks]
        summed = summed + low(jnp.dot(row_block.T, hid_block, precision=highest))
    chan_out = low_back(summed + chan_shift[:, None])
    masked = kept[None, :] * (mixture + chan_out)
    pooled = lax.optimization_barrier(jnp.sum(masked, axis=1)) / jnp.sum(kept)
    return (masked, pooled)

def reference(mixer_input, keep_mask, ln_gain, ln_shift, token_w1, token_b1, token_w2, token_b2, chan_w1, chan_b1, chan_w2, chan_b2, grad_out, grad_pooled):
    weights = tuple((weight_item.astype(jnp.float32) for weight_item in (ln_gain, ln_shift, token_w1, token_b1, token_w2, token_b2, chan_w1, chan_b1, chan_w2, chan_b2)))

    def one_image(picture, kept, cot_out, cot_pool):

        def forward(params, source):
            return image_forward(params, source, kept)
        outputs, backward = jax.vjp(forward, weights, picture)
        weight_grads, picture_grad = backward((cot_out, cot_pool))
        squares = jnp.sum(jnp.square(weight_grads[6])) + jnp.sum(jnp.square(weight_grads[7]))
        squares = squares + jnp.sum(jnp.square(weight_grads[8])) + jnp.sum(jnp.square(weight_grads[9]))
        return (outputs[0], outputs[1], picture_grad, weight_grads, squares)

    def group_step(running, items):
        masked, pooled, picture_grad, weight_grads, squares = jax.vmap(one_image)(*items)
        running = tuple((running_sum + lax.optimization_barrier(jnp.sum(image_grads, axis=0)) for running_sum, image_grads in zip(running, weight_grads)))
        return (running, (masked, pooled, picture_grad, squares))
    groups = IMAGES // IMG_DEV
    items = (mixer_input.astype(jnp.float32).reshape(groups, IMG_DEV, D, S), keep_mask.astype(jnp.float32).reshape(groups, IMG_DEV, S), grad_out.astype(jnp.float32).reshape(groups, IMG_DEV, D, S), grad_pooled.astype(jnp.float32).reshape(groups, IMG_DEV, D))
    initial = tuple((jnp.zeros_like(weight_item) for weight_item in weights))
    totals, stacked = lax.scan(group_step, initial, items)
    block_out = stacked[0].reshape(IMAGES, D, S)
    pooled = stacked[1].reshape(IMAGES, D)
    grad_input = stacked[2].reshape(IMAGES, D, S)
    example_sq = stacked[3].reshape(IMAGES)
    return (block_out, pooled, grad_input, totals[0], totals[1], totals[2], totals[3], totals[4], totals[5], totals[6], totals[7], totals[8], totals[9], example_sq)
```

```python
import functools
import math

import jax
import jax.numpy as jnp
from jax import lax
from jax.experimental import pallas as pl
from jax.experimental.pallas import tpu as pltpu
from jax.sharding import PartitionSpec as P

MESH = pl.DeviceIdType.MESH
EPS = 1e-05
F32 = jnp.float32
BF16 = jnp.bfloat16
VM = pl.BlockSpec(memory_space=pltpu.VMEM)
ANY = pl.BlockSpec(memory_space=pl.ANY)
BLK = 256
VMEM_BYTES = 63 * 2**20


def up(n, m):
    return -(-n // m) * m


def nn(a, b):
    return lax.dot_general(a, b, (((1,), (0,)), ((), ())), preferred_element_type=F32)


def nt(a, b):
    return lax.dot_general(a, b, (((1,), (1,)), ((), ())), preferred_element_type=F32)


def tn(a, b):
    return lax.dot_general(a, b, (((0,), (0,)), ((), ())), preferred_element_type=F32)


def eye(rows, cols):
    r = lax.broadcasted_iota(jnp.int32, (rows, cols), 0)
    c = lax.broadcasted_iota(jnp.int32, (rows, cols), 1)
    return (r == c).astype(F32).astype(BF16)


def gelu_parts(v):
    cdf = 0.5 + 0.5 * lax.erf(v * math.sqrt(0.5))
    return cdf, jnp.exp(-0.5 * (v * v)) * (1.0 / math.sqrt(2.0 * math.pi))


def fold(v):
    return jnp.sum(v.reshape(v.shape[0] // 8, 8, v.shape[1]), 0)


def wide(v):
    return jnp.concatenate([v, v], axis=1)


def where_am_i():
    return lax.axis_index("dp"), lax.axis_index("tensor")


def greet_all(dp_size, dp, core):
    barrier = pltpu.get_barrier_semaphore()

    def one(n, c):
        pl.semaphore_signal(
            barrier, inc=1, device_id=(lax.rem(dp + n, dp_size), core), device_id_type=MESH
        )
        return c

    lax.fori_loop(1, dp_size, one, 0)
    pl.semaphore_signal(barrier, inc=1, device_id=(dp, 1 - core), device_id_type=MESH)
    pl.semaphore_wait(barrier, dp_size)


def remote(src, dst, send, recv, device):
    return pltpu.make_async_remote_copy(
        src_ref=src,
        dst_ref=dst,
        send_sem=send,
        recv_sem=recv,
        device_id=device,
        device_id_type=MESH,
    )


def front_kernel(
    dims,
    x_hbm,
    go_hbm,
    col_ref,
    w1_hbm,
    w2_hbm,
    b1_hbm,
    msg_ref,
    keep_ref,
    tb2_ref,
    st_o,
    yt_o,
    xp_o,
    f_o,
    hid_o,
    slope_o,
    mix_o,
    yp_o,
    stat_o,
    prm_o,
    colf_o,
    tw1_o,
    tw2_o,
    w1p_o,
    w2p_o,
    b1p_o,
    xf,
    gof,
    tok,
    wide_prm,
    colr,
    tmp_w,
    s_buf,
    tok_send,
    tok_recv,
    pair_send,
    pair_recv,
    loc_sem,
):
    n_dp, ni, ch, pat, tp, unit_d = dims
    dp, core = where_am_i()
    full = 2 * ch
    step = pl.program_id(0)
    other = (dp, 1 - core)
    mine = pl.ds(pl.multiple_of(core * ch, 128), ch)
    my_first = core * ni

    def pair_copies():
        return [
            remote(
                x_hbm.at[pl.ds((1 - core) * ni, ni)],
                xf.at[:, mine],
                pair_send.at[0],
                pair_recv.at[0],
                other,
            ),
            remote(
                go_hbm.at[pl.ds((1 - core) * ni, ni)],
                gof.at[:, mine],
                pair_send.at[1],
                pair_recv.at[1],
                other,
            ),
            remote(col_ref, colr.at[mine], pair_send.at[2], pair_recv.at[2], other),
            remote(w1_hbm, w1p_o, pair_send.at[3], pair_recv.at[3], other),
            remote(w2_hbm, w2p_o, pair_send.at[4], pair_recv.at[4], other),
            remote(b1_hbm, b1p_o, pair_send.at[5], pair_recv.at[5], other),
        ]

    def local_copies():
        return [
            pltpu.make_async_copy(
                x_hbm.at[pl.ds(my_first, ni)], xf.at[:, mine], loc_sem.at[0]
            ),
            pltpu.make_async_copy(
                go_hbm.at[pl.ds(my_first, ni)], gof.at[:, mine], loc_sem.at[1]
            ),
        ]

    def token_copy(n):
        return remote(
            msg_ref,
            tok.at[dp],
            tok_send.at[n],
            tok_recv.at[dp],
            (lax.rem(dp + n, n_dp), core),
        )

    def token_arrival(n):
        source = lax.rem(dp + n_dp - n, n_dp)
        return remote(
            msg_ref, tok.at[source], tok_send.at[n], tok_recv.at[source], (source, core)
        )

    @pl.when(step == 0)
    def _():
        for c in local_copies():
            c.start()
        greet_all(n_dp, dp, core)

        def send(n, c):
            token_copy(n).start()
            return c

        lax.fori_loop(1, n_dp, send, 0)
        for c in pair_copies():
            c.start()
        tok[dp] = msg_ref[...]
        colr[mine, :] = col_ref[...]
        for c in local_copies():
            c.wait()
        copies = pair_copies()
        for n in range(3):
            copies[n].wait_recv()

        colf_o[...] = colr[...]

        def arrive(n, c):
            token_arrival(n).wait_recv()
            return c

        lax.fori_loop(1, n_dp, arrive, 0)
        rows = unit_d
        lane = lax.broadcasted_iota(jnp.int32, (rows, pad_lanes(pat)), 1)
        for d in range(n_dp):
            block = tok[d].astype(F32)
            tmp_w[0, rows * d : rows * (d + 1), :] = jnp.where(
                lane <= pat, block[:rows], 0.0
            )
            tmp_w[1, rows * d : rows * (d + 1), :] = jnp.where(
                lane < pat, block[rows:], 0.0
            )
            prm_o[2 * rows * d : 2 * rows * (d + 1), :] = block[:, 128:256]
        tw1_o[...] = tmp_w[0].astype(BF16)
        tw2_o[...] = tmp_w[1].astype(BF16)
        for n in range(4):
            at = PRM_LANE - 128 + n
            wide_prm[n] = jnp.broadcast_to(prm_o[:, at : at + 1], (full, 128))

    image = step
    chunk = 64
    chunks = [slice(r, r + chunk) for r in range(0, full, chunk)]
    xp_o[0, :, 128:] = jnp.zeros((full, xp_o.shape[2] - 128), BF16)
    yp_o[0, :, 128:] = jnp.zeros((full, xp_o.shape[2] - 128), BF16)
    lanes = xp_o.shape[2]
    total = jnp.zeros((8, lanes), F32)
    square = jnp.zeros((8, lanes), F32)
    for r in chunks:
        xp_o[0, r, :pat] = xf[image, r, :]
        v = xp_o[0, r, :].astype(F32)
        total += fold(v)
        square += fold(v * v)
    mean0 = jnp.sum(total, 0, keepdims=True) / full
    rstd0 = lax.rsqrt(jnp.sum(square, 0, keepdims=True) / full - mean0 * mean0 + EPS)
    one_lane = lax.broadcasted_iota(jnp.int32, (chunk, lanes), 1) == pat
    for r in chunks:
        v = xp_o[0, r, :].astype(F32)
        f = (v - mean0) * rstd0 * wide(wide_prm[0, r, :]) + wide(wide_prm[2, r, :])
        f_o[0, r, :] = jnp.where(one_lane, 1.0, f).astype(BF16)
    total = jnp.zeros((8, lanes), F32)
    square = jnp.zeros((8, lanes), F32)
    big = 128
    for r0 in range(0, full, big):
        pre = nt(f_o[0, r0 : r0 + big, :], tw1_o[...])
        for a in range(0, big, 32):
            v = pre[a : a + 32]
            cdf, pdf = gelu_parts(v)
            hid_o[0, r0 + a : r0 + a + 32, :] = (v * cdf).astype(BF16)
            slope_o[0, r0 + a : r0 + a + 32, :] = (cdf + v * pdf).astype(BF16)
    for r0 in range(0, full, big):
        out = nn(hid_o[0, r0 : r0 + big, :], tw2_o[...])
        for a in range(0, big, chunk):
            r = slice(r0 + a, r0 + a + chunk)
            v = xp_o[0, r, :].astype(F32) + (out[a : a + chunk] + tb2_ref[0:1, :])
            mix_o[0, r, :] = v
            total += fold(v)
            square += fold(v * v)
    mean1 = jnp.sum(total, 0, keepdims=True) / full
    rstd1 = lax.rsqrt(jnp.sum(square, 0, keepdims=True) / full - mean1 * mean1 + EPS)
    for r in chunks:
        v = mix_o[0, r, :]
        s = (v - mean1) * rstd1 * wide(wide_prm[1, r, :]) + wide(wide_prm[3, r, :])
        s_buf[r, :] = s.astype(BF16)
    ident = eye(tp, lanes)
    st_o[...] = nt(ident, s_buf[...]).astype(BF16)
    kept = keep_ref[pl.ds(my_first + image, 1), :].astype(F32)
    count = jnp.sum(kept, 1, keepdims=True)
    pick = lax.broadcasted_iota(jnp.int32, (chunk, 128), 1) == my_first + image
    for r in chunks:
        g = jnp.sum(jnp.where(pick, colr[r, :], 0.0), 1, keepdims=True)
        y = kept * (gof[image, r, :].astype(F32) + g / count)
        yp_o[0, r, :pat] = y.astype(BF16)
    yt_o[...] = nt(ident, yp_o[0]).astype(BF16)
    stat_o[0] = jnp.zeros((8, lanes), F32)
    stat_o[0, 0:1, :] = mean0
    stat_o[0, 1:2, :] = rstd0
    stat_o[0, 2:3, :] = mean1
    stat_o[0, 3:4, :] = rstd1
    stat_o[0, 4:5, :pat] = kept
    stat_o[0, 5:6, :] = jnp.broadcast_to(1.0 / count, (1, lanes))

    @pl.when(step == ni - 1)
    def _():
        copies = pair_copies()
        for n in range(3, 6):
            copies[n].wait_recv()
        for c in copies:
            c.wait_send()

        def sent(n, c):
            token_copy(n).wait_send()
            return c

        lax.fori_loop(1, n_dp, sent, 0)


PRM_LANE = 200


def pad_lanes(n):
    return up(n, 128)


def front(n_dp, x, go, col, w1, w2, b1, msg, keep, tb2):
    images, ch, pat = x.shape
    ni = images // 2
    full = 2 * ch
    unit_d = msg.shape[0] // 2
    ds = unit_d * n_dp
    tp = up(pat, 16)
    lanes = pad_lanes(pat)
    hid = w1.shape[1]
    sds = jax.ShapeDtypeStruct
    per = lambda *s: pl.BlockSpec((1,) + s, lambda i: (i, 0, 0))
    once = lambda *s: pl.BlockSpec(s, lambda i: (0, 0))
    outs = [
        (sds((ni * tp, full), BF16), pl.BlockSpec((tp, full), lambda i: (i, 0))),
        (sds((ni * tp, full), BF16), pl.BlockSpec((tp, full), lambda i: (i, 0))),
        (sds((ni, full, lanes), BF16), per(full, lanes)),
        (sds((ni, full, lanes), BF16), per(full, lanes)),
        (sds((ni, full, ds), BF16), per(full, ds)),
        (sds((ni, full, ds), BF16), per(full, ds)),
        (sds((ni, full, lanes), F32), per(full, lanes)),
        (sds((ni, full, lanes), BF16), per(full, lanes)),
        (sds((ni, 8, lanes), F32), per(8, lanes)),
        (sds((full, 128), F32), once(full, 128)),
        (sds((full, 128), F32), once(full, 128)),
        (sds((ds, lanes), BF16), once(ds, lanes)),
        (sds((ds, lanes), BF16), once(ds, lanes)),
        (sds(w1.shape, BF16), ANY),
        (sds(w2.shape, BF16), ANY),
        (sds(b1.shape, F32), ANY),
    ]
    return pl.pallas_call(
        functools.partial(front_kernel, (n_dp, ni, ch, pat, tp, unit_d)),
        grid=(ni,),
        out_shape=[o[0] for o in outs],
        in_specs=[ANY, ANY, once(*col.shape), ANY, ANY, ANY]
        + [once(*msg.shape), once(*keep.shape), once(*tb2.shape)],
        out_specs=[o[1] for o in outs],
        scratch_shapes=[
            pltpu.VMEM((ni, full, pat), BF16),
            pltpu.VMEM((ni, full, pat), BF16),
            pltpu.VMEM((n_dp,) + msg.shape, BF16),
            pltpu.VMEM((4, full, 128), F32),
            pltpu.VMEM((full, 128), F32),
            pltpu.VMEM((2, ds, lanes), F32),
            pltpu.VMEM((full, lanes), BF16),
            pltpu.SemaphoreType.DMA((n_dp,)),
            pltpu.SemaphoreType.DMA((n_dp,)),
            pltpu.SemaphoreType.DMA((6,)),
            pltpu.SemaphoreType.DMA((6,)),
            pltpu.SemaphoreType.DMA((2,)),
        ],
        compiler_params=pltpu.CompilerParams(
            collective_id=0, has_side_effects=True, vmem_limit_bytes=VMEM_BYTES
        ),
        name="front",
    )(x, go, col, w1, w2, b1, msg, keep, tb2)


def back_kernel(
    dims,
    st_hbm,
    yt_hbm,
    w1_hbm,
    w1p_hbm,
    w2_hbm,
    w2p_hbm,
    b1_ref,
    b1p_ref,
    xp_hbm,
    f_hbm,
    hid_hbm,
    slope_hbm,
    mix_hbm,
    yp_hbm,
    stat_ref,
    prm_ref,
    colf_ref,
    tw1_ref,
    tw2_ref,
    bo_hbm,
    gi_hbm,
    pool_o,
    sq_o,
    red_o,
    gw_o,
    st,
    yt,
    sc,
    yc,
    w1s,
    w2s,
    gh,
    ph,
    gs,
    pb,
    ra,
    r1,
    b2,
    r2,
    b3,
    r3,
    xs,
    fs,
    hs,
    ls,
    ms,
    ys,
    bos,
    gis,
    ob,
    sb,
    ol,
    tg,
    wide_prm,
    acc_col,
    acc_tok,
    row_h,
    row_c,
    row_p,
    pool_a,
    pool_r,
    sq_a,
    sq_r,
    msgs,
    msgr,
    red_a,
    red_r,
    w_sem,
    in_sem,
    sa,
    rsa,
    s1,
    rs1,
    s2,
    rs2,
    s3,
    rs3,
    out_s,
    out_r,
    out_l,
    tok_s,
    tok_r,
    fin_s,
    fin_r,
):
    n_dp, ni, ch, pat, tp, unit_d, nz, ny, nx = dims
    dp, core = where_am_i()
    x = lax.rem(dp, nx)
    y = lax.rem(dp // nx, ny)
    z = dp // (nx * ny)
    other = (dp, 1 - core)
    x_dev = ((z * ny + y) * nx + (1 - x), core)
    y_dev = ((z * ny + (1 - y)) * nx + x, core)
    full = 2 * ch
    rows_own = full // n_dp
    half = w1s.shape[2]
    n_blk = half // BLK
    toks = ni * tp
    toks_pad = gh.shape[0]
    lanes = xs.shape[2]
    my_first = core * ni
    ds = tw1_ref.shape[0]

    loads = [
        pltpu.make_async_copy(st_hbm, st.at[pl.ds(0, toks)], w_sem.at[0]),
        pltpu.make_async_copy(yt_hbm, yt.at[pl.ds(0, toks)], w_sem.at[1]),
        pltpu.make_async_copy(w1p_hbm, w1s.at[1], w_sem.at[2]),
        pltpu.make_async_copy(w2p_hbm, w2s.at[1], w_sem.at[3]),
        pltpu.make_async_copy(w1_hbm, w1s.at[0], w_sem.at[4]),
        pltpu.make_async_copy(w2_hbm, w2s.at[0], w_sem.at[5]),
    ]
    for c in loads:
        c.start()

    def image_loads(i, slot):
        pairs = ((xp_hbm, xs), (f_hbm, fs), (hid_hbm, hs), (slope_hbm, ls), (mix_hbm, ms), (yp_hbm, ys))
        return [
            pltpu.make_async_copy(a.at[i], b.at[slot], in_sem.at[slot, n])
            for n, (a, b) in enumerate(pairs)
        ]

    for c in image_loads(0, 0):
        c.start()
    greet_all(n_dp, dp, core)

    zero_rows = jnp.zeros((toks_pad - toks, gh.shape[1]), BF16)
    gh[toks:, :] = zero_rows
    ph[toks:, :] = zero_rows
    sc[:, toks // 128 * 128 :] = jnp.zeros((full, toks_pad - toks // 128 * 128), BF16)
    yc[:, toks // 128 * 128 :] = jnp.zeros((full, toks_pad - toks // 128 * 128), BF16)
    row_h[...] = jnp.zeros_like(row_h)
    row_c[...] = jnp.zeros_like(row_c)
    row_p[...] = jnp.zeros_like(row_p)
    acc_col[...] = jnp.zeros_like(acc_col)
    acc_tok[...] = jnp.zeros_like(acc_tok)
    pool_a[...] = jnp.zeros_like(pool_a)
    sq_a[...] = jnp.zeros_like(sq_a)
    for n in range(4):
        at = PRM_LANE - 128 + n
        wide_prm[n] = jnp.broadcast_to(prm_ref[:, at : at + 1], (full, 128))
    at = 2 * ni
    wide_prm[4] = jnp.broadcast_to(colf_ref[:, at : at + 1], (full, 128))
    ob[...] = jnp.zeros_like(ob)
    sb[...] = jnp.zeros_like(sb)
    ident = eye(256, 256)
    loads[0].wait()
    loads[1].wait()
    for c0 in range(0, full, 256):
        sc[c0 : c0 + 256, :toks] = nt(ident, st[:toks, c0 : c0 + 256]).astype(BF16)
        yc[c0 : c0 + 256, :toks] = nt(ident, yt[:toks, c0 : c0 + 256]).astype(BF16)
    for n in range(2, 6):
        loads[n].wait()

    def pair_copy(slot):
        return remote(pb.at[slot], ra.at[slot], sa.at[slot], rsa.at[slot], other)

    def first_copies(slot):
        return (
            remote(
                gs.at[slot, 0, :, :, 1 - x], r1.at[slot, 0], s1.at[slot, 0], rs1.at[slot, 0], x_dev
            ),
            remote(gs.at[slot, 1, :, 1 - y], r1.at[slot, 1], s1.at[slot, 1], rs1.at[slot, 1], y_dev),
        )

    def second_copies(slot):
        return (
            remote(b2.at[slot, 0, :, 1 - y], r2.at[slot, 0], s2.at[slot, 0], rs2.at[slot, 0], y_dev),
            remote(b2.at[slot, 1, :, 1 - x], r2.at[slot, 1], s2.at[slot, 1], rs2.at[slot, 1], x_dev),
        )

    def third_copies(slot):
        out = []
        for n in range(1, nz):
            to = lax.rem(z + n, nz)
            out.append(
                remote(
                    b3.at[slot, to],
                    r3.at[slot, n - 1],
                    s3.at[slot, n - 1],
                    rs3.at[slot, n - 1],
                    ((to * ny + y) * nx + x, core),
                )
            )
        return out

    def finish_third(j):
        slot = lax.rem(j, 2)
        for c in third_copies(slot):
            c.wait()
        at = pl.ds(pl.multiple_of(j * BLK, BLK), BLK)
        for m in range(2):
            v = b3[slot, z, m].astype(F32)
            for n in range(nz - 1):
                v = v + r3[slot, n, m].astype(F32)
            gw_o[m, :, at] = v

    def finish_second(j):
        slot = lax.rem(j, 2)
        for c in second_copies(slot):
            c.wait()
        for m, mine in ((0, y), (1, x)):
            for k in range(nz):
                v = b2[slot, m, k, mine].astype(F32) + r2[slot, m, k].astype(F32)
                b3[slot, k, m] = v.astype(BF16)
        for c in third_copies(slot):
            c.start()

    def finish_first(j):
        slot = lax.rem(j, 2)
        for c in first_copies(slot):
            c.wait()
        for k in range(nz):
            for n in range(2):
                v = gs[slot, 0, k, n, x].astype(F32) + r1[slot, 0, k, n].astype(F32)
                b2[slot, 0, k, n] = v.astype(BF16)
                v = gs[slot, 1, k, y, n].astype(F32) + r1[slot, 1, k, n].astype(F32)
                b2[slot, 1, k, n] = v.astype(BF16)
        for c in second_copies(slot):
            c.start()

    def hidden_block(side, j, bias_ref):
        at = pl.ds(pl.multiple_of(j * BLK, BLK), BLK)
        col = pl.ds(pl.multiple_of(side * half + j * BLK, BLK), BLK)
        w1 = w1s[side, :, at]
        w2 = w2s[side, at, :]
        bias = bias_ref[0:1, at]
        for i in range(ni):
            r0 = i * tp
            r = slice(r0, r0 + tp)
            pre = nn(st[r, :], w1)
            up_grad = nt(yt[r, :], w2)
            acc = jnp.zeros((8, BLK), F32)
            for a in range(0, tp, 16):
                v = pre[a : a + 16] + bias
                cdf, pdf = gelu_parts(v)
                gh[r0 + a : r0 + a + 16, col] = (v * cdf).astype(BF16)
                p = up_grad[a : a + 16] * (cdf + v * pdf)
                ph[r0 + a : r0 + a + 16, col] = p.astype(BF16)
                acc += fold(p)
            row = jnp.sum(acc, 0, keepdims=True)
            row_h[0:1, col] += row
            row_h[1 + i : 2 + i, col] = row
        return nn(sc[...], ph[:, col]), nn(yc[...], gh[:, col])

    def split(v, k):
        per = full // nz
        return v[k * per : (k + 1) * per].reshape(ny, nx, rows_own, BLK)

    def block_step(j, carry):
        slot = lax.rem(j, 2)
        for m, v in enumerate(hidden_block(1, j, b1p_ref)):
            for k in range(nz):
                pb[slot, m, k] = split(v, k).astype(BF16)
        pair_copy(slot).start()
        grads = hidden_block(0, j, b1_ref)
        pair_copy(slot).wait()
        for m, v in enumerate(grads):
            for k in range(nz):
                gs[slot, m, k] = (split(v, k) + ra[slot, m, k].astype(F32)).astype(BF16)

        @pl.when(j >= 3)
        def _():
            finish_third(j - 3)

        @pl.when(j >= 2)
        def _():
            finish_second(j - 2)

        @pl.when(j >= 1)
        def _():
            finish_first(j - 1)

        for c in first_copies(slot):
            c.start()
        return carry

    lax.fori_loop(0, n_blk, block_step, 0)

    def second_half(i):
        r = pl.ds(pl.multiple_of(i * tp, 16), tp)
        g = gh[r, :]
        p = ph[r, :]
        s = st[r, :]
        yv = yt[r, :]
        both = nt(s, s) * nt(p, p) + nt(g, g) * nt(yv, yv)
        sq = jnp.sum(jnp.sum(both, 0, keepdims=True), 1, keepdims=True)
        rh = row_h[pl.ds(1 + i, 1), :]
        rc = jnp.sum(fold(yv.astype(F32)), 0, keepdims=True)
        row_c[0:1, :] += rc
        sq = sq + jnp.sum(rh * rh, 1, keepdims=True) + jnp.sum(rc * rc, 1, keepdims=True)
        lane = lax.broadcasted_iota(jnp.int32, (1, 128), 1)
        sq_a[0:1, :] += jnp.where(lane == my_first + i, sq, 0.0)
        out = nn(gh[r, :half], w2s[0]) + nn(gh[r, half:], w2s[1])
        grad = nt(ph[r, :half], w1s[0]) + nt(ph[r, half:], w1s[1])
        ob[:tp, :] = out.astype(BF16)
        sb[:tp, :] = grad.astype(BF16)

    def drain(i):
        @pl.when(i == 0)
        def _():
            finish_third(n_blk - 3)
            finish_second(n_blk - 2)
            finish_first(n_blk - 1)

        @pl.when(i == 1)
        def _():
            finish_third(n_blk - 2)
            finish_second(n_blk - 1)

        @pl.when(i == 2)
        def _():
            finish_third(n_blk - 1)

    chunk = 64
    chunks = [slice(r, r + chunk) for r in range(0, full, chunk)]

    def out_copies(i, slot):
        there = pl.ds(pl.multiple_of((1 - core) * ch, 128), ch)
        here = pl.ds(pl.multiple_of(core * ch, 128), ch)
        res = []
        for n, (src, dst) in enumerate(((bos, bo_hbm), (gis, gi_hbm))):
            res.append(
                remote(
                    src.at[slot, there],
                    dst.at[my_first + i],
                    out_s.at[slot, n],
                    out_r.at[i, n],
                    other,
                )
            )
            res.append(
                pltpu.make_async_copy(
                    src.at[slot, here], dst.at[my_first + i], out_l.at[slot, n]
                )
            )
        return res

    def out_arrivals(i):
        there = pl.ds(pl.multiple_of((1 - core) * ch, 128), ch)
        return [
            remote(
                src.at[0, there],
                dst.at[(1 - core) * ni + i],
                out_s.at[0, n],
                out_r.at[i, n],
                other,
            )
            for n, (src, dst) in enumerate(((bos, bo_hbm), (gis, gi_hbm)))
        ]

    def image_step(i, carry):
        slot = lax.rem(i, 2)
        second_half(i)
        drain(i)

        @pl.when(i + 1 < ni)
        def _():
            for c in image_loads(i + 1, 1 - slot):
                c.start()

        for c in image_loads(i, slot):
            c.wait()

        @pl.when(i >= 2)
        def _():
            for n, c in enumerate(out_copies(i - 2, slot)):
                if n % 2 == 0:
                    c.wait_send()
                else:
                    c.wait()

        stats = stat_ref[i]
        mean0, rstd0, mean1, rstd1 = (stats[n : n + 1, :] for n in range(4))
        kept = stats[4:5, :]
        inv_count = stats[5:6, 0:128]
        lane = lax.broadcasted_iota(jnp.int32, (chunk, 128), 1)
        pick = lane == my_first + i
        zero8 = jnp.zeros((8, lanes), F32)
        e_sum, eu_sum = zero8, zero8
        outs, backs = [], []
        for c0 in range(0, full, 256):
            outs.append(nt(ident, ob[:, c0 : c0 + 256]))
            backs.append(nt(ident, sb[:, c0 : c0 + 256]))

        def piece(parts, r):
            c0 = r.start // 256
            return parts[c0][r.start - 256 * c0 : r.stop - 256 * c0]

        for r in chunks:
            mix = ms[slot, r, :]
            bo = kept * (mix + (piece(outs, r) + wide(wide_prm[4, r, :])))
            bos[slot, r, :] = bo[:, :pat].astype(BF16)
            pooled = jnp.sum(bo, 1, keepdims=True) * inv_count
            pool_a[r, :] += jnp.where(pick, pooled, 0.0)
        for r in chunks:
            sg = piece(backs, r)
            unit = (ms[slot, r, :] - mean1) * rstd1
            su = sg * unit
            acc_col[1, r, :] += su[:, :128] + su[:, 128:]
            acc_col[3, r, :] += sg[:, :128] + sg[:, 128:]
            e = sg * wide(wide_prm[1, r, :])
            e_sum += fold(e)
            eu_sum += fold(e * unit)
        em = jnp.sum(e_sum, 0, keepdims=True) / full
        eum = jnp.sum(eu_sum, 0, keepdims=True) / full
        b2_sum = zero8
        for r in chunks:
            sg = piece(backs, r)
            unit = (ms[slot, r, :] - mean1) * rstd1
            e = sg * wide(wide_prm[1, r, :])
            mg = ys[slot, r, :].astype(F32) + rstd1 * (e - em - unit * eum)
            ms[slot, r, :] = mg
            ol[r, :] = mg.astype(BF16)
            b2_sum += fold(mg)
        row_p[0:8, :] += b2_sum
        big = 128
        for r0 in range(0, full, big):
            hg = nt(ol[r0 : r0 + big, :], tw2_ref[...])
            for a in range(0, big, 32):
                r = slice(r0 + a, r0 + a + 32)
                tg[r, :] = (hg[a : a + 32] * ls[slot, r, :].astype(F32)).astype(BF16)
        acc_tok[0] += tn(tg[...], fs[slot])
        acc_tok[1] += tn(hs[slot], ol[...])
        e_sum, eu_sum = zero8, zero8
        valid = lax.broadcasted_iota(jnp.int32, (chunk, lanes), 1) < pat
        firsts = []
        for r0 in range(0, full, big):
            firsts.append(nn(tg[r0 : r0 + big, :], tw1_ref[...]))

        def first_piece(r):
            v = firsts[r.start // big][r.start % big : r.start % big + chunk]
            return jnp.where(valid, v, 0.0)

        for r in chunks:
            fg = first_piece(r)
            unit = (xs[slot, r, :].astype(F32) - mean0) * rstd0
            su = fg * unit
            acc_col[0, r, :] += su[:, :128] + su[:, 128:]
            acc_col[2, r, :] += fg[:, :128] + fg[:, 128:]
            e = fg * wide(wide_prm[0, r, :])
            e_sum += fold(e)
            eu_sum += fold(e * unit)
        em = jnp.sum(e_sum, 0, keepdims=True) / full
        eum = jnp.sum(eu_sum, 0, keepdims=True) / full
        for r in chunks:
            fg = first_piece(r)
            unit = (xs[slot, r, :].astype(F32) - mean0) * rstd0
            e = fg * wide(wide_prm[0, r, :])
            gi = ms[slot, r, :] + rstd0 * (e - em - unit * eum)
            gis[slot, r, :] = gi[:, :pat].astype(BF16)
        for c in out_copies(i, slot):
            c.start()
        return carry

    lax.fori_loop(0, ni, image_step, 0)

    lane = lax.broadcasted_iota(jnp.int32, (2 * unit_d, 128), 1)
    h_0 = jnp.where(core == 0, row_h[0:1, :half], row_h[0:1, half:])
    h_1 = jnp.where(core == 0, row_h[0:1, half:], row_h[0:1, :half])
    per_h = half // n_dp
    per_c = ch // n_dp
    tail = msgs.shape[1] - 2 * unit_d
    b2_row = jnp.sum(row_p[...], 0, keepdims=True)

    def cut(v, start, size):
        n = v.shape[1]
        v = jnp.broadcast_to(v, (8, n))
        v = pltpu.roll(v, (n - start) % n, 1)[0:1, :lanes]
        return jnp.where(lax.broadcasted_iota(jnp.int32, (1, lanes), 1) < size, v, 0.0)

    for d in range(n_dp):
        top = jnp.concatenate(
            [
                acc_tok[0, unit_d * d : unit_d * (d + 1), :],
                acc_tok[1, unit_d * d : unit_d * (d + 1), :],
            ],
            axis=0,
        )
        rows = slice(rows_own * d, rows_own * (d + 1))
        right = top[:, 128:]
        for n in range(4):
            s = jnp.sum(acc_col[n, rows, :], 1, keepdims=True)
            right = jnp.where(lane == PRM_LANE - 128 + n, s, right)
        msgs[d, : 2 * unit_d, :128] = top[:, :128].astype(BF16)
        msgs[d, : 2 * unit_d, 128:] = right.astype(BF16)
        extra = jnp.concatenate(
            [
                b2_row,
                cut(h_0, per_h * d, per_h),
                cut(h_1, per_h * d, per_h),
                cut(row_c[0:1, :], per_c * d, per_c),
                cut(row_c[0:1, :], ch + per_c * d, per_c),
                jnp.zeros((tail - 5, lanes), F32),
            ],
            axis=0,
        )
        msgs[d, 2 * unit_d :, :] = extra.astype(BF16)

    def token_send(n):
        to = lax.rem(dp + n, n_dp)
        return remote(msgs.at[to], msgr.at[dp], tok_s.at[n], tok_r.at[dp], (to, core))

    def token_arrival(n):
        source = lax.rem(dp + n_dp - n, n_dp)
        return remote(
            msgs.at[source], msgr.at[source], tok_s.at[n], tok_r.at[source], (source, core)
        )

    def send(n, c):
        token_send(n).start()
        return c

    lax.fori_loop(1, n_dp, send, 0)
    pool_copy = remote(
        pool_a.at[pl.ds(pl.multiple_of((1 - core) * ch, 128), ch)], pool_r, fin_s.at[0], fin_r.at[0], other
    )
    pool_copy.start()
    sq_copy = remote(sq_a, sq_r, fin_s.at[1], fin_r.at[1], other)
    sq_copy.start()
    msgr[dp] = msgs[dp]

    def arrive(n, c):
        token_arrival(n).wait_recv()
        return c

    lax.fori_loop(1, n_dp, arrive, 0)
    total = msgr[0].astype(F32)
    for d in range(1, n_dp):
        total = total + msgr[d].astype(F32)
    red_a[...] = total
    red_copy = remote(red_a, red_r, fin_s.at[2], fin_r.at[2], other)
    red_copy.start()

    def sent(n, c):
        token_send(n).wait_send()
        return c

    lax.fori_loop(1, n_dp, sent, 0)
    for i in (ni - 2, ni - 1):
        for n, c in enumerate(out_copies(i, i % 2)):
            if n % 2 == 0:
                c.wait_send()
            else:
                c.wait()
    for i in range(ni):
        for c in out_arrivals(i):
            c.wait_recv()
    pool_copy.wait()
    sq_copy.wait()
    pool_o[...] = pool_a[pl.ds(pl.multiple_of(core * ch, 128), ch), :] + pool_r[...]
    sq_o[...] = sq_a[...] + sq_r[...]
    red_copy.wait()
    red_o[...] = red_a[...] + red_r[...]


def back(n_dp, grid3, st, yt, w1, w1p, w2, w2p, b1, b1p, xp, f, hid, slope, mix, yp, stat, prm, colf, tw1, tw2, pat):
    ni, full, lanes = xp.shape
    ch = full // 2
    half = w1.shape[1]
    toks = st.shape[0]
    tp = toks // ni
    ds = tw1.shape[0]
    unit_d = ds // n_dp
    toks_pad = up(toks, 256)
    nz, ny, nx = grid3
    rows_own = full // n_dp
    n_msg = up(2 * unit_d + 5, 16)
    sds = jax.ShapeDtypeStruct
    vm = pltpu.VMEM
    dma = pltpu.SemaphoreType.DMA
    part = (nz, ny, nx, rows_own, BLK)
    return pl.pallas_call(
        functools.partial(back_kernel, (n_dp, ni, ch, pat, tp, unit_d, nz, ny, nx)),
        out_shape=[
            sds((2 * ni, ch, pat), BF16),
            sds((2 * ni, ch, pat), BF16),
            sds((ch, 128), F32),
            sds((8, 128), F32),
            sds((n_msg, lanes), F32),
            sds((2, rows_own, half), F32),
        ],
        in_specs=[ANY] * 6 + [VM, VM] + [ANY] * 6 + [VM] * 5,
        out_specs=[ANY, ANY, VM, VM, VM, VM],
        scratch_shapes=[
            vm((toks_pad, full), BF16),
            vm((toks_pad, full), BF16),
            vm((full, toks_pad), BF16),
            vm((full, toks_pad), BF16),
            vm((2, full, half), BF16),
            vm((2, half, full), BF16),
            vm((toks_pad, 2 * half), BF16),
            vm((toks_pad, 2 * half), BF16),
            vm((2, 2) + part, BF16),
            vm((2, 2) + part, BF16),
            vm((2, 2) + part, BF16),
            vm((2, 2, nz, 2, rows_own, BLK), BF16),
            vm((2, 2, nz, 2, rows_own, BLK), BF16),
            vm((2, 2, nz, rows_own, BLK), BF16),
            vm((2, nz, 2, rows_own, BLK), BF16),
            vm((2, nz - 1, 2, rows_own, BLK), BF16),
            vm((2, full, lanes), BF16),
            vm((2, full, lanes), BF16),
            vm((2, full, ds), BF16),
            vm((2, full, ds), BF16),
            vm((2, full, lanes), F32),
            vm((2, full, lanes), BF16),
            vm((2, full, pat), BF16),
            vm((2, full, pat), BF16),
            vm((256, full), BF16),
            vm((256, full), BF16),
            vm((full, lanes), BF16),
            vm((full, ds), BF16),
            vm((5, full, 128), F32),
            vm((4, full, 128), F32),
            vm((2, ds, lanes), F32),
            vm((8, 2 * half), F32),
            vm((8, full), F32),
            vm((8, lanes), F32),
            vm((full, 128), F32),
            vm((ch, 128), F32),
            vm((8, 128), F32),
            vm((8, 128), F32),
            vm((n_dp, n_msg, lanes), BF16),
            vm((n_dp, n_msg, lanes), BF16),
            vm((n_msg, lanes), F32),
            vm((n_msg, lanes), F32),
            dma((6,)),
            dma((2, 6)),
            dma((2,)),
            dma((2,)),
            dma((2, 2)),
            dma((2, 2)),
            dma((2, 2)),
            dma((2, 2)),
            dma((2, nz - 1)),
            dma((2, nz - 1)),
            dma((2, 2)),
            dma((ni, 2)),
            dma((2, 2)),
            dma((n_dp,)),
            dma((n_dp,)),
            dma((3,)),
            dma((3,)),
        ],
        compiler_params=pltpu.CompilerParams(
            collective_id=1, has_side_effects=True, vmem_limit_bytes=VMEM_BYTES
        ),
        name="back",
    )(st, yt, w1, w1p, w2, w2p, b1, b1p, xp, f, hid, slope, mix, yp, stat, prm, colf, tw1, tw2)


def finish_kernel(
    dims,
    bo_ref,
    gi_ref,
    pool_ref,
    sq_ref,
    red_ref,
    gw_ref,
    bo_o,
    pool_o,
    gi_o,
    gain_o,
    shift_o,
    tw1_o,
    tb1_o,
    tw2_o,
    tb2_o,
    w1_o,
    b1_o,
    w2_o,
    b2_o,
    sq_o,
):
    pat, unit_d, per_h, per_c = dims
    _, core = where_am_i()
    bo_o[...] = bo_ref[...].astype(F32)
    gi_o[...] = gi_ref[...].astype(F32)

    @pl.when(pl.program_id(0) == 0)
    def _():
        images = pool_o.shape[0]
        pool_o[...] = jnp.transpose(pool_ref[...])[:images]
        sq_o[...] = sq_ref[0:1, :images]
        red = red_ref[...]
        flat = jnp.transpose(red[: 2 * unit_d, 128:])
        at = PRM_LANE - 128
        gain_o[...] = flat[at : at + 2]
        shift_o[...] = flat[at + 2 : at + 4]
        first = jnp.transpose(red[:unit_d, :])
        tw1_o[...] = first[:pat]
        tb1_o[...] = first[pat : pat + 1]
        tw2_o[...] = red[unit_d : 2 * unit_d, :pat]
        n = 2 * unit_d
        tb2_o[...] = red[n : n + 1, :pat]
        w1_o[...] = gw_ref[0]
        w2_o[...] = jnp.transpose(gw_ref[1])
        b1_o[...] = jnp.where(core == 0, red[n + 1 : n + 2, :per_h], red[n + 2 : n + 3, :per_h])
        b2_o[...] = jnp.where(core == 0, red[n + 3 : n + 4, :per_c], red[n + 4 : n + 5, :per_c])


def finish(bo, gi, pool, sq, red, gw, unit_d, per_h, per_c):
    images, ch, pat = bo.shape
    ds = unit_d
    sds = jax.ShapeDtypeStruct
    once = lambda s: pl.BlockSpec(s, lambda i: (0,) * len(s))
    per = pl.BlockSpec((1, ch, pat), lambda i: (i, 0, 0))
    rows_own, half = gw.shape[1:]
    outs = [
        (images, ch, pat),
        (images, ch),
        (images, ch, pat),
        (2, rows_own),
        (2, rows_own),
        (pat, ds),
        (1, ds),
        (ds, pat),
        (1, pat),
        (rows_own, half),
        (1, per_h),
        (half, rows_own),
        (1, per_c),
        (1, images),
    ]
    res = pl.pallas_call(
        functools.partial(finish_kernel, (pat, unit_d, per_h, per_c)),
        grid=(images,),
        out_shape=[sds(s, F32) for s in outs],
        in_specs=[per, per] + [once(a.shape) for a in (pool, sq, red, gw)],
        out_specs=[per if len(s) == 3 else once(s) for s in outs],
        compiler_params=pltpu.CompilerParams(vmem_limit_bytes=VMEM_BYTES),
        name="finish",
    )(bo, gi, pool, sq, red, gw)
    return tuple(r.reshape(-1) if r.shape[0] == 1 else r for r in res)


def fused_body(
    n_dp,
    grid3,
    mixer_input,
    keep_mask,
    ln_gain,
    ln_shift,
    token_w1,
    token_b1,
    token_w2,
    token_b2,
    chan_w1,
    chan_b1,
    chan_w2,
    chan_b2,
    grad_out,
    grad_pooled,
):
    images, ch, pat = mixer_input.shape
    unit_d = token_b1.shape[0]
    half = chan_b1.shape[0]
    lanes = pad_lanes(pat)
    left = jnp.concatenate([token_w1.T, token_w2], 0)
    bias = jnp.pad(token_b1[:, None], ((0, unit_d), (0, PRM_LANE - pat - 1)))
    norms = jnp.concatenate([ln_gain.T, ln_shift.T], 1)
    msg = jnp.concatenate(
        [left, bias, jnp.pad(norms, ((0, 0), (0, lanes - PRM_LANE - 4)))], 1
    )
    col = jnp.concatenate([grad_pooled.T, chan_b2.astype(F32)[:, None]], 1)
    col = jnp.pad(col, ((0, 0), (0, 128 - col.shape[1])))
    b1 = jnp.broadcast_to(chan_b1.astype(F32)[None, :], (8, half))
    tb2 = jnp.broadcast_to(jnp.pad(token_b2.astype(F32), (0, lanes - pat))[None, :], (8, lanes))
    st, yt, xp, f, hid, slope, mix, yp, stat, prm, colf, tw1, tw2, w1p, w2p, b1p = front(
        n_dp, mixer_input, grad_out, col, chan_w1, chan_w2, b1, msg, keep_mask, tb2
    )
    bo, gi, pool, sq, red, gw = back(
        n_dp, grid3, st, yt, chan_w1, w1p, chan_w2, w2p, b1, b1p, xp, f, hid, slope, mix, yp,
        stat, prm, colf, tw1, tw2, pat,
    )
    return finish(bo, gi, pool, sq, red, gw, unit_d, half // n_dp, ch // n_dp)


D = 768


epsilon = 1e-05


def gelu_exact(values_in):
    return jax.nn.gelu(values_in, approximate=False)


def gelu_slope(pre_sum, upstream):
    unused, backward = jax.vjp(gelu_exact, pre_sum)
    return backward(upstream)[0]


def channel_sums(first_term, second_term):
    return lax.psum((first_term, second_term), "tensor")


def normalize(values_in, gains, shifts):
    totals, square = channel_sums(jnp.sum(values_in, 1), jnp.sum(values_in * values_in, 1))
    average = totals / D
    spread = square / D - average * average
    scaling = lax.rsqrt(spread + epsilon)[:, None, :]
    unit_part = (values_in - average[:, None, :]) * scaling
    return (unit_part * gains[None, :, None] + shifts[None, :, None], unit_part, scaling)


def normalize_back(upstream, unit_part, scaling, gains):
    scaled = upstream * gains[None, :, None]
    totals, along_unit = channel_sums(jnp.sum(scaled, 1), jnp.sum(scaled * unit_part, 1))
    inner_part = scaled - totals[:, None, :] / D - unit_part * along_unit[:, None, :] / D
    return (scaling * inner_part, jnp.sum(upstream * unit_part, (0, 2)), jnp.sum(upstream, (0, 2)))


def body(
    mixer_input,
    keep_mask,
    ln_gain,
    ln_shift,
    token_w1,
    token_b1,
    token_w2,
    token_b2,
    chan_w1,
    chan_b1,
    chan_w2,
    chan_b2,
    grad_out,
    grad_pooled,
):
    images, channels, patches = mixer_input.shape
    full_width = channels * lax.axis_size("tensor")
    offset = lax.axis_index("tensor") * channels
    gains, shifts, weight_in, bias_in, weight_back = (
        lax.all_gather(ln_gain, "dp", axis=1, tiled=True),
        lax.all_gather(ln_shift, "dp", axis=1, tiled=True),
        lax.all_gather(token_w1, "dp", axis=1, tiled=True),
        lax.all_gather(token_b1, "dp", axis=0, tiled=True),
        lax.all_gather(token_w2, "dp", axis=0, tiled=True),
    )
    gain_own = lax.dynamic_slice_in_dim(gains, offset, channels, 1).astype(jnp.float32)
    shift_own = lax.dynamic_slice_in_dim(shifts, offset, channels, 1).astype(jnp.float32)
    kept = keep_mask.astype(jnp.float32)
    counts = jnp.sum(kept, 1)
    source = mixer_input.astype(jnp.float32)
    normed, unit_first, scale_first = normalize(source, gain_own[0], shift_own[0])
    first_low = normed.astype(jnp.bfloat16)
    token_pre = jnp.einsum(
        "bcp,ph->bch", first_low, weight_in, preferred_element_type=jnp.float32
    ) + bias_in.astype(jnp.float32)
    token_hid = gelu_exact(token_pre).astype(jnp.bfloat16)
    token_out = jnp.einsum(
        "bch,hp->bcp", token_hid, weight_back, preferred_element_type=jnp.float32
    ) + token_b2.astype(jnp.float32)
    mixture = source + token_out
    normed, unit_second, scale_second = normalize(mixture, gain_own[1], shift_own[1])
    second = normed.astype(jnp.bfloat16)
    section = lax.all_gather(second, "tensor", axis=1, tiled=True)
    pre_sum = jnp.einsum("bcp,ch->bhp", section, chan_w1, preferred_element_type=jnp.float32)
    gathered = section
    grams = jnp.einsum("bcp,bcq->bpq", section, section, preferred_element_type=jnp.float32)
    chan_pre = pre_sum
    gram_second = grams
    chan_pre = chan_pre + chan_b1.astype(jnp.float32)[None, :, None]
    chan_hid = gelu_exact(chan_pre).astype(jnp.bfloat16)
    partial_value = jnp.einsum("bhp,hc->bcp", chan_hid, chan_w2, preferred_element_type=jnp.float32)
    chan_out = (
        lax.psum_scatter(
            partial_value.astype(jnp.bfloat16), "tensor", scatter_dimension=1, tiled=True
        ).astype(jnp.float32)
        + chan_b2.astype(jnp.float32)[None, :, None]
    )
    masked = kept[:, None, :] * (mixture + chan_out)
    pooled = jnp.sum(masked, 2) / counts[:, None]
    grad_result = kept[:, None, :] * (
        grad_out.astype(jnp.float32) + grad_pooled[:, :, None] / counts[:, None, None]
    )
    grad_low = grad_result.astype(jnp.bfloat16)
    grad_chan_b2 = jnp.sum(grad_low, (0, 2), dtype=jnp.float32)
    section = lax.all_gather(grad_low, "tensor", axis=1, tiled=True)
    hid_sum = jnp.einsum("bcp,hc->bhp", section, chan_w2, preferred_element_type=jnp.float32)
    column_block = jnp.einsum("bhp,bcp->hc", chan_hid, section, preferred_element_type=jnp.float32)
    grams = jnp.einsum("bcp,bcq->bpq", section, section, preferred_element_type=jnp.float32)
    pre_grad = gelu_slope(chan_pre, hid_sum).astype(jnp.bfloat16)
    grad_chan_b1 = jnp.sum(pre_grad, (0, 2), dtype=jnp.float32)
    grad_chan_w1 = jnp.einsum("bcp,bhp->ch", gathered, pre_grad, preferred_element_type=jnp.float32)
    share_w1, share_b1, share_w2, share_b2 = (
        lax.psum_scatter(
            grad_chan_w1.astype(jnp.bfloat16), "dp", scatter_dimension=0, tiled=True
        ).astype(jnp.float32),
        lax.psum_scatter(
            grad_chan_b1.astype(jnp.bfloat16), "dp", scatter_dimension=0, tiled=True
        ).astype(jnp.float32),
        lax.psum_scatter(
            column_block.astype(jnp.bfloat16), "dp", scatter_dimension=1, tiled=True
        ).astype(jnp.float32),
        lax.psum_scatter(
            grad_chan_b2.astype(jnp.bfloat16), "dp", scatter_dimension=0, tiled=True
        ).astype(jnp.float32),
    )
    second_part = jnp.einsum("bhp,ch->bcp", pre_grad, chan_w1, preferred_element_type=jnp.float32)
    second_grad = lax.psum_scatter(
        second_part.astype(jnp.bfloat16), "tensor", scatter_dimension=1, tiled=True
    ).astype(jnp.float32)
    gram_pre = jnp.einsum("bhp,bhq->bpq", pre_grad, pre_grad, preferred_element_type=jnp.float32)
    gram_hid = jnp.einsum("bhp,bhq->bpq", chan_hid, chan_hid, preferred_element_type=jnp.float32)
    own_terms = jnp.sum(gram_second * gram_pre + gram_hid * grams, (1, 2))
    own_terms = own_terms + jnp.sum(jnp.square(jnp.sum(pre_grad, 2, dtype=jnp.float32)), 1)
    own_terms = own_terms + jnp.sum(jnp.square(jnp.sum(grad_low, 2, dtype=jnp.float32)), 1)
    example_sq = lax.psum(own_terms, "tensor")
    back_second, gain_second, shift_second = normalize_back(
        second_grad, unit_second, scale_second, gain_own[1]
    )
    mixture_grad = grad_result + back_second
    out_low = mixture_grad.astype(jnp.bfloat16)
    grad_token_b2 = jnp.sum(out_low, (0, 1), dtype=jnp.float32)
    token_hid_grad = jnp.einsum(
        "bcp,hp->bch", out_low, weight_back, preferred_element_type=jnp.float32
    )
    grad_token_w2 = jnp.einsum(
        "bch,bcp->hp", token_hid, out_low, preferred_element_type=jnp.float32
    )
    token_pre_grad = gelu_slope(token_pre, token_hid_grad).astype(jnp.bfloat16)
    grad_token_b1 = jnp.sum(token_pre_grad, (0, 1), dtype=jnp.float32)
    grad_token_w1 = jnp.einsum(
        "bcp,bch->ph", first_low, token_pre_grad, preferred_element_type=jnp.float32
    )
    first_grad = jnp.einsum(
        "bch,ph->bcp", token_pre_grad, weight_in, preferred_element_type=jnp.float32
    )
    back_first, gain_first, shift_first = normalize_back(
        first_grad, unit_first, scale_first, gain_own[0]
    )
    grad_input = mixture_grad + back_first
    gain_parts = lax.dynamic_update_slice_in_dim(
        jnp.zeros((2, full_width), jnp.float32), jnp.stack([gain_first, gain_second]), offset, 1
    )
    shift_parts = lax.dynamic_update_slice_in_dim(
        jnp.zeros((2, full_width), jnp.float32), jnp.stack([shift_first, shift_second]), offset, 1
    )
    total_gain, total_shift, total_w1, total_b1, total_w2 = (
        lax.psum(gain_parts.astype(jnp.bfloat16), "tensor").astype(jnp.float32),
        lax.psum(shift_parts.astype(jnp.bfloat16), "tensor").astype(jnp.float32),
        lax.psum(grad_token_w1.astype(jnp.bfloat16), "tensor").astype(jnp.float32),
        lax.psum(grad_token_b1.astype(jnp.bfloat16), "tensor").astype(jnp.float32),
        lax.psum(grad_token_w2.astype(jnp.bfloat16), "tensor").astype(jnp.float32),
    )
    share_gain, share_shift, share_tw1, share_tb1, share_tw2 = (
        lax.psum_scatter(
            total_gain.astype(jnp.bfloat16), "dp", scatter_dimension=1, tiled=True
        ).astype(jnp.float32),
        lax.psum_scatter(
            total_shift.astype(jnp.bfloat16), "dp", scatter_dimension=1, tiled=True
        ).astype(jnp.float32),
        lax.psum_scatter(
            total_w1.astype(jnp.bfloat16), "dp", scatter_dimension=1, tiled=True
        ).astype(jnp.float32),
        lax.psum_scatter(
            total_b1.astype(jnp.bfloat16), "dp", scatter_dimension=0, tiled=True
        ).astype(jnp.float32),
        lax.psum_scatter(
            total_w2.astype(jnp.bfloat16), "dp", scatter_dimension=0, tiled=True
        ).astype(jnp.float32),
    )
    share_tb2 = lax.psum(grad_token_b2, ("dp", "tensor"))
    return (
        masked,
        pooled,
        grad_input,
        share_gain,
        share_shift,
        share_tw1,
        share_tb1,
        share_tw2,
        share_tb2,
        share_w1,
        share_b1,
        share_w2,
        share_b2,
        example_sq,
    )


def solution(mesh):
    n_dp, n_tensor = mesh.shape["dp"], mesh.shape["tensor"]
    chosen = body
    if (n_dp, n_tensor) == (16, 2):
        chosen = functools.partial(fused_body, n_dp, (4, 2, 2))
    return jax.shard_map(
        chosen,
        mesh=mesh,
        in_specs=(
            P("dp", "tensor", None),
            P("dp", None),
            P(None, "dp"),
            P(None, "dp"),
            P(None, "dp"),
            P("dp"),
            P("dp", None),
            P(),
            P(None, "tensor"),
            P("tensor"),
            P("tensor", None),
            P("tensor"),
            P("dp", "tensor", None),
            P("dp", "tensor"),
        ),
        out_specs=(
            P("dp", "tensor", None),
            P("dp", "tensor"),
            P("dp", "tensor", None),
            P(None, "dp"),
            P(None, "dp"),
            P(None, "dp"),
            P("dp"),
            P("dp", None),
            P(),
            P("dp", "tensor"),
            P(("tensor", "dp")),
            P("tensor", "dp"),
            P(("tensor", "dp")),
            P("dp"),
        ),
        check_vma=False,
    )
```

```python
import functools
import math

import jax
import jax.numpy as jnp
from jax import lax
from jax.experimental import pallas as pl
from jax.experimental.pallas import tpu as pltpu
from jax.sharding import PartitionSpec as P

MESH = pl.DeviceIdType.MESH
EPS = 1e-05
F32 = jnp.float32
BF16 = jnp.bfloat16
VM = pl.BlockSpec(memory_space=pltpu.VMEM)
ANY = pl.BlockSpec(memory_space=pl.ANY)
BLK = 256
VMEM_BYTES = 63 * 2**20


def up(n, m):
    return -(-n // m) * m


def nn(a, b):
    return lax.dot_general(a, b, (((1,), (0,)), ((), ())), preferred_element_type=F32)


def nt(a, b):
    return lax.dot_general(a, b, (((1,), (1,)), ((), ())), preferred_element_type=F32)


def tn(a, b):
    return lax.dot_general(a, b, (((0,), (0,)), ((), ())), preferred_element_type=F32)


def eye(rows, cols):
    r = lax.broadcasted_iota(jnp.int32, (rows, cols), 0)
    c = lax.broadcasted_iota(jnp.int32, (rows, cols), 1)
    return (r == c).astype(F32).astype(BF16)


def gelu_parts(v):
    cdf = 0.5 + 0.5 * lax.erf(v * math.sqrt(0.5))
    return cdf, jnp.exp(-0.5 * (v * v)) * (1.0 / math.sqrt(2.0 * math.pi))


def fold(v):
    return jnp.sum(v.reshape(v.shape[0] // 8, 8, v.shape[1]), 0)


def where_am_i():
    return lax.axis_index("dp"), lax.axis_index("tensor")


def greet_all(dp_size, dp, core):
    barrier = pltpu.get_barrier_semaphore()

    def one(n, c):
        pl.semaphore_signal(
            barrier, inc=1, device_id=(lax.rem(dp + n, dp_size), core), device_id_type=MESH
        )
        return c

    lax.fori_loop(1, dp_size, one, 0)
    pl.semaphore_signal(barrier, inc=1, device_id=(dp, 1 - core), device_id_type=MESH)
    pl.semaphore_wait(barrier, dp_size)


def remote(src, dst, send, recv, device):
    return pltpu.make_async_remote_copy(
        src_ref=src,
        dst_ref=dst,
        send_sem=send,
        recv_sem=recv,
        device_id=device,
        device_id_type=MESH,
    )


ROWS = 16


def row_pieces(pat):
    return [slice(r, min(r + ROWS, pat)) for r in range(0, pat, ROWS)]


def lane_pieces(full):
    return [slice(c, c + 256) for c in range(0, full, 256)]


def across(v, full):
    return jnp.concatenate([v] * (full // 128), axis=1)


def centre(v):
    n = v.shape[1]
    d = v - jnp.sum(v, 1, keepdims=True) * (1.0 / n)
    r = lax.rsqrt(jnp.sum(d * d, 1, keepdims=True) * (1.0 / n) + EPS)
    return d * r, r


def front_kernel(
    dims,
    x_hbm,
    go_hbm,
    gp_ref,
    w1_hbm,
    w2_hbm,
    b1_ref,
    cb2_ref,
    gain_ref,
    shift_ref,
    tw1_ref,
    tb1_ref,
    tw2_ref,
    tb2_ref,
    keep_ref,
    st_o,
    yt_o,
    u0_o,
    f_o,
    hid_o,
    slope_o,
    mix_o,
    u1_o,
    col_o,
    norm_o,
    pack_o,
    tw_o,
    twt_o,
    w1p_o,
    w2p_o,
    xf,
    gof,
    msg,
    square,
    pack,
    packf,
    tok,
    tmp_w,
    prm,
    keep_t,
    tb2_w,
    outs,
    tok_send,
    tok_recv,
    pair_send,
    pair_recv,
    loc_sem,
):
    n_dp, ni, ch, pat, tp, unit_d = dims
    dp, core = where_am_i()
    full = 2 * ch
    image = pl.program_id(0)
    other = (dp, 1 - core)
    mine = pl.ds(pl.multiple_of(core * ch, 128), ch)
    my_first = core * ni
    ds = unit_d * n_dp
    rows_own = 2 * unit_d
    images = 2 * ni
    bias_rows = b1_ref.shape[1] // ch
    kp = f_o.shape[1]

    def pair_copies():
        theirs = pl.ds((1 - core) * ni, ni)
        pairs = [
            (pack, packf.at[:, mine]),
            (x_hbm.at[theirs], xf.at[:, :, mine]),
            (go_hbm.at[theirs], gof.at[:, :, mine]),
            (w1_hbm, w1p_o),
            (w2_hbm, w2p_o),
        ]
        return [
            remote(a, b, pair_send.at[n], pair_recv.at[n], other)
            for n, (a, b) in enumerate(pairs)
        ]

    def local_copies():
        ours = pl.ds(my_first, ni)
        return [
            pltpu.make_async_copy(x_hbm.at[ours], xf.at[:, :, mine], loc_sem.at[0]),
            pltpu.make_async_copy(go_hbm.at[ours], gof.at[:, :, mine], loc_sem.at[1]),
        ]

    def token_copy(n):
        to = lax.rem(dp + n, n_dp)
        return remote(msg, tok.at[dp], tok_send.at[n], tok_recv.at[dp], (to, core))

    def token_arrival(n):
        source = lax.rem(dp + n_dp - n, n_dp)
        return remote(
            msg, tok.at[source], tok_send.at[n], tok_recv.at[source], (source, core)
        )

    @pl.when(image == 0)
    def _():
        for c in local_copies():
            c.start()
        square[...] = jnp.zeros_like(square)
        at = pat - 128
        square[at : at + 1, :unit_d] = tb1_ref[...].astype(F32)
        square[at + 4 : at + 6, :rows_own] = gain_ref[...].astype(F32)
        square[at + 6 : at + 8, :rows_own] = shift_ref[...].astype(F32)
        columns = jnp.transpose(square[...])[:rows_own]
        tmp_w[0, :rows_own, :] = jnp.zeros((rows_own, kp), F32)
        tmp_w[0, :unit_d, :pat] = tw1_ref[...].astype(F32)
        tmp_w[0, unit_d:rows_own, :pat] = tw2_ref[...].astype(F32)
        msg[:, :128] = tmp_w[0, :rows_own, :128].astype(BF16)
        msg[:, 128:] = (tmp_w[0, :rows_own, 128:] + columns).astype(BF16)
        pack[...] = jnp.zeros_like(pack)
        pack[:images, :] = gp_ref[...]
        pack[images : images + 1, :] = cb2_ref[...].astype(F32)
        for n in range(bias_rows):
            pack[images + 1 + n : images + 2 + n, :] = b1_ref[
                :, n * ch : (n + 1) * ch
            ].astype(F32)
        greet_all(n_dp, dp, core)

        def send(n, c):
            token_copy(n).start()
            return c

        lax.fori_loop(1, n_dp, send, 0)
        copies = pair_copies()
        for c in copies:
            c.start()
        tok[dp] = msg[...]
        packf[:, mine] = pack[...]
        keep_t[...] = jnp.zeros_like(keep_t)
        keep_t[:images, :pat] = keep_ref[...].astype(F32)
        keep_t[images : images + 1, :pat] = tb2_ref[...].astype(F32)
        turned = jnp.transpose(keep_t[...])
        keep_t[:, :] = turned
        tb2_w[...] = jnp.broadcast_to(turned[:tp, images : images + 1], (tp, 128))
        for c in local_copies():
            c.wait()
        for n in range(3):
            copies[n].wait_recv()
        pack_o[...] = packf[...]

        def arrive(n, c):
            token_arrival(n).wait_recv()
            return c

        lax.fori_loop(1, n_dp, arrive, 0)
        lane = lax.broadcasted_iota(jnp.int32, (unit_d, kp), 1)
        for d in range(n_dp):
            block = tok[d].astype(F32)
            tmp_w[0, unit_d * d : unit_d * (d + 1), :] = jnp.where(
                lane <= pat, block[:unit_d], 0.0
            )
            tmp_w[1, unit_d * d : unit_d * (d + 1), :] = jnp.where(
                lane < pat, block[unit_d:], 0.0
            )
            prm[rows_own * d : rows_own * (d + 1), :] = tok[d, :, 128:]
        r = lax.broadcasted_iota(jnp.int32, (16, 128), 0)
        c = lax.broadcasted_iota(jnp.int32, (16, 128), 1)
        pick = ((c - (at + 4) == r) & (r < 4)).astype(F32).astype(BF16)
        norm_o[...] = nt(pick, prm[...])
        ident = eye(kp, kp)
        for n in range(2):
            w = tmp_w[n].astype(BF16)
            tw_o[n] = w
            t = nt(ident, w)
            r = lax.broadcasted_iota(jnp.int32, t.shape, 0)
            twt_o[n] = jnp.where(r < pat, t, 0.0)[:tp].astype(BF16)

    pieces = row_pieces(pat)
    last = slice(pat // ROWS * ROWS, tp)
    blank = jnp.zeros((last.stop - last.start, full), BF16)
    for ref in (st_o, yt_o):
        ref[last, :] = blank
    for ref in (u0_o, mix_o, u1_o):
        ref[0, last, :] = blank
    f_o[0, last.start :, :] = jnp.zeros((kp - last.start, full), BF16)
    f_o[0, pat : pat + 1, :] = jnp.ones((1, full), BF16)
    col_o[0, :, last, :] = jnp.zeros((3, tp - last.start, 128), F32)
    for r in pieces:
        unit, rstd = centre(xf[image, r, :].astype(F32))
        u0_o[0, r, :] = unit.astype(BF16)
        f_o[0, r, :] = (unit * norm_o[0:1, :] + norm_o[2:3, :]).astype(BF16)
        col_o[0, 0, r, :] = jnp.broadcast_to(rstd, (r.stop - r.start, 128))
    for c in lane_pieces(full):
        pre = nn(tw_o[0], f_o[0, :, c])
        for a in range(0, ds, 32):
            v = pre[a : a + 32]
            cdf, pdf = gelu_parts(v)
            hid_o[0, a : a + 32, c] = (v * cdf).astype(BF16)
            slope_o[0, a : a + 32, c] = (cdf + v * pdf).astype(BF16)
        outs[:, c] = nn(twt_o[1], hid_o[0, :, c])
    for r in pieces:
        v = xf[image, r, :].astype(F32) + (outs[r, :] + across(tb2_w[r, :], full))
        mix_o[0, r, :] = v.astype(BF16)
        unit, rstd = centre(v)
        u1_o[0, r, :] = unit.astype(BF16)
        st_o[r, :] = (unit * norm_o[1:2, :] + norm_o[3:4, :]).astype(BF16)
        col_o[0, 1, r, :] = jnp.broadcast_to(rstd, (r.stop - r.start, 128))
    number = my_first + image
    count = jnp.sum(keep_ref[pl.ds(number, 1), :].astype(F32), 1, keepdims=True)
    g = packf[pl.ds(number, 1), :] / count
    for r in pieces:
        size = r.stop - r.start
        lane = lax.broadcasted_iota(jnp.int32, (size, 128), 1)
        k = jnp.sum(jnp.where(lane == number, keep_t[r, :128], 0.0), 1, keepdims=True)
        yt_o[r, :] = (k * (gof[image, r, :].astype(F32) + g)).astype(BF16)
        col_o[0, 2, r, :] = jnp.broadcast_to(k, (size, 128))

    @pl.when(image == ni - 1)
    def _():
        copies = pair_copies()
        for c in copies[3:]:
            c.wait_recv()
        for c in copies:
            c.wait_send()

        def sent(n, c):
            token_copy(n).wait_send()
            return c

        lax.fori_loop(1, n_dp, sent, 0)


def front(n_dp, x, go, gp, w1, w2, b1, cb2, gain, shift, tw1, tb1, tw2, tb2, keep):
    images, pat, ch = x.shape
    ni = images // 2
    full = 2 * ch
    unit_d = tw1.shape[0]
    ds = unit_d * n_dp
    tp = up(pat, 16)
    kp = up(pat, 256)
    n_pack = up(images + 1 + b1.shape[1] // ch, 8)
    sds = jax.ShapeDtypeStruct
    per = lambda *s: pl.BlockSpec((1,) + s, lambda i: (i,) + (0,) * len(s))
    once = lambda *s: pl.BlockSpec(s, lambda i: (0,) * len(s))
    tokens = pl.BlockSpec((tp, full), lambda i: (i, 0))
    outs = [
        (sds((ni * tp, full), BF16), tokens),
        (sds((ni * tp, full), BF16), tokens),
        (sds((ni, tp, full), BF16), per(tp, full)),
        (sds((ni, kp, full), BF16), per(kp, full)),
        (sds((ni, ds, full), BF16), per(ds, full)),
        (sds((ni, ds, full), BF16), per(ds, full)),
        (sds((ni, tp, full), BF16), per(tp, full)),
        (sds((ni, tp, full), BF16), per(tp, full)),
        (sds((ni, 3, tp, 128), F32), per(3, tp, 128)),
        (sds((16, full), F32), once(16, full)),
        (sds((n_pack, full), F32), once(n_pack, full)),
        (sds((2, ds, kp), BF16), once(2, ds, kp)),
        (sds((2, tp, ds), BF16), once(2, tp, ds)),
        (sds(w1.shape, BF16), ANY),
        (sds(w2.shape, BF16), ANY),
    ]
    small = (b1, cb2, gain, shift, tw1, tb1, tw2, tb2, keep)
    return pl.pallas_call(
        functools.partial(front_kernel, (n_dp, ni, ch, pat, tp, unit_d)),
        grid=(ni,),
        out_shape=[o[0] for o in outs],
        in_specs=[ANY, ANY, once(*gp.shape), ANY, ANY] + [once(*a.shape) for a in small],
        out_specs=[o[1] for o in outs],
        scratch_shapes=[
            pltpu.VMEM((ni, pat, full), BF16),
            pltpu.VMEM((ni, pat, full), BF16),
            pltpu.VMEM((2 * unit_d, kp), BF16),
            pltpu.VMEM((128, 128), F32),
            pltpu.VMEM((n_pack, ch), F32),
            pltpu.VMEM((n_pack, full), F32),
            pltpu.VMEM((n_dp, 2 * unit_d, kp), BF16),
            pltpu.VMEM((2, ds, kp), F32),
            pltpu.VMEM((full, 128), BF16),
            pltpu.VMEM((kp, kp), F32),
            pltpu.VMEM((tp, 128), F32),
            pltpu.VMEM((tp, full), F32),
            pltpu.SemaphoreType.DMA((n_dp,)),
            pltpu.SemaphoreType.DMA((n_dp,)),
            pltpu.SemaphoreType.DMA((5,)),
            pltpu.SemaphoreType.DMA((5,)),
            pltpu.SemaphoreType.DMA((2,)),
        ],
        compiler_params=pltpu.CompilerParams(
            collective_id=0, has_side_effects=True, vmem_limit_bytes=VMEM_BYTES
        ),
        name="front",
    )(x, go, gp, w1, w2, *small)


def back_kernel(
    dims,
    st_hbm,
    yt_hbm,
    w1_hbm,
    w1p_hbm,
    w2_hbm,
    w2p_hbm,
    u0_hbm,
    f_hbm,
    hid_hbm,
    slope_hbm,
    mix_hbm,
    u1_hbm,
    col_hbm,
    norm_ref,
    pack_ref,
    tw_ref,
    twt_ref,
    bo_hbm,
    gi_hbm,
    pool_o,
    sq_o,
    red_o,
    gw_o,
    st,
    yt,
    sc,
    yc,
    w1s,
    w2s,
    bias,
    gh,
    ph,
    gs,
    pb,
    ra,
    r1,
    b2,
    r2,
    b3,
    r3,
    us,
    fs,
    hs,
    ls,
    ms,
    vs,
    cs,
    bos,
    gis,
    ob,
    sb,
    mg,
    ol,
    tg,
    fg,
    acc_norm,
    acc_tok,
    row_h,
    row_c,
    row_p,
    pool_a,
    pool_r,
    sq_a,
    sq_r,
    msgs,
    msgr,
    red_a,
    red_r,
    w_sem,
    in_sem,
    sa,
    rsa,
    s1,
    rs1,
    s2,
    rs2,
    s3,
    rs3,
    out_s,
    out_r,
    out_l,
    tok_s,
    tok_r,
    fin_s,
    fin_r,
):
    n_dp, ni, ch, pat, tp, unit_d, nz, ny, nx = dims
    dp, core = where_am_i()
    x = lax.rem(dp, nx)
    y = lax.rem(dp // nx, ny)
    z = dp // (nx * ny)
    other = (dp, 1 - core)
    x_dev = ((z * ny + y) * nx + (1 - x), core)
    y_dev = ((z * ny + (1 - y)) * nx + x, core)
    full = 2 * ch
    rows_own = full // n_dp
    half = w1s.shape[2]
    n_blk = half // BLK
    toks = ni * tp
    toks_pad = gh.shape[0]
    kp = fs.shape[1]
    my_first = core * ni
    ds = tw_ref.shape[1]
    images = 2 * ni

    loads = [
        pltpu.make_async_copy(st_hbm, st.at[pl.ds(0, toks)], w_sem.at[0]),
        pltpu.make_async_copy(yt_hbm, yt.at[pl.ds(0, toks)], w_sem.at[1]),
        pltpu.make_async_copy(w1p_hbm, w1s.at[1], w_sem.at[2]),
        pltpu.make_async_copy(w2p_hbm, w2s.at[1], w_sem.at[3]),
        pltpu.make_async_copy(w1_hbm, w1s.at[0], w_sem.at[4]),
        pltpu.make_async_copy(w2_hbm, w2s.at[0], w_sem.at[5]),
    ]
    for c in loads:
        c.start()

    def image_loads(i, slot):
        pairs = (
            (u0_hbm, us),
            (f_hbm, fs),
            (hid_hbm, hs),
            (slope_hbm, ls),
            (mix_hbm, ms),
            (u1_hbm, vs),
            (col_hbm, cs),
        )
        return [
            pltpu.make_async_copy(a.at[i], b.at[slot], in_sem.at[slot, n])
            for n, (a, b) in enumerate(pairs)
        ]

    for c in image_loads(0, 0):
        c.start()
    greet_all(n_dp, dp, core)

    zero_rows = jnp.zeros((toks_pad - toks, gh.shape[1]), BF16)
    gh[toks:, :] = zero_rows
    ph[toks:, :] = zero_rows
    sc[:, toks // 128 * 128 :] = jnp.zeros((full, toks_pad - toks // 128 * 128), BF16)
    yc[:, toks // 128 * 128 :] = jnp.zeros((full, toks_pad - toks // 128 * 128), BF16)
    row_h[...] = jnp.zeros_like(row_h)
    row_c[...] = jnp.zeros_like(row_c)
    row_p[...] = jnp.zeros_like(row_p)
    acc_norm[...] = jnp.zeros_like(acc_norm)
    acc_tok[...] = jnp.zeros_like(acc_tok)
    pool_a[...] = jnp.zeros_like(pool_a)
    sq_a[...] = jnp.zeros_like(sq_a)
    for n in range(half // ch):
        row = pack_ref[images + 1 + n : images + 2 + n, :]
        swapped = jnp.concatenate([row[:, ch:], row[:, :ch]], axis=1)
        row = jnp.where(core == 0, row, swapped)
        bias[0:1, n * ch : (n + 1) * ch] = row[:, :ch]
        bias[0:1, half + n * ch : half + (n + 1) * ch] = row[:, ch:]
    ol[...] = jnp.zeros_like(ol)
    ident = eye(256, 256)
    loads[0].wait()
    loads[1].wait()
    for c0 in range(0, full, 256):
        sc[c0 : c0 + 256, :toks] = nt(ident, st[:toks, c0 : c0 + 256]).astype(BF16)
        yc[c0 : c0 + 256, :toks] = nt(ident, yt[:toks, c0 : c0 + 256]).astype(BF16)
    for n in range(2, 6):
        loads[n].wait()

    def pair_copy(slot):
        return remote(pb.at[slot], ra.at[slot], sa.at[slot], rsa.at[slot], other)

    def first_copies(slot):
        return (
            remote(
                gs.at[slot, 0, :, :, 1 - x], r1.at[slot, 0], s1.at[slot, 0], rs1.at[slot, 0], x_dev
            ),
            remote(gs.at[slot, 1, :, 1 - y], r1.at[slot, 1], s1.at[slot, 1], rs1.at[slot, 1], y_dev),
        )

    def second_copies(slot):
        return (
            remote(b2.at[slot, 0, :, 1 - y], r2.at[slot, 0], s2.at[slot, 0], rs2.at[slot, 0], y_dev),
            remote(b2.at[slot, 1, :, 1 - x], r2.at[slot, 1], s2.at[slot, 1], rs2.at[slot, 1], x_dev),
        )

    def third_copies(slot):
        out = []
        for n in range(1, nz):
            to = lax.rem(z + n, nz)
            out.append(
                remote(
                    b3.at[slot, to],
                    r3.at[slot, n - 1],
                    s3.at[slot, n - 1],
                    rs3.at[slot, n - 1],
                    ((to * ny + y) * nx + x, core),
                )
            )
        return out

    def finish_third(j):
        slot = lax.rem(j, 2)
        for c in third_copies(slot):
            c.wait()
        at = pl.ds(pl.multiple_of(j * BLK, BLK), BLK)
        for m in range(2):
            v = b3[slot, z, m].astype(F32)
            for n in range(nz - 1):
                v = v + r3[slot, n, m].astype(F32)
            gw_o[m, :, at] = v

    def finish_second(j):
        slot = lax.rem(j, 2)
        for c in second_copies(slot):
            c.wait()
        for m, mine in ((0, y), (1, x)):
            for k in range(nz):
                v = b2[slot, m, k, mine].astype(F32) + r2[slot, m, k].astype(F32)
                b3[slot, k, m] = v.astype(BF16)
        for c in third_copies(slot):
            c.start()

    def finish_first(j):
        slot = lax.rem(j, 2)
        for c in first_copies(slot):
            c.wait()
        for k in range(nz):
            for n in range(2):
                v = gs[slot, 0, k, n, x].astype(F32) + r1[slot, 0, k, n].astype(F32)
                b2[slot, 0, k, n] = v.astype(BF16)
                v = gs[slot, 1, k, y, n].astype(F32) + r1[slot, 1, k, n].astype(F32)
                b2[slot, 1, k, n] = v.astype(BF16)
        for c in second_copies(slot):
            c.start()

    def hidden_block(side, j):
        at = pl.ds(pl.multiple_of(j * BLK, BLK), BLK)
        col = pl.ds(pl.multiple_of(side * half + j * BLK, BLK), BLK)
        w1 = w1s[side, :, at]
        w2 = w2s[side, at, :]
        b_row = bias[0:1, col]
        for i in range(ni):
            r0 = i * tp
            r = slice(r0, r0 + tp)
            pre = nn(st[r, :], w1)
            up_grad = nt(yt[r, :], w2)
            acc = jnp.zeros((8, BLK), F32)
            for a in range(0, tp, 16):
                v = pre[a : a + 16] + b_row
                cdf, pdf = gelu_parts(v)
                gh[r0 + a : r0 + a + 16, col] = (v * cdf).astype(BF16)
                p = up_grad[a : a + 16] * (cdf + v * pdf)
                ph[r0 + a : r0 + a + 16, col] = p.astype(BF16)
                acc += fold(p)
            row = jnp.sum(acc, 0, keepdims=True)
            row_h[0:1, col] += row
            row_h[1 + i : 2 + i, col] = row
        return nn(sc[...], ph[:, col]), nn(yc[...], gh[:, col])

    def split(v, k):
        per = full // nz
        return v[k * per : (k + 1) * per].reshape(ny, nx, rows_own, BLK)

    def block_step(j, carry):
        slot = lax.rem(j, 2)
        for m, v in enumerate(hidden_block(1, j)):
            for k in range(nz):
                pb[slot, m, k] = split(v, k).astype(BF16)
        pair_copy(slot).start()
        grads = hidden_block(0, j)
        pair_copy(slot).wait()
        for m, v in enumerate(grads):
            for k in range(nz):
                gs[slot, m, k] = (split(v, k) + ra[slot, m, k].astype(F32)).astype(BF16)

        @pl.when(j >= 3)
        def _():
            finish_third(j - 3)

        @pl.when(j >= 2)
        def _():
            finish_second(j - 2)

        @pl.when(j >= 1)
        def _():
            finish_first(j - 1)

        for c in first_copies(slot):
            c.start()
        return carry

    lax.fori_loop(0, n_blk, block_step, 0)

    def second_half(i):
        r = pl.ds(pl.multiple_of(i * tp, 16), tp)
        g = gh[r, :]
        p = ph[r, :]
        s = st[r, :]
        yv = yt[r, :]
        both = nt(s, s) * nt(p, p) + nt(g, g) * nt(yv, yv)
        sq = jnp.sum(jnp.sum(both, 0, keepdims=True), 1, keepdims=True)
        rh = row_h[pl.ds(1 + i, 1), :]
        rc = jnp.sum(fold(yv.astype(F32)), 0, keepdims=True)
        row_c[0:1, :] += rc
        sq = sq + jnp.sum(rh * rh, 1, keepdims=True) + jnp.sum(rc * rc, 1, keepdims=True)
        lane = lax.broadcasted_iota(jnp.int32, (1, 128), 1)
        sq_a[0:1, :] += jnp.where(lane == my_first + i, sq, 0.0)
        out = nn(gh[r, :half], w2s[0]) + nn(gh[r, half:], w2s[1])
        grad = nt(ph[r, :half], w1s[0]) + nt(ph[r, half:], w1s[1])
        ob[...] = out
        sb[...] = grad

    def drain(i):
        @pl.when(i == 0)
        def _():
            finish_third(n_blk - 3)
            finish_second(n_blk - 2)
            finish_first(n_blk - 1)

        @pl.when(i == 1)
        def _():
            finish_third(n_blk - 2)
            finish_second(n_blk - 1)

        @pl.when(i == 2)
        def _():
            finish_third(n_blk - 1)

    pieces = [slice(r, r + ROWS) for r in range(0, tp, ROWS)]

    def out_copies(i, slot):
        there = pl.ds(pl.multiple_of((1 - core) * ch, 128), ch)
        here = pl.ds(pl.multiple_of(core * ch, 128), ch)
        res = []
        for n, (src, dst) in enumerate(((bos, bo_hbm), (gis, gi_hbm))):
            res.append(
                remote(
                    src.at[slot, :, there],
                    dst.at[my_first + i],
                    out_s.at[slot, n],
                    out_r.at[i, n],
                    other,
                )
            )
            res.append(
                pltpu.make_async_copy(
                    src.at[slot, :, here], dst.at[my_first + i], out_l.at[slot, n]
                )
            )
        return res

    def out_arrivals(i):
        there = pl.ds(pl.multiple_of((1 - core) * ch, 128), ch)
        return [
            remote(
                src.at[0, :, there],
                dst.at[(1 - core) * ni + i],
                out_s.at[0, n],
                out_r.at[i, n],
                other,
            )
            for n, (src, dst) in enumerate(((bos, bo_hbm), (gis, gi_hbm)))
        ]

    def store_rows(ref, slot, r, v):
        stop = min(r.stop, pat)
        ref[slot, r.start : stop, :] = v[: stop - r.start].astype(BF16)

    def image_step(i, carry):
        slot = lax.rem(i, 2)
        second_half(i)
        drain(i)

        @pl.when(i + 1 < ni)
        def _():
            for c in image_loads(i + 1, 1 - slot):
                c.start()

        for c in image_loads(i, slot):
            c.wait()

        @pl.when(i >= 2)
        def _():
            for n, c in enumerate(out_copies(i - 2, slot)):
                if n % 2 == 0:
                    c.wait_send()
                else:
                    c.wait()

        chan_bias = pack_ref[images : images + 1, :]
        zero8 = jnp.zeros((8, full), F32)
        pool, gain, shift = zero8, zero8, zero8
        kept_sum = jnp.zeros((8, 128), F32)
        for r in pieces:
            kept = cs[slot, 2, r, :]
            kept_sum += fold(kept)
            bo = across(kept, full) * (ms[slot, r, :].astype(F32) + (ob[r, :] + chan_bias))
            pool += fold(bo)
            store_rows(bos, slot, r, bo)
            sg = sb[r, :]
            unit = vs[slot, r, :].astype(F32)
            gain += fold(sg * unit)
            shift += fold(sg)
            e = sg * norm_ref[1:2, :]
            m = jnp.sum(e, 1, keepdims=True) * (1.0 / full)
            n = jnp.sum(e * unit, 1, keepdims=True) * (1.0 / full)
            y_rows = pl.ds(pl.multiple_of(i * tp + r.start, 16), ROWS)
            v = yt[y_rows, :].astype(F32) + across(cs[slot, 1, r, :], full) * (e - m - unit * n)
            mg[r, :] = v
            ol[r, :] = v.astype(BF16)
        acc_norm[1] += gain
        acc_norm[3] += shift
        count = jnp.sum(kept_sum, 0, keepdims=True)
        pool_a[pl.ds(my_first + i, 1), :] = jnp.sum(pool, 0, keepdims=True) / across(count, full)
        for c in lane_pieces(full):
            hg = nn(tw_ref[1], ol[:, c])
            for a in range(0, ds, 32):
                r = slice(a, a + 32)
                tg[r, c] = (hg[r] * ls[slot, r, c].astype(F32)).astype(BF16)
            fg[:, c] = nn(twt_ref[0], tg[:, c])
        acc_tok[0] += nt(tg[...], fs[slot])
        acc_tok[1] += nt(hs[slot], ol[...])
        row_p[...] += nt(jnp.ones((16, full), BF16), ol[...])
        gain, shift = zero8, zero8
        for r in pieces:
            g = fg[r, :]
            unit = us[slot, r, :].astype(F32)
            gain += fold(g * unit)
            shift += fold(g)
            e = g * norm_ref[0:1, :]
            m = jnp.sum(e, 1, keepdims=True) * (1.0 / full)
            n = jnp.sum(e * unit, 1, keepdims=True) * (1.0 / full)
            v = mg[r, :] + across(cs[slot, 0, r, :], full) * (e - m - unit * n)
            store_rows(gis, slot, r, v)
        acc_norm[0] += gain
        acc_norm[2] += shift
        for c in out_copies(i, slot):
            c.start()
        return carry

    lax.fori_loop(0, ni, image_step, 0)

    h_0 = jnp.where(core == 0, row_h[0:1, :half], row_h[0:1, half:])
    h_1 = jnp.where(core == 0, row_h[0:1, half:], row_h[0:1, :half])
    norms = jnp.concatenate([jnp.sum(acc_norm[n], 0, keepdims=True) for n in range(4)], 0)
    norms = jnp.concatenate([norms, jnp.zeros((4, full), F32)], 0)
    per_h = half // n_dp
    per_c = ch // n_dp
    tail = msgs.shape[1] - 2 * unit_d

    def cut(v, start, size):
        n = v.shape[1]
        a = min(start // 128 * 128, n - 256)
        v = v[:, a : a + 256]
        if v.shape[0] == 1:
            v = jnp.broadcast_to(v, (8, 256))
        if start > a:
            v = pltpu.roll(v, 256 - (start - a), 1)
        lane = lax.broadcasted_iota(jnp.int32, v.shape, 1)
        return jnp.where(lane < size, v, 0.0)

    for d in range(n_dp):
        top = jnp.concatenate(
            [
                acc_tok[0, unit_d * d : unit_d * (d + 1), :],
                acc_tok[1, unit_d * d : unit_d * (d + 1), :],
            ],
            axis=0,
        )
        msgs[d, : 2 * unit_d, :] = top.astype(BF16)
        extra = jnp.concatenate(
            [
                row_p[0:1, :],
                cut(h_0, per_h * d, per_h)[0:1],
                cut(h_1, per_h * d, per_h)[0:1],
                cut(row_c[0:1, :], per_c * d, per_c)[0:1],
                cut(row_c[0:1, :], ch + per_c * d, per_c)[0:1],
                jnp.zeros((3, kp), F32),
                cut(norms, rows_own * d, rows_own),
            ],
            axis=0,
        )
        msgs[d, 2 * unit_d :, :] = extra.astype(BF16)

    def token_send(n):
        to = lax.rem(dp + n, n_dp)
        return remote(msgs.at[to], msgr.at[dp], tok_s.at[n], tok_r.at[dp], (to, core))

    def token_arrival(n):
        source = lax.rem(dp + n_dp - n, n_dp)
        return remote(
            msgs.at[source], msgr.at[source], tok_s.at[n], tok_r.at[source], (source, core)
        )

    def send(n, c):
        token_send(n).start()
        return c

    lax.fori_loop(1, n_dp, send, 0)
    pool_copy = remote(
        pool_a.at[:, pl.ds(pl.multiple_of((1 - core) * ch, 128), ch)], pool_r, fin_s.at[0], fin_r.at[0], other
    )
    pool_copy.start()
    sq_copy = remote(sq_a, sq_r, fin_s.at[1], fin_r.at[1], other)
    sq_copy.start()
    msgr[dp] = msgs[dp]

    def arrive(n, c):
        token_arrival(n).wait_recv()
        return c

    lax.fori_loop(1, n_dp, arrive, 0)
    total = msgr[0].astype(F32)
    for d in range(1, n_dp):
        total = total + msgr[d].astype(F32)
    red_a[...] = total
    red_copy = remote(red_a, red_r, fin_s.at[2], fin_r.at[2], other)
    red_copy.start()

    def sent(n, c):
        token_send(n).wait_send()
        return c

    lax.fori_loop(1, n_dp, sent, 0)
    for i in (ni - 2, ni - 1):
        for n, c in enumerate(out_copies(i, i % 2)):
            if n % 2 == 0:
                c.wait_send()
            else:
                c.wait()
    for i in range(ni):
        for c in out_arrivals(i):
            c.wait_recv()
    pool_copy.wait()
    sq_copy.wait()
    pool_o[...] = pool_a[:, pl.ds(pl.multiple_of(core * ch, 128), ch)] + pool_r[...]
    sq_o[...] = sq_a[...] + sq_r[...]
    red_copy.wait()
    red_o[...] = red_a[...] + red_r[...]


def back(n_dp, grid3, st, yt, w1, w1p, w2, w2p, u0, f, hid, slope, mix, u1, col, norm, pack, tw, twt, pat):
    ni, tp, full = u0.shape
    ch = full // 2
    half = w1.shape[1]
    toks = st.shape[0]
    ds, kp = tw.shape[1:]
    unit_d = ds // n_dp
    toks_pad = up(toks, 256)
    nz, ny, nx = grid3
    rows_own = full // n_dp
    n_msg = 2 * unit_d + 16
    sds = jax.ShapeDtypeStruct
    vm = pltpu.VMEM
    dma = pltpu.SemaphoreType.DMA
    part = (nz, ny, nx, rows_own, BLK)
    return pl.pallas_call(
        functools.partial(back_kernel, (n_dp, ni, ch, pat, tp, unit_d, nz, ny, nx)),
        out_shape=[
            sds((2 * ni, pat, ch), BF16),
            sds((2 * ni, pat, ch), BF16),
            sds((up(2 * ni, 8), ch), F32),
            sds((8, 128), F32),
            sds((n_msg, kp), F32),
            sds((2, rows_own, half), F32),
        ],
        in_specs=[ANY] * 13 + [VM] * 4,
        out_specs=[ANY, ANY, VM, VM, VM, VM],
        scratch_shapes=[
            vm((toks_pad, full), BF16),
            vm((toks_pad, full), BF16),
            vm((full, toks_pad), BF16),
            vm((full, toks_pad), BF16),
            vm((2, full, half), BF16),
            vm((2, half, full), BF16),
            vm((8, 2 * half), F32),
            vm((toks_pad, 2 * half), BF16),
            vm((toks_pad, 2 * half), BF16),
            vm((2, 2) + part, BF16),
            vm((2, 2) + part, BF16),
            vm((2, 2) + part, BF16),
            vm((2, 2, nz, 2, rows_own, BLK), BF16),
            vm((2, 2, nz, 2, rows_own, BLK), BF16),
            vm((2, 2, nz, rows_own, BLK), BF16),
            vm((2, nz, 2, rows_own, BLK), BF16),
            vm((2, nz - 1, 2, rows_own, BLK), BF16),
            vm((2, tp, full), BF16),
            vm((2, kp, full), BF16),
            vm((2, ds, full), BF16),
            vm((2, ds, full), BF16),
            vm((2, tp, full), BF16),
            vm((2, tp, full), BF16),
            vm((2, 3, tp, 128), F32),
            vm((2, pat, full), BF16),
            vm((2, pat, full), BF16),
            vm((tp, full), F32),
            vm((tp, full), F32),
            vm((tp, full), F32),
            vm((kp, full), BF16),
            vm((ds, full), BF16),
            vm((tp, full), F32),
            vm((4, 8, full), F32),
            vm((2, ds, kp), F32),
            vm((8, 2 * half), F32),
            vm((8, full), F32),
            vm((16, kp), F32),
            vm((up(2 * ni, 8), full), F32),
            vm((up(2 * ni, 8), ch), F32),
            vm((8, 128), F32),
            vm((8, 128), F32),
            vm((n_dp, n_msg, kp), BF16),
            vm((n_dp, n_msg, kp), BF16),
            vm((n_msg, kp), F32),
            vm((n_msg, kp), F32),
            dma((6,)),
            dma((2, 7)),
            dma((2,)),
            dma((2,)),
            dma((2, 2)),
            dma((2, 2)),
            dma((2, 2)),
            dma((2, 2)),
            dma((2, nz - 1)),
            dma((2, nz - 1)),
            dma((2, 2)),
            dma((ni, 2)),
            dma((2, 2)),
            dma((n_dp,)),
            dma((n_dp,)),
            dma((3,)),
            dma((3,)),
        ],
        compiler_params=pltpu.CompilerParams(
            collective_id=1, has_side_effects=True, vmem_limit_bytes=VMEM_BYTES
        ),
        name="back",
    )(st, yt, w1, w1p, w2, w2p, u0, f, hid, slope, mix, u1, col, norm, pack, tw, twt)


def finish_kernel(
    dims,
    bo_ref,
    gi_ref,
    pool_ref,
    sq_ref,
    red_ref,
    gw_ref,
    bo_o,
    pool_o,
    gi_o,
    gain_o,
    shift_o,
    tw1_o,
    tb1_o,
    tw2_o,
    tb2_o,
    w1_o,
    b1_o,
    w2_o,
    b2_o,
    sq_o,
):
    pat, unit_d, per_h, per_c = dims
    _, core = where_am_i()
    bo_o[...] = bo_ref[...].astype(F32)
    gi_o[...] = gi_ref[...].astype(F32)

    @pl.when(pl.program_id(0) == 0)
    def _():
        images = pool_o.shape[0]
        pool_o[...] = pool_ref[:images, :]
        sq_o[...] = sq_ref[0:1, :images]
        red = red_ref[...]
        n = 2 * unit_d
        tw1_o[...] = red[:unit_d, :pat]
        tw2_o[...] = red[unit_d:n, :pat]
        gain_o[...] = red[n + 8 : n + 10, :n]
        shift_o[...] = red[n + 10 : n + 12, :n]
        tb1_o[...] = jnp.transpose(red[: up(unit_d, 8), 128:])[pat - 128 : pat - 127, :unit_d]
        tb2_o[...] = red[n : n + 1, :pat]
        w1_o[...] = gw_ref[0]
        w2_o[...] = gw_ref[1]
        b1_o[...] = jnp.where(core == 0, red[n + 1 : n + 2, :per_h], red[n + 2 : n + 3, :per_h])
        b2_o[...] = jnp.where(core == 0, red[n + 3 : n + 4, :per_c], red[n + 4 : n + 5, :per_c])


def finish(bo, gi, pool, sq, red, gw, unit_d, per_h, per_c):
    images, pat, ch = bo.shape
    ds = unit_d
    sds = jax.ShapeDtypeStruct
    once = lambda s: pl.BlockSpec(s, lambda i: (0,) * len(s))
    steps = 4 if images % 4 == 0 else images
    per = pl.BlockSpec((images // steps, pat, ch), lambda i: (i, 0, 0))
    rows_own, half = gw.shape[1:]
    outs = [
        (images, pat, ch),
        (images, ch),
        (images, pat, ch),
        (2, rows_own),
        (2, rows_own),
        (ds, pat),
        (1, ds),
        (ds, pat),
        (1, pat),
        (rows_own, half),
        (1, per_h),
        (rows_own, half),
        (1, per_c),
        (1, images),
    ]
    res = pl.pallas_call(
        functools.partial(finish_kernel, (pat, unit_d, per_h, per_c)),
        grid=(steps,),
        out_shape=[sds(s, F32) for s in outs],
        in_specs=[per, per] + [once(a.shape) for a in (pool, sq, red, gw)],
        out_specs=[per if len(s) == 3 else once(s) for s in outs],
        compiler_params=pltpu.CompilerParams(vmem_limit_bytes=VMEM_BYTES),
        name="finish",
    )(bo, gi, pool, sq, red, gw)
    res = [r.reshape(-1) if r.shape[0] == 1 else r for r in res]
    for n in (0, 2):
        res[n] = jnp.swapaxes(res[n], 1, 2)
    for n in (5, 11):
        res[n] = res[n].T
    return tuple(res)


def fused_body(
    n_dp,
    grid3,
    mixer_input,
    keep_mask,
    ln_gain,
    ln_shift,
    token_w1,
    token_b1,
    token_w2,
    token_b2,
    chan_w1,
    chan_b1,
    chan_w2,
    chan_b2,
    grad_out,
    grad_pooled,
):
    images, ch, pat = mixer_input.shape
    unit_d = token_b1.shape[0]
    half = chan_b1.shape[0]
    st, yt, u0, f, hid, slope, mix, u1, col, norm, pack, tw, twt, w1p, w2p = front(
        n_dp,
        jnp.swapaxes(mixer_input, 1, 2),
        jnp.swapaxes(grad_out, 1, 2),
        grad_pooled,
        chan_w1,
        chan_w2,
        chan_b1.reshape(1, -1),
        chan_b2.reshape(1, -1),
        ln_gain,
        ln_shift,
        token_w1.T,
        token_b1.reshape(1, -1),
        token_w2,
        token_b2.reshape(1, -1),
        keep_mask,
    )
    bo, gi, pool, sq, red, gw = back(
        n_dp, grid3, st, yt, chan_w1, w1p, chan_w2, w2p, u0, f, hid, slope, mix, u1, col,
        norm, pack, tw, twt, pat,
    )
    return finish(bo, gi, pool, sq, red, gw, unit_d, half // n_dp, ch // n_dp)


D = 768


epsilon = 1e-05


def gelu_exact(values_in):
    return jax.nn.gelu(values_in, approximate=False)


def gelu_slope(pre_sum, upstream):
    unused, backward = jax.vjp(gelu_exact, pre_sum)
    return backward(upstream)[0]


def channel_sums(first_term, second_term):
    return lax.psum((first_term, second_term), "tensor")


def normalize(values_in, gains, shifts):
    totals, square = channel_sums(jnp.sum(values_in, 1), jnp.sum(values_in * values_in, 1))
    average = totals / D
    spread = square / D - average * average
    scaling = lax.rsqrt(spread + epsilon)[:, None, :]
    unit_part = (values_in - average[:, None, :]) * scaling
    return (unit_part * gains[None, :, None] + shifts[None, :, None], unit_part, scaling)


def normalize_back(upstream, unit_part, scaling, gains):
    scaled = upstream * gains[None, :, None]
    totals, along_unit = channel_sums(jnp.sum(scaled, 1), jnp.sum(scaled * unit_part, 1))
    inner_part = scaled - totals[:, None, :] / D - unit_part * along_unit[:, None, :] / D
    return (scaling * inner_part, jnp.sum(upstream * unit_part, (0, 2)), jnp.sum(upstream, (0, 2)))


def body(
    mixer_input,
    keep_mask,
    ln_gain,
    ln_shift,
    token_w1,
    token_b1,
    token_w2,
    token_b2,
    chan_w1,
    chan_b1,
    chan_w2,
    chan_b2,
    grad_out,
    grad_pooled,
):
    images, channels, patches = mixer_input.shape
    full_width = channels * lax.axis_size("tensor")
    offset = lax.axis_index("tensor") * channels
    gains, shifts, weight_in, bias_in, weight_back = (
        lax.all_gather(ln_gain, "dp", axis=1, tiled=True),
        lax.all_gather(ln_shift, "dp", axis=1, tiled=True),
        lax.all_gather(token_w1, "dp", axis=1, tiled=True),
        lax.all_gather(token_b1, "dp", axis=0, tiled=True),
        lax.all_gather(token_w2, "dp", axis=0, tiled=True),
    )
    gain_own = lax.dynamic_slice_in_dim(gains, offset, channels, 1).astype(jnp.float32)
    shift_own = lax.dynamic_slice_in_dim(shifts, offset, channels, 1).astype(jnp.float32)
    kept = keep_mask.astype(jnp.float32)
    counts = jnp.sum(kept, 1)
    source = mixer_input.astype(jnp.float32)
    normed, unit_first, scale_first = normalize(source, gain_own[0], shift_own[0])
    first_low = normed.astype(jnp.bfloat16)
    token_pre = jnp.einsum(
        "bcp,ph->bch", first_low, weight_in, preferred_element_type=jnp.float32
    ) + bias_in.astype(jnp.float32)
    token_hid = gelu_exact(token_pre).astype(jnp.bfloat16)
    token_out = jnp.einsum(
        "bch,hp->bcp", token_hid, weight_back, preferred_element_type=jnp.float32
    ) + token_b2.astype(jnp.float32)
    mixture = source + token_out
    normed, unit_second, scale_second = normalize(mixture, gain_own[1], shift_own[1])
    second = normed.astype(jnp.bfloat16)
    section = lax.all_gather(second, "tensor", axis=1, tiled=True)
    pre_sum = jnp.einsum("bcp,ch->bhp", section, chan_w1, preferred_element_type=jnp.float32)
    gathered = section
    grams = jnp.einsum("bcp,bcq->bpq", section, section, preferred_element_type=jnp.float32)
    chan_pre = pre_sum
    gram_second = grams
    chan_pre = chan_pre + chan_b1.astype(jnp.float32)[None, :, None]
    chan_hid = gelu_exact(chan_pre).astype(jnp.bfloat16)
    partial_value = jnp.einsum("bhp,hc->bcp", chan_hid, chan_w2, preferred_element_type=jnp.float32)
    chan_out = (
        lax.psum_scatter(
            partial_value.astype(jnp.bfloat16), "tensor", scatter_dimension=1, tiled=True
        ).astype(jnp.float32)
        + chan_b2.astype(jnp.float32)[None, :, None]
    )
    masked = kept[:, None, :] * (mixture + chan_out)
    pooled = jnp.sum(masked, 2) / counts[:, None]
    grad_result = kept[:, None, :] * (
        grad_out.astype(jnp.float32) + grad_pooled[:, :, None] / counts[:, None, None]
    )
    grad_low = grad_result.astype(jnp.bfloat16)
    grad_chan_b2 = jnp.sum(grad_low, (0, 2), dtype=jnp.float32)
    section = lax.all_gather(grad_low, "tensor", axis=1, tiled=True)
    hid_sum = jnp.einsum("bcp,hc->bhp", section, chan_w2, preferred_element_type=jnp.float32)
    column_block = jnp.einsum("bhp,bcp->hc", chan_hid, section, preferred_element_type=jnp.float32)
    grams = jnp.einsum("bcp,bcq->bpq", section, section, preferred_element_type=jnp.float32)
    pre_grad = gelu_slope(chan_pre, hid_sum).astype(jnp.bfloat16)
    grad_chan_b1 = jnp.sum(pre_grad, (0, 2), dtype=jnp.float32)
    grad_chan_w1 = jnp.einsum("bcp,bhp->ch", gathered, pre_grad, preferred_element_type=jnp.float32)
    share_w1, share_b1, share_w2, share_b2 = (
        lax.psum_scatter(
            grad_chan_w1.astype(jnp.bfloat16), "dp", scatter_dimension=0, tiled=True
        ).astype(jnp.float32),
        lax.psum_scatter(
            grad_chan_b1.astype(jnp.bfloat16), "dp", scatter_dimension=0, tiled=True
        ).astype(jnp.float32),
        lax.psum_scatter(
            column_block.astype(jnp.bfloat16), "dp", scatter_dimension=1, tiled=True
        ).astype(jnp.float32),
        lax.psum_scatter(
            grad_chan_b2.astype(jnp.bfloat16), "dp", scatter_dimension=0, tiled=True
        ).astype(jnp.float32),
    )
    second_part = jnp.einsum("bhp,ch->bcp", pre_grad, chan_w1, preferred_element_type=jnp.float32)
    second_grad = lax.psum_scatter(
        second_part.astype(jnp.bfloat16), "tensor", scatter_dimension=1, tiled=True
    ).astype(jnp.float32)
    gram_pre = jnp.einsum("bhp,bhq->bpq", pre_grad, pre_grad, preferred_element_type=jnp.float32)
    gram_hid = jnp.einsum("bhp,bhq->bpq", chan_hid, chan_hid, preferred_element_type=jnp.float32)
    own_terms = jnp.sum(gram_second * gram_pre + gram_hid * grams, (1, 2))
    own_terms = own_terms + jnp.sum(jnp.square(jnp.sum(pre_grad, 2, dtype=jnp.float32)), 1)
    own_terms = own_terms + jnp.sum(jnp.square(jnp.sum(grad_low, 2, dtype=jnp.float32)), 1)
    example_sq = lax.psum(own_terms, "tensor")
    back_second, gain_second, shift_second = normalize_back(
        second_grad, unit_second, scale_second, gain_own[1]
    )
    mixture_grad = grad_result + back_second
    out_low = mixture_grad.astype(jnp.bfloat16)
    grad_token_b2 = jnp.sum(out_low, (0, 1), dtype=jnp.float32)
    token_hid_grad = jnp.einsum(
        "bcp,hp->bch", out_low, weight_back, preferred_element_type=jnp.float32
    )
    grad_token_w2 = jnp.einsum(
        "bch,bcp->hp", token_hid, out_low, preferred_element_type=jnp.float32
    )
    token_pre_grad = gelu_slope(token_pre, token_hid_grad).astype(jnp.bfloat16)
    grad_token_b1 = jnp.sum(token_pre_grad, (0, 1), dtype=jnp.float32)
    grad_token_w1 = jnp.einsum(
        "bcp,bch->ph", first_low, token_pre_grad, preferred_element_type=jnp.float32
    )
    first_grad = jnp.einsum(
        "bch,ph->bcp", token_pre_grad, weight_in, preferred_element_type=jnp.float32
    )
    back_first, gain_first, shift_first = normalize_back(
        first_grad, unit_first, scale_first, gain_own[0]
    )
    grad_input = mixture_grad + back_first
    gain_parts = lax.dynamic_update_slice_in_dim(
        jnp.zeros((2, full_width), jnp.float32), jnp.stack([gain_first, gain_second]), offset, 1
    )
    shift_parts = lax.dynamic_update_slice_in_dim(
        jnp.zeros((2, full_width), jnp.float32), jnp.stack([shift_first, shift_second]), offset, 1
    )
    total_gain, total_shift, total_w1, total_b1, total_w2 = (
        lax.psum(gain_parts.astype(jnp.bfloat16), "tensor").astype(jnp.float32),
        lax.psum(shift_parts.astype(jnp.bfloat16), "tensor").astype(jnp.float32),
        lax.psum(grad_token_w1.astype(jnp.bfloat16), "tensor").astype(jnp.float32),
        lax.psum(grad_token_b1.astype(jnp.bfloat16), "tensor").astype(jnp.float32),
        lax.psum(grad_token_w2.astype(jnp.bfloat16), "tensor").astype(jnp.float32),
    )
    share_gain, share_shift, share_tw1, share_tb1, share_tw2 = (
        lax.psum_scatter(
            total_gain.astype(jnp.bfloat16), "dp", scatter_dimension=1, tiled=True
        ).astype(jnp.float32),
        lax.psum_scatter(
            total_shift.astype(jnp.bfloat16), "dp", scatter_dimension=1, tiled=True
        ).astype(jnp.float32),
        lax.psum_scatter(
            total_w1.astype(jnp.bfloat16), "dp", scatter_dimension=1, tiled=True
        ).astype(jnp.float32),
        lax.psum_scatter(
            total_b1.astype(jnp.bfloat16), "dp", scatter_dimension=0, tiled=True
        ).astype(jnp.float32),
        lax.psum_scatter(
            total_w2.astype(jnp.bfloat16), "dp", scatter_dimension=0, tiled=True
        ).astype(jnp.float32),
    )
    share_tb2 = lax.psum(grad_token_b2, ("dp", "tensor"))
    return (
        masked,
        pooled,
        grad_input,
        share_gain,
        share_shift,
        share_tw1,
        share_tb1,
        share_tw2,
        share_tb2,
        share_w1,
        share_b1,
        share_w2,
        share_b2,
        example_sq,
    )


def solution(mesh):
    n_dp, n_tensor = mesh.shape["dp"], mesh.shape["tensor"]
    chosen = body
    if (n_dp, n_tensor) == (16, 2):
        chosen = functools.partial(fused_body, n_dp, (4, 2, 2))
    return jax.shard_map(
        chosen,
        mesh=mesh,
        in_specs=(
            P("dp", "tensor", None),
            P("dp", None),
            P(None, "dp"),
            P(None, "dp"),
            P(None, "dp"),
            P("dp"),
            P("dp", None),
            P(),
            P(None, "tensor"),
            P("tensor"),
            P("tensor", None),
            P("tensor"),
            P("dp", "tensor", None),
            P("dp", "tensor"),
        ),
        out_specs=(
            P("dp", "tensor", None),
            P("dp", "tensor"),
            P("dp", "tensor", None),
            P(None, "dp"),
            P(None, "dp"),
            P(None, "dp"),
            P("dp"),
            P("dp", None),
            P(),
            P("dp", "tensor"),
            P(("tensor", "dp")),
            P("tensor", "dp"),
            P(("tensor", "dp")),
            P("dp"),
        ),
        check_vma=False,
    )
```

```python
import functools
import math

import jax
import jax.numpy as jnp
from jax import lax
from jax.experimental import pallas as pl
from jax.experimental.pallas import tpu as pltpu
from jax.sharding import PartitionSpec as P

MESH = pl.DeviceIdType.MESH
EPS = 1e-05
F32 = jnp.float32
BF16 = jnp.bfloat16
VM = pl.BlockSpec(memory_space=pltpu.VMEM)
ANY = pl.BlockSpec(memory_space=pl.ANY)
BLK = 256
VMEM_BYTES = 63 * 2**20


def up(n, m):
    return -(-n // m) * m


def nn(a, b):
    return lax.dot_general(a, b, (((1,), (0,)), ((), ())), preferred_element_type=F32)


def nt(a, b):
    return lax.dot_general(a, b, (((1,), (1,)), ((), ())), preferred_element_type=F32)


def tn(a, b):
    return lax.dot_general(a, b, (((0,), (0,)), ((), ())), preferred_element_type=F32)


def eye(rows, cols):
    r = lax.broadcasted_iota(jnp.int32, (rows, cols), 0)
    c = lax.broadcasted_iota(jnp.int32, (rows, cols), 1)
    return (r == c).astype(F32).astype(BF16)


def gelu_parts(v):
    cdf = 0.5 + 0.5 * lax.erf(v * math.sqrt(0.5))
    return cdf, jnp.exp(-0.5 * (v * v)) * (1.0 / math.sqrt(2.0 * math.pi))


def fold(v):
    return jnp.sum(v.reshape(v.shape[0] // 8, 8, v.shape[1]), 0)


def where_am_i():
    return lax.axis_index("dp"), lax.axis_index("tensor")


def greet_all(dp_size, dp, core):
    barrier = pltpu.get_barrier_semaphore()

    def one(n, c):
        pl.semaphore_signal(
            barrier, inc=1, device_id=(lax.rem(dp + n, dp_size), core), device_id_type=MESH
        )
        return c

    lax.fori_loop(1, dp_size, one, 0)
    pl.semaphore_signal(barrier, inc=1, device_id=(dp, 1 - core), device_id_type=MESH)
    pl.semaphore_wait(barrier, dp_size)


def remote(src, dst, send, recv, device):
    return pltpu.make_async_remote_copy(
        src_ref=src,
        dst_ref=dst,
        send_sem=send,
        recv_sem=recv,
        device_id=device,
        device_id_type=MESH,
    )


ROWS = 16


def row_pieces(pat):
    return [slice(r, min(r + ROWS, pat)) for r in range(0, pat, ROWS)]


def lane_pieces(full):
    return [slice(c, c + 256) for c in range(0, full, 256)]


def across(v, full):
    return jnp.concatenate([v] * (full // 128), axis=1)


def centre(v):
    n = v.shape[1]
    d = v - jnp.sum(v, 1, keepdims=True) * (1.0 / n)
    r = lax.rsqrt(jnp.sum(d * d, 1, keepdims=True) * (1.0 / n) + EPS)
    return d * r, r


def mixer_kernel(
    dims,
    x_hbm,
    go_hbm,
    gp_ref,
    w1_hbm,
    w2_hbm,
    b1_ref,
    cb2_ref,
    gain_ref,
    shift_ref,
    tw1_ref,
    tb1_ref,
    tw2_ref,
    tb2_ref,
    keep_ref,
    bo_hbm,
    gi_hbm,
    u0_hbm,
    f_hbm,
    hid_hbm,
    slope_hbm,
    mix_hbm,
    u1_hbm,
    pool_o,
    sq_o,
    red_o,
    gw_o,
    xf,
    gof,
    msg,
    square,
    pack,
    packf,
    tok,
    tmp_w,
    prm,
    keep_t,
    tb2_w,
    norm,
    tw,
    twt,
    st,
    yt,
    w1s,
    w2s,
    bias,
    gh,
    ph,
    gs,
    pb,
    ra,
    r1,
    b2,
    r2,
    b3,
    r3,
    us,
    fs,
    hs,
    ls,
    ms,
    vs,
    cs,
    bos,
    gis,
    ob,
    mg,
    ol,
    tg,
    fg,
    acc_norm,
    acc_tok,
    row_h,
    row_c,
    row_p,
    pool_a,
    pool_r,
    sq_a,
    sq_r,
    msgs,
    msgr,
    red_a,
    red_r,
    tg_s,
    tg_r,
    pair_send,
    pair_recv,
    loc_sem,
    spill,
    in_sem,
    sa,
    rsa,
    s1,
    rs1,
    s2,
    rs2,
    s3,
    rs3,
    out_s,
    out_r,
    out_l,
    tok_s,
    tok_r,
    fin_s,
    fin_r,
):
    n_dp, ni, ch, pat, tp, unit_d, nz, ny, nx = dims
    dp, core = where_am_i()
    x = lax.rem(dp, nx)
    y = lax.rem(dp // nx, ny)
    z = dp // (nx * ny)
    other = (dp, 1 - core)
    x_dev = ((z * ny + y) * nx + (1 - x), core)
    y_dev = ((z * ny + (1 - y)) * nx + x, core)
    full = 2 * ch
    rows_own = full // n_dp
    half = w1s.shape[2]
    n_blk = half // BLK
    toks = ni * tp
    toks_pad = gh.shape[0]
    kp = fs.shape[1]
    my_first = core * ni
    ds = tw.shape[1]
    images = 2 * ni
    here = pl.ds(pl.multiple_of(core * ch, 128), ch)
    there = pl.ds(pl.multiple_of((1 - core) * ch, 128), ch)
    bias_rows = half // ch
    pieces = [slice(r, r + ROWS) for r in range(0, tp, ROWS)]

    ours = pl.ds(my_first, ni)
    theirs = pl.ds((1 - core) * ni, ni)
    pair_copies = [
        remote(a, b, pair_send.at[n], pair_recv.at[n], other)
        for n, (a, b) in enumerate(
            (
                (pack, packf.at[:, here]),
                (x_hbm.at[theirs], xf.at[:, :, here]),
                (go_hbm.at[theirs], gof.at[:, :, here]),
                (w1_hbm, w1s.at[1]),
                (w2_hbm, w2s.at[1]),
            )
        )
    ]
    local_copies = [
        pltpu.make_async_copy(a, b, loc_sem.at[n])
        for n, (a, b) in enumerate(
            (
                (x_hbm.at[ours], xf.at[:, :, here]),
                (go_hbm.at[ours], gof.at[:, :, here]),
                (w1_hbm, w1s.at[0]),
                (w2_hbm, w2s.at[0]),
            )
        )
    ]

    def weights_copy(n):
        to = lax.rem(dp + n, n_dp)
        return remote(msg, tok.at[dp], tg_s.at[n], tg_r.at[dp], (to, core))

    def weights_arrival(n):
        source = lax.rem(dp + n_dp - n, n_dp)
        return remote(msg, tok.at[source], tg_s.at[n], tg_r.at[source], (source, core))

    for c in local_copies:
        c.start()
    square[...] = jnp.zeros_like(square)
    at = pat - 128
    square[at : at + 1, :unit_d] = tb1_ref[...].astype(F32)
    square[at + 4 : at + 6, :rows_own] = gain_ref[...].astype(F32)
    square[at + 6 : at + 8, :rows_own] = shift_ref[...].astype(F32)
    columns = jnp.transpose(square[...])[:rows_own]
    tmp_w[0, :rows_own, :] = jnp.zeros((rows_own, kp), F32)
    tmp_w[0, :unit_d, :pat] = tw1_ref[...].astype(F32)
    tmp_w[0, unit_d:rows_own, :pat] = tw2_ref[...].astype(F32)
    msg[:, :128] = tmp_w[0, :rows_own, :128].astype(BF16)
    msg[:, 128:] = (tmp_w[0, :rows_own, 128:] + columns).astype(BF16)
    pack[...] = jnp.zeros_like(pack)
    pack[:images, :] = gp_ref[...]
    pack[images : images + 1, :] = cb2_ref[...].astype(F32)
    for n in range(bias_rows):
        pack[images + 1 + n : images + 2 + n, :] = b1_ref[:, n * ch : (n + 1) * ch].astype(F32)
    greet_all(n_dp, dp, core)

    def send(n, c):
        weights_copy(n).start()
        return c

    lax.fori_loop(1, n_dp, send, 0)
    for c in pair_copies:
        c.start()

    tok[dp] = msg[...]
    packf[:, here] = pack[...]
    keep_t[...] = jnp.zeros_like(keep_t)
    keep_t[:images, :pat] = keep_ref[...].astype(F32)
    keep_t[images : images + 1, :pat] = tb2_ref[...].astype(F32)
    turned = jnp.transpose(keep_t[...])
    keep_t[...] = turned
    tb2_w[...] = jnp.broadcast_to(turned[:tp, images : images + 1], (tp, 128))
    zero_rows = jnp.zeros((toks_pad - toks, gh.shape[1]), BF16)
    gh[toks:, :] = zero_rows
    ph[toks:, :] = zero_rows
    st[toks:, :] = zero_rows[:, :full]
    yt[toks:, :] = zero_rows[:, :full]
    for ref in (row_h, row_c, row_p, acc_norm, acc_tok, pool_a, sq_a, ol):
        ref[...] = jnp.zeros_like(ref)
    partial = row_pieces(pat)
    last = slice(pat // ROWS * ROWS, tp)
    blank = jnp.zeros((last.stop - last.start, full), BF16)
    for n in range(2):
        us[n, last, :] = blank
        vs[n, last, :] = blank
        ms[n, last, :] = blank
        fs[n, last.start :, :] = jnp.zeros((kp - last.start, full), BF16)
        fs[n, pat : pat + 1, :] = jnp.ones((1, full), BF16)
    for c in local_copies[:2]:
        c.wait()
    for c in pair_copies[:3]:
        c.wait_recv()

    def token_rows(i, r):
        return pl.ds(pl.multiple_of(i * tp + r.start, 16), r.stop - r.start)

    def early_step(i, carry):
        number = my_first + i
        count = jnp.sum(keep_ref[pl.ds(number, 1), :].astype(F32), 1, keepdims=True)
        g = packf[pl.ds(number, 1), :] / count
        rows = token_rows(i, last)
        st[rows, :] = blank
        yt[rows, :] = blank
        cs[i, :, last, :] = jnp.zeros((3, tp - last.start, 128), F32)
        for r in partial:
            size = r.stop - r.start
            rows = token_rows(i, r)
            unit, rstd = centre(xf[i, r, :].astype(F32))
            st[rows, :] = unit.astype(BF16)
            cs[i, 0, r, :] = jnp.broadcast_to(rstd, (size, 128))
            lane = lax.broadcasted_iota(jnp.int32, (size, 128), 1)
            k = jnp.sum(jnp.where(lane == number, keep_t[r, :128], 0.0), 1, keepdims=True)
            yt[rows, :] = (k * (gof[i, r, :].astype(F32) + g)).astype(BF16)
            cs[i, 2, r, :] = jnp.broadcast_to(k, (size, 128))
        return carry

    lax.fori_loop(0, ni, early_step, 0)
    for n in range(bias_rows):
        row = packf[images + 1 + n : images + 2 + n, :]
        swapped = jnp.concatenate([row[:, ch:], row[:, :ch]], axis=1)
        row = jnp.where(core == 0, row, swapped)
        bias[0:1, n * ch : (n + 1) * ch] = row[:, :ch]
        bias[0:1, half + n * ch : half + (n + 1) * ch] = row[:, ch:]

    def arrive_w(n, c):
        weights_arrival(n).wait_recv()
        return c

    lax.fori_loop(1, n_dp, arrive_w, 0)
    lane = lax.broadcasted_iota(jnp.int32, (unit_d, kp), 1)
    for d in range(n_dp):
        block = tok[d].astype(F32)
        tmp_w[0, unit_d * d : unit_d * (d + 1), :] = jnp.where(lane <= pat, block[:unit_d], 0.0)
        tmp_w[1, unit_d * d : unit_d * (d + 1), :] = jnp.where(lane < pat, block[unit_d:], 0.0)
        prm[rows_own * d : rows_own * (d + 1), :] = tok[d, :, 128:]
    r = lax.broadcasted_iota(jnp.int32, (16, 128), 0)
    c = lax.broadcasted_iota(jnp.int32, (16, 128), 1)
    norm[...] = nt(((c - (at + 4) == r) & (r < 4)).astype(F32).astype(BF16), prm[...])
    ident = eye(kp, kp)
    for n in range(2):
        w = tmp_w[n].astype(BF16)
        tw[n] = w
        t = nt(ident, w)
        r = lax.broadcasted_iota(jnp.int32, t.shape, 0)
        twt[n] = jnp.where(r < pat, t, 0.0)[:tp].astype(BF16)

    def saved(i):
        slot = lax.rem(i, 2)
        pairs = (
            (us, u0_hbm),
            (fs, f_hbm),
            (hs, hid_hbm),
            (ls, slope_hbm),
            (vs, u1_hbm),
            (ms, mix_hbm),
        )
        return [
            pltpu.make_async_copy(a.at[slot], b.at[i], spill.at[slot, n])
            for n, (a, b) in enumerate(pairs)
        ]

    def token_step(i, carry):
        slot = lax.rem(i, 2)

        @pl.when(i >= 2)
        def _():
            for c in saved(i - 2):
                c.wait()

        for r in partial:
            unit = st[token_rows(i, r), :]
            us[slot, r, :] = unit
            f = unit.astype(F32) * norm[0:1, :] + norm[2:3, :]
            fs[slot, r, :] = f.astype(BF16)
        for c in lane_pieces(full):
            pre = nn(tw[0], fs[slot, :, c])
            for a in range(0, ds, 32):
                v = pre[a : a + 32]
                cdf, pdf = gelu_parts(v)
                hs[slot, a : a + 32, c] = (v * cdf).astype(BF16)
                ls[slot, a : a + 32, c] = (cdf + v * pdf).astype(BF16)
            ob[:, c] = nn(twt[1], hs[slot, :, c])
        for r in partial:
            v = xf[i, r, :].astype(F32) + (ob[r, :] + across(tb2_w[r, :], full))
            ms[slot, r, :] = v.astype(BF16)
            unit, rstd = centre(v)
            vs[slot, r, :] = unit.astype(BF16)
            st[token_rows(i, r), :] = (unit * norm[1:2, :] + norm[3:4, :]).astype(BF16)
            cs[i, 1, r, :] = jnp.broadcast_to(rstd, (r.stop - r.start, 128))
        for c in saved(i):
            c.start()
        return carry

    lax.fori_loop(0, ni, token_step, 0)
    for i in (ni - 2, ni - 1):
        for c in saved(i):
            c.wait()
    for c in local_copies[2:]:
        c.wait()
    for c in pair_copies[3:]:
        c.wait_recv()

    def image_loads(i, slot):
        pairs = ((u0_hbm, us), (f_hbm, fs), (hid_hbm, hs), (slope_hbm, ls), (u1_hbm, vs))
        return [
            pltpu.make_async_copy(a.at[i], b.at[slot], in_sem.at[slot, n])
            for n, (a, b) in enumerate(pairs)
        ]

    def late_loads(i, slot):
        return [pltpu.make_async_copy(mix_hbm.at[i], ms.at[slot], in_sem.at[slot, 5])]

    for c in image_loads(0, 0):
        c.start()
    for c in late_loads(0, 0):
        c.start()

    def pair_copy(slot):
        return remote(pb, ra.at[slot], sa.at[0], rsa.at[slot], other)

    def first_copies(j):
        slot = lax.rem(j, 3)
        return (
            remote(
                gs.at[slot, 0, :, :, 1 - x], r1.at[j, 0], s1.at[slot, 0], rs1.at[j, 0], x_dev
            ),
            remote(gs.at[slot, 1, :, 1 - y], r1.at[j, 1], s1.at[slot, 1], rs1.at[j, 1], y_dev),
        )

    def second_copies(j):
        slot = lax.rem(j, 3)
        return (
            remote(b2.at[slot, 0, :, 1 - y], r2.at[j, 0], s2.at[slot, 0], rs2.at[j, 0], y_dev),
            remote(b2.at[slot, 1, :, 1 - x], r2.at[j, 1], s2.at[slot, 1], rs2.at[j, 1], x_dev),
        )

    def third_copies(j):
        slot = lax.rem(j, 2)
        out = []
        for n in range(1, nz):
            to = lax.rem(z + n, nz)
            out.append(
                remote(
                    b3.at[slot, to],
                    r3.at[j, n - 1],
                    s3.at[slot, n - 1],
                    rs3.at[j, n - 1],
                    ((to * ny + y) * nx + x, core),
                )
            )
        return out

    def finish_third(j):
        slot = lax.rem(j, 2)
        for c in third_copies(j):
            c.wait()
        at = pl.ds(pl.multiple_of(j * BLK, BLK), BLK)
        for m in range(2):
            v = b3[slot, z, m].astype(F32)
            for n in range(nz - 1):
                v = v + r3[j, n, m].astype(F32)
            gw_o[m, :, at] = v

    def finish_second(j):
        slot, into = lax.rem(j, 3), lax.rem(j, 2)
        for c in second_copies(j):
            c.wait()
        for m, mine in ((0, y), (1, x)):
            for k in range(nz):
                v = b2[slot, m, k, mine].astype(F32) + r2[j, m, k].astype(F32)
                b3[into, k, m] = v.astype(BF16)
        for c in third_copies(j):
            c.start()

    def finish_first(j):
        slot = lax.rem(j, 3)
        for c in first_copies(j):
            c.wait()
        for k in range(nz):
            for n in range(2):
                v = gs[slot, 0, k, n, x].astype(F32) + r1[j, 0, k, n].astype(F32)
                b2[slot, 0, k, n] = v.astype(BF16)
                v = gs[slot, 1, k, y, n].astype(F32) + r1[j, 1, k, n].astype(F32)
                b2[slot, 1, k, n] = v.astype(BF16)
        for c in second_copies(j):
            c.start()

    def hidden_block(side, j):
        at = pl.ds(pl.multiple_of(j * BLK, BLK), BLK)
        col = pl.ds(pl.multiple_of(side * half + j * BLK, BLK), BLK)
        w1 = w1s[side, :, at]
        w2 = w2s[side, at, :]
        b_row = bias[0:1, col]
        for i in range(ni):
            r0 = i * tp
            r = slice(r0, r0 + tp)
            pre = nn(st[r, :], w1)
            up_grad = nt(yt[r, :], w2)
            acc = jnp.zeros((8, BLK), F32)
            for a in range(0, tp, 16):
                v = pre[a : a + 16] + b_row
                cdf, pdf = gelu_parts(v)
                gh[r0 + a : r0 + a + 16, col] = (v * cdf).astype(BF16)
                p = up_grad[a : a + 16] * (cdf + v * pdf)
                ph[r0 + a : r0 + a + 16, col] = p.astype(BF16)
                acc += fold(p)
            row = jnp.sum(acc, 0, keepdims=True)
            row_h[0:1, col] += row
            row_h[1 + i : 2 + i, col] = row
        return tn(st[...], ph[:, col]), tn(yt[...], gh[:, col])

    def rounds(s):
        for lag, work in ((8, finish_third), (6, finish_second), (3, finish_first)):

            @pl.when((s >= lag) & (s < n_blk + lag))
            def _():
                work(s - lag)

    def split(v, k):
        per = full // nz
        return v[k * per : (k + 1) * per].reshape(ny, nx, rows_own, BLK)

    def block_step(j, carry):
        slot = lax.rem(j, 2)
        for m, v in enumerate(hidden_block(1, j)):
            for k in range(nz):
                pb[m, k] = split(v, k).astype(BF16)
        pair_copy(slot).start()
        grads = hidden_block(0, j)
        pair_copy(slot).wait()
        rounds(j)
        for m, v in enumerate(grads):
            for k in range(nz):
                gs[lax.rem(j, 3), m, k] = (split(v, k) + ra[slot, m, k].astype(F32)).astype(BF16)
        for c in first_copies(j):
            c.start()
        return carry

    lax.fori_loop(0, n_blk, block_step, 0)

    def out_copies(n, i):
        src, dst = ((bos, bo_hbm), (gis, gi_hbm))[n]
        slot = lax.rem(i, 2)
        to = dst.at[my_first + i]
        return (
            remote(src.at[slot, :, there], to, out_s.at[slot, n], out_r.at[i, n], other),
            pltpu.make_async_copy(src.at[slot, :, here], to, out_l.at[slot, n]),
        )

    def out_start(n, i):
        for c in out_copies(n, i):
            c.start()

    def out_sent(n, i):
        away, local = out_copies(n, i)
        away.wait_send()
        local.wait()

    def out_arrived(n, i):
        src, dst = ((bos, bo_hbm), (gis, gi_hbm))[n]
        remote(
            src.at[0, :, there],
            dst.at[(1 - core) * ni + i],
            out_s.at[0, n],
            out_r.at[i, n],
            other,
        ).wait_recv()

    def store_rows(ref, slot, r, v):
        stop = min(r.stop, pat)
        ref[slot, r.start : stop, :] = v[: stop - r.start].astype(BF16)

    def backward_step(i, carry):
        slot = lax.rem(i, 2)
        rounds(n_blk + i)
        rows = pl.ds(pl.multiple_of(i * tp, 16), tp)
        ob[...] = nt(ph[rows, :half], w1s[0]) + nt(ph[rows, half:], w1s[1])

        @pl.when(i + 1 < ni)
        def _():
            for c in image_loads(i + 1, 1 - slot):
                c.start()

        for c in image_loads(i, slot):
            c.wait()

        @pl.when(i >= 2)
        def _():
            out_sent(1, i - 2)

        zero8 = jnp.zeros((8, full), F32)
        dy, gain, shift = zero8, zero8, zero8
        for r in pieces:
            sg = ob[r, :]
            unit = vs[slot, r, :].astype(F32)
            gain += fold(sg * unit)
            shift += fold(sg)
            e = sg * norm[1:2, :]
            m = jnp.sum(e, 1, keepdims=True) * (1.0 / full)
            n = jnp.sum(e * unit, 1, keepdims=True) * (1.0 / full)
            y_rows = pl.ds(pl.multiple_of(i * tp + r.start, 16), ROWS)
            v = yt[y_rows, :].astype(F32)
            dy += fold(v)
            v = v + across(cs[i, 1, r, :], full) * (e - m - unit * n)
            mg[r, :] = v
            ol[r, :] = v.astype(BF16)
        dy = jnp.sum(dy, 0, keepdims=True)
        row_c[0:1, :] += dy
        row_c[pl.ds(1 + i, 1), :] = dy
        acc_norm[1] += gain
        acc_norm[3] += shift
        for c in lane_pieces(full):
            hg = nn(tw[1], ol[:, c])
            for a in range(0, ds, 32):
                r = slice(a, a + 32)
                tg[r, c] = (hg[r] * ls[slot, r, c].astype(F32)).astype(BF16)
            fg[:, c] = nn(twt[0], tg[:, c])
        acc_tok[0] += nt(tg[...], fs[slot])
        acc_tok[1] += nt(hs[slot], ol[...])
        row_p[...] += nt(jnp.ones((16, full), BF16), ol[...])
        gain, shift = zero8, zero8
        for r in pieces:
            g = fg[r, :]
            unit = us[slot, r, :].astype(F32)
            gain += fold(g * unit)
            shift += fold(g)
            e = g * norm[0:1, :]
            m = jnp.sum(e, 1, keepdims=True) * (1.0 / full)
            n = jnp.sum(e * unit, 1, keepdims=True) * (1.0 / full)
            v = mg[r, :] + across(cs[i, 0, r, :], full) * (e - m - unit * n)
            store_rows(gis, slot, r, v)
        acc_norm[0] += gain
        acc_norm[2] += shift
        out_start(1, i)
        return carry

    lax.fori_loop(0, ni, backward_step, 0)
    h_0 = jnp.where(core == 0, row_h[0:1, :half], row_h[0:1, half:])
    h_1 = jnp.where(core == 0, row_h[0:1, half:], row_h[0:1, :half])
    norms = jnp.concatenate([jnp.sum(acc_norm[n], 0, keepdims=True) for n in range(4)], 0)
    norms = jnp.concatenate([norms, jnp.zeros((4, full), F32)], 0)
    per_h = half // n_dp
    per_c = ch // n_dp
    tail = msgs.shape[1] - 2 * unit_d

    def cut(v, start, size):
        n = v.shape[1]
        a = min(start // 128 * 128, n - 256)
        v = v[:, a : a + 256]
        if v.shape[0] == 1:
            v = jnp.broadcast_to(v, (8, 256))
        if start > a:
            v = pltpu.roll(v, 256 - (start - a), 1)
        lane = lax.broadcasted_iota(jnp.int32, v.shape, 1)
        return jnp.where(lane < size, v, 0.0)

    for d in range(n_dp):
        top = jnp.concatenate(
            [
                acc_tok[0, unit_d * d : unit_d * (d + 1), :],
                acc_tok[1, unit_d * d : unit_d * (d + 1), :],
            ],
            axis=0,
        )
        msgs[d, : 2 * unit_d, :] = top.astype(BF16)
        extra = jnp.concatenate(
            [
                row_p[0:1, :],
                cut(h_0, per_h * d, per_h)[0:1],
                cut(h_1, per_h * d, per_h)[0:1],
                cut(row_c[0:1, :], per_c * d, per_c)[0:1],
                cut(row_c[0:1, :], ch + per_c * d, per_c)[0:1],
                jnp.zeros((3, kp), F32),
                cut(norms, rows_own * d, rows_own),
            ],
            axis=0,
        )
        msgs[d, 2 * unit_d :, :] = extra.astype(BF16)

    def token_send(n):
        to = lax.rem(dp + n, n_dp)
        return remote(msgs.at[to], msgr.at[dp], tok_s.at[n], tok_r.at[dp], (to, core))

    def token_arrival(n):
        source = lax.rem(dp + n_dp - n, n_dp)
        return remote(
            msgs.at[source], msgr.at[source], tok_s.at[n], tok_r.at[source], (source, core)
        )

    def send(n, c):
        token_send(n).start()
        return c

    lax.fori_loop(1, n_dp, send, 0)
    msgr[dp] = msgs[dp]

    def forward_step(i, carry):
        slot = lax.rem(i, 2)
        rounds(n_blk + ni + i)
        r = pl.ds(pl.multiple_of(i * tp, 16), tp)

        @pl.when(i + 1 < ni)
        def _():
            for c in late_loads(i + 1, 1 - slot):
                c.start()

        ob[...] = nn(gh[r, :half], w2s[0]) + nn(gh[r, half:], w2s[1])
        g = gh[r, :]
        p = ph[r, :]
        s = st[r, :]
        y_all = yt[r, :]
        both = nt(s, s) * nt(p, p) + nt(g, g) * nt(y_all, y_all)
        sq = jnp.sum(jnp.sum(both, 0, keepdims=True), 1, keepdims=True)
        rh = row_h[pl.ds(1 + i, 1), :]
        rc = row_c[pl.ds(1 + i, 1), :]
        sq = sq + jnp.sum(rh * rh, 1, keepdims=True) + jnp.sum(rc * rc, 1, keepdims=True)
        lane = lax.broadcasted_iota(jnp.int32, (1, 128), 1)
        sq_a[0:1, :] += jnp.where(lane == my_first + i, sq, 0.0)
        for c in late_loads(i, slot):
            c.wait()

        @pl.when(i >= 2)
        def _():
            out_sent(0, i - 2)

        chan_bias = packf[images : images + 1, :]
        pool = jnp.zeros((8, full), F32)
        kept_sum = jnp.zeros((8, 128), F32)
        for r in pieces:
            kept = cs[i, 2, r, :]
            kept_sum += fold(kept)
            bo = across(kept, full) * (ms[slot, r, :].astype(F32) + (ob[r, :] + chan_bias))
            pool += fold(bo)
            store_rows(bos, slot, r, bo)
        count = jnp.sum(kept_sum, 0, keepdims=True)
        pool_a[pl.ds(my_first + i, 1), :] = jnp.sum(pool, 0, keepdims=True) / across(count, full)
        out_start(0, i)
        return carry

    lax.fori_loop(0, ni, forward_step, 0)
    pool_copy = remote(pool_a.at[:, there], pool_r, fin_s.at[0], fin_r.at[0], other)
    pool_copy.start()
    sq_copy = remote(sq_a, sq_r, fin_s.at[1], fin_r.at[1], other)
    sq_copy.start()

    def arrive(n, c):
        token_arrival(n).wait_recv()
        return c

    lax.fori_loop(1, n_dp, arrive, 0)
    total = msgr[0].astype(F32)
    for d in range(1, n_dp):
        total = total + msgr[d].astype(F32)
    red_a[...] = total
    red_copy = remote(red_a, red_r, fin_s.at[2], fin_r.at[2], other)
    red_copy.start()

    def sent(n, c):
        token_send(n).wait_send()
        return c

    lax.fori_loop(1, n_dp, sent, 0)

    def sent_w(n, c):
        weights_copy(n).wait_send()
        return c

    lax.fori_loop(1, n_dp, sent_w, 0)
    for c in pair_copies:
        c.wait_send()
    for n in range(2):
        for i in (ni - 2, ni - 1):
            out_sent(n, i)
        for i in range(ni):
            out_arrived(n, i)
    pool_copy.wait()
    sq_copy.wait()
    pool_o[...] = pool_a[:, here] + pool_r[...]
    sq_o[...] = sq_a[...] + sq_r[...]
    red_copy.wait()
    red_o[...] = red_a[...] + red_r[...]


def mixer(n_dp, grid3, x, go, gp, w1, w2, b1, cb2, gain, shift, tw1, tb1, tw2, tb2, keep):
    images, pat, ch = x.shape
    ni = images // 2
    full = 2 * ch
    half = w1.shape[1]
    unit_d = tw1.shape[0]
    ds = unit_d * n_dp
    tp = up(pat, 16)
    kp = up(pat, 256)
    toks_pad = up(ni * tp, 256)
    n_pack = up(images + 1 + half // ch, 8)
    n_img = up(images, 8)
    nz, ny, nx = grid3
    rows_own = full // n_dp
    n_msg = 2 * unit_d + 16
    n_blk = half // BLK
    sds = jax.ShapeDtypeStruct
    vm = pltpu.VMEM
    dma = pltpu.SemaphoreType.DMA
    part = (nz, ny, nx, rows_own, BLK)
    outs = [
        (sds((images, pat, ch), BF16), ANY),
        (sds((images, pat, ch), BF16), ANY),
        (sds((ni, tp, full), BF16), ANY),
        (sds((ni, kp, full), BF16), ANY),
        (sds((ni, ds, full), BF16), ANY),
        (sds((ni, ds, full), BF16), ANY),
        (sds((ni, tp, full), BF16), ANY),
        (sds((ni, tp, full), BF16), ANY),
        (sds((n_img, ch), F32), VM),
        (sds((8, 128), F32), VM),
        (sds((n_msg, kp), F32), VM),
        (sds((2, rows_own, half), F32), VM),
    ]
    res = pl.pallas_call(
        functools.partial(mixer_kernel, (n_dp, ni, ch, pat, tp, unit_d, nz, ny, nx)),
        out_shape=[o[0] for o in outs],
        in_specs=[ANY, ANY, VM, ANY, ANY] + [VM] * 9,
        out_specs=[o[1] for o in outs],
        scratch_shapes=[
            vm((ni, pat, full), BF16),
            vm((ni, pat, full), BF16),
            vm((2 * unit_d, kp), BF16),
            vm((128, 128), F32),
            vm((n_pack, ch), F32),
            vm((n_pack, full), F32),
            vm((n_dp, 2 * unit_d, kp), BF16),
            vm((2, ds, kp), F32),
            vm((full, 128), BF16),
            vm((kp, kp), F32),
            vm((tp, 128), F32),
            vm((16, full), F32),
            vm((2, ds, kp), BF16),
            vm((2, tp, ds), BF16),
            vm((toks_pad, full), BF16),
            vm((toks_pad, full), BF16),
            vm((2, full, half), BF16),
            vm((2, half, full), BF16),
            vm((8, 2 * half), F32),
            vm((toks_pad, 2 * half), BF16),
            vm((toks_pad, 2 * half), BF16),
            vm((3, 2) + part, BF16),
            vm((2,) + part, BF16),
            vm((2, 2) + part, BF16),
            vm((n_blk, 2, nz, 2, rows_own, BLK), BF16),
            vm((3, 2, nz, 2, rows_own, BLK), BF16),
            vm((n_blk, 2, nz, rows_own, BLK), BF16),
            vm((2, nz, 2, rows_own, BLK), BF16),
            vm((n_blk, nz - 1, 2, rows_own, BLK), BF16),
            vm((2, tp, full), BF16),
            vm((2, kp, full), BF16),
            vm((2, ds, full), BF16),
            vm((2, ds, full), BF16),
            vm((2, tp, full), BF16),
            vm((2, tp, full), BF16),
            vm((ni, 3, tp, 128), F32),
            vm((2, pat, full), BF16),
            vm((2, pat, full), BF16),
            vm((tp, full), F32),
            vm((tp, full), F32),
            vm((kp, full), BF16),
            vm((ds, full), BF16),
            vm((tp, full), F32),
            vm((4, 8, full), F32),
            vm((2, ds, kp), F32),
            vm((8, 2 * half), F32),
            vm((8, full), F32),
            vm((16, kp), F32),
            vm((n_img, full), F32),
            vm((n_img, ch), F32),
            vm((8, 128), F32),
            vm((8, 128), F32),
            vm((n_dp, n_msg, kp), BF16),
            vm((n_dp, n_msg, kp), BF16),
            vm((n_msg, kp), F32),
            vm((n_msg, kp), F32),
            dma((n_dp,)),
            dma((n_dp,)),
            dma((5,)),
            dma((5,)),
            dma((4,)),
            dma((2, 6)),
            dma((2, 6)),
            dma((1,)),
            dma((2,)),
            dma((3, 2)),
            dma((n_blk, 2)),
            dma((3, 2)),
            dma((n_blk, 2)),
            dma((2, nz - 1)),
            dma((n_blk, nz - 1)),
            dma((2, 2)),
            dma((ni, 2)),
            dma((2, 2)),
            dma((n_dp,)),
            dma((n_dp,)),
            dma((3,)),
            dma((3,)),
        ],
        compiler_params=pltpu.CompilerParams(
            collective_id=0, has_side_effects=True, vmem_limit_bytes=VMEM_BYTES
        ),
        name="mixer",
    )(x, go, gp, w1, w2, b1, cb2, gain, shift, tw1, tb1, tw2, tb2, keep)
    return res[:2] + res[8:]


def finish_kernel(
    dims,
    bo_ref,
    gi_ref,
    pool_ref,
    sq_ref,
    red_ref,
    gw_ref,
    bo_o,
    pool_o,
    gi_o,
    gain_o,
    shift_o,
    tw1_o,
    tb1_o,
    tw2_o,
    tb2_o,
    w1_o,
    b1_o,
    w2_o,
    b2_o,
    sq_o,
):
    pat, unit_d, per_h, per_c = dims
    _, core = where_am_i()
    bo_o[...] = bo_ref[...].astype(F32)
    gi_o[...] = gi_ref[...].astype(F32)

    @pl.when(pl.program_id(0) == 0)
    def _():
        images = pool_o.shape[0]
        pool_o[...] = pool_ref[:images, :]
        sq_o[...] = sq_ref[0:1, :images]
        red = red_ref[...]
        n = 2 * unit_d
        tw1_o[...] = red[:unit_d, :pat]
        tw2_o[...] = red[unit_d:n, :pat]
        gain_o[...] = red[n + 8 : n + 10, :n]
        shift_o[...] = red[n + 10 : n + 12, :n]
        tb1_o[...] = jnp.transpose(red[: up(unit_d, 8), 128:])[pat - 128 : pat - 127, :unit_d]
        tb2_o[...] = red[n : n + 1, :pat]
        w1_o[...] = gw_ref[0]
        w2_o[...] = gw_ref[1]
        b1_o[...] = jnp.where(core == 0, red[n + 1 : n + 2, :per_h], red[n + 2 : n + 3, :per_h])
        b2_o[...] = jnp.where(core == 0, red[n + 3 : n + 4, :per_c], red[n + 4 : n + 5, :per_c])


def finish(bo, gi, pool, sq, red, gw, unit_d, per_h, per_c):
    images, pat, ch = bo.shape
    ds = unit_d
    sds = jax.ShapeDtypeStruct
    once = lambda s: pl.BlockSpec(s, lambda i: (0,) * len(s))
    steps = 4 if images % 4 == 0 else images
    per = pl.BlockSpec((images // steps, pat, ch), lambda i: (i, 0, 0))
    rows_own, half = gw.shape[1:]
    outs = [
        (images, pat, ch),
        (images, ch),
        (images, pat, ch),
        (2, rows_own),
        (2, rows_own),
        (ds, pat),
        (1, ds),
        (ds, pat),
        (1, pat),
        (rows_own, half),
        (1, per_h),
        (rows_own, half),
        (1, per_c),
        (1, images),
    ]
    res = pl.pallas_call(
        functools.partial(finish_kernel, (pat, unit_d, per_h, per_c)),
        grid=(steps,),
        out_shape=[sds(s, F32) for s in outs],
        in_specs=[per, per] + [once(a.shape) for a in (pool, sq, red, gw)],
        out_specs=[per if len(s) == 3 else once(s) for s in outs],
        compiler_params=pltpu.CompilerParams(vmem_limit_bytes=VMEM_BYTES),
        name="finish",
    )(bo, gi, pool, sq, red, gw)
    res = [r.reshape(-1) if r.shape[0] == 1 else r for r in res]
    for n in (0, 2):
        res[n] = jnp.swapaxes(res[n], 1, 2)
    for n in (5, 11):
        res[n] = res[n].T
    return tuple(res)


def fused_body(
    n_dp,
    grid3,
    mixer_input,
    keep_mask,
    ln_gain,
    ln_shift,
    token_w1,
    token_b1,
    token_w2,
    token_b2,
    chan_w1,
    chan_b1,
    chan_w2,
    chan_b2,
    grad_out,
    grad_pooled,
):
    images, ch, pat = mixer_input.shape
    unit_d = token_b1.shape[0]
    half = chan_b1.shape[0]
    bo, gi, pool, sq, red, gw = mixer(
        n_dp,
        grid3,
        jnp.swapaxes(mixer_input, 1, 2),
        jnp.swapaxes(grad_out, 1, 2),
        grad_pooled,
        chan_w1,
        chan_w2,
        chan_b1.reshape(1, -1),
        chan_b2.reshape(1, -1),
        ln_gain,
        ln_shift,
        token_w1.T,
        token_b1.reshape(1, -1),
        token_w2,
        token_b2.reshape(1, -1),
        keep_mask,
    )
    return finish(bo, gi, pool, sq, red, gw, unit_d, half // n_dp, ch // n_dp)


D = 768


epsilon = 1e-05


def gelu_exact(values_in):
    return jax.nn.gelu(values_in, approximate=False)


def gelu_slope(pre_sum, upstream):
    unused, backward = jax.vjp(gelu_exact, pre_sum)
    return backward(upstream)[0]


def channel_sums(first_term, second_term):
    return lax.psum((first_term, second_term), "tensor")


def normalize(values_in, gains, shifts):
    totals, square = channel_sums(jnp.sum(values_in, 1), jnp.sum(values_in * values_in, 1))
    average = totals / D
    spread = square / D - average * average
    scaling = lax.rsqrt(spread + epsilon)[:, None, :]
    unit_part = (values_in - average[:, None, :]) * scaling
    return (unit_part * gains[None, :, None] + shifts[None, :, None], unit_part, scaling)


def normalize_back(upstream, unit_part, scaling, gains):
    scaled = upstream * gains[None, :, None]
    totals, along_unit = channel_sums(jnp.sum(scaled, 1), jnp.sum(scaled * unit_part, 1))
    inner_part = scaled - totals[:, None, :] / D - unit_part * along_unit[:, None, :] / D
    return (scaling * inner_part, jnp.sum(upstream * unit_part, (0, 2)), jnp.sum(upstream, (0, 2)))


def body(
    mixer_input,
    keep_mask,
    ln_gain,
    ln_shift,
    token_w1,
    token_b1,
    token_w2,
    token_b2,
    chan_w1,
    chan_b1,
    chan_w2,
    chan_b2,
    grad_out,
    grad_pooled,
):
    images, channels, patches = mixer_input.shape
    full_width = channels * lax.axis_size("tensor")
    offset = lax.axis_index("tensor") * channels
    gains, shifts, weight_in, bias_in, weight_back = (
        lax.all_gather(ln_gain, "dp", axis=1, tiled=True),
        lax.all_gather(ln_shift, "dp", axis=1, tiled=True),
        lax.all_gather(token_w1, "dp", axis=1, tiled=True),
        lax.all_gather(token_b1, "dp", axis=0, tiled=True),
        lax.all_gather(token_w2, "dp", axis=0, tiled=True),
    )
    gain_own = lax.dynamic_slice_in_dim(gains, offset, channels, 1).astype(jnp.float32)
    shift_own = lax.dynamic_slice_in_dim(shifts, offset, channels, 1).astype(jnp.float32)
    kept = keep_mask.astype(jnp.float32)
    counts = jnp.sum(kept, 1)
    source = mixer_input.astype(jnp.float32)
    normed, unit_first, scale_first = normalize(source, gain_own[0], shift_own[0])
    first_low = normed.astype(jnp.bfloat16)
    token_pre = jnp.einsum(
        "bcp,ph->bch", first_low, weight_in, preferred_element_type=jnp.float32
    ) + bias_in.astype(jnp.float32)
    token_hid = gelu_exact(token_pre).astype(jnp.bfloat16)
    token_out = jnp.einsum(
        "bch,hp->bcp", token_hid, weight_back, preferred_element_type=jnp.float32
    ) + token_b2.astype(jnp.float32)
    mixture = source + token_out
    normed, unit_second, scale_second = normalize(mixture, gain_own[1], shift_own[1])
    second = normed.astype(jnp.bfloat16)
    section = lax.all_gather(second, "tensor", axis=1, tiled=True)
    pre_sum = jnp.einsum("bcp,ch->bhp", section, chan_w1, preferred_element_type=jnp.float32)
    gathered = section
    grams = jnp.einsum("bcp,bcq->bpq", section, section, preferred_element_type=jnp.float32)
    chan_pre = pre_sum
    gram_second = grams
    chan_pre = chan_pre + chan_b1.astype(jnp.float32)[None, :, None]
    chan_hid = gelu_exact(chan_pre).astype(jnp.bfloat16)
    partial_value = jnp.einsum("bhp,hc->bcp", chan_hid, chan_w2, preferred_element_type=jnp.float32)
    chan_out = (
        lax.psum_scatter(
            partial_value.astype(jnp.bfloat16), "tensor", scatter_dimension=1, tiled=True
        ).astype(jnp.float32)
        + chan_b2.astype(jnp.float32)[None, :, None]
    )
    masked = kept[:, None, :] * (mixture + chan_out)
    pooled = jnp.sum(masked, 2) / counts[:, None]
    grad_result = kept[:, None, :] * (
        grad_out.astype(jnp.float32) + grad_pooled[:, :, None] / counts[:, None, None]
    )
    grad_low = grad_result.astype(jnp.bfloat16)
    grad_chan_b2 = jnp.sum(grad_low, (0, 2), dtype=jnp.float32)
    section = lax.all_gather(grad_low, "tensor", axis=1, tiled=True)
    hid_sum = jnp.einsum("bcp,hc->bhp", section, chan_w2, preferred_element_type=jnp.float32)
    column_block = jnp.einsum("bhp,bcp->hc", chan_hid, section, preferred_element_type=jnp.float32)
    grams = jnp.einsum("bcp,bcq->bpq", section, section, preferred_element_type=jnp.float32)
    pre_grad = gelu_slope(chan_pre, hid_sum).astype(jnp.bfloat16)
    grad_chan_b1 = jnp.sum(pre_grad, (0, 2), dtype=jnp.float32)
    grad_chan_w1 = jnp.einsum("bcp,bhp->ch", gathered, pre_grad, preferred_element_type=jnp.float32)
    share_w1, share_b1, share_w2, share_b2 = (
        lax.psum_scatter(
            grad_chan_w1.astype(jnp.bfloat16), "dp", scatter_dimension=0, tiled=True
        ).astype(jnp.float32),
        lax.psum_scatter(
            grad_chan_b1.astype(jnp.bfloat16), "dp", scatter_dimension=0, tiled=True
        ).astype(jnp.float32),
        lax.psum_scatter(
            column_block.astype(jnp.bfloat16), "dp", scatter_dimension=1, tiled=True
        ).astype(jnp.float32),
        lax.psum_scatter(
            grad_chan_b2.astype(jnp.bfloat16), "dp", scatter_dimension=0, tiled=True
        ).astype(jnp.float32),
    )
    second_part = jnp.einsum("bhp,ch->bcp", pre_grad, chan_w1, preferred_element_type=jnp.float32)
    second_grad = lax.psum_scatter(
        second_part.astype(jnp.bfloat16), "tensor", scatter_dimension=1, tiled=True
    ).astype(jnp.float32)
    gram_pre = jnp.einsum("bhp,bhq->bpq", pre_grad, pre_grad, preferred_element_type=jnp.float32)
    gram_hid = jnp.einsum("bhp,bhq->bpq", chan_hid, chan_hid, preferred_element_type=jnp.float32)
    own_terms = jnp.sum(gram_second * gram_pre + gram_hid * grams, (1, 2))
    own_terms = own_terms + jnp.sum(jnp.square(jnp.sum(pre_grad, 2, dtype=jnp.float32)), 1)
    own_terms = own_terms + jnp.sum(jnp.square(jnp.sum(grad_low, 2, dtype=jnp.float32)), 1)
    example_sq = lax.psum(own_terms, "tensor")
    back_second, gain_second, shift_second = normalize_back(
        second_grad, unit_second, scale_second, gain_own[1]
    )
    mixture_grad = grad_result + back_second
    out_low = mixture_grad.astype(jnp.bfloat16)
    grad_token_b2 = jnp.sum(out_low, (0, 1), dtype=jnp.float32)
    token_hid_grad = jnp.einsum(
        "bcp,hp->bch", out_low, weight_back, preferred_element_type=jnp.float32
    )
    grad_token_w2 = jnp.einsum(
        "bch,bcp->hp", token_hid, out_low, preferred_element_type=jnp.float32
    )
    token_pre_grad = gelu_slope(token_pre, token_hid_grad).astype(jnp.bfloat16)
    grad_token_b1 = jnp.sum(token_pre_grad, (0, 1), dtype=jnp.float32)
    grad_token_w1 = jnp.einsum(
        "bcp,bch->ph", first_low, token_pre_grad, preferred_element_type=jnp.float32
    )
    first_grad = jnp.einsum(
        "bch,ph->bcp", token_pre_grad, weight_in, preferred_element_type=jnp.float32
    )
    back_first, gain_first, shift_first = normalize_back(
        first_grad, unit_first, scale_first, gain_own[0]
    )
    grad_input = mixture_grad + back_first
    gain_parts = lax.dynamic_update_slice_in_dim(
        jnp.zeros((2, full_width), jnp.float32), jnp.stack([gain_first, gain_second]), offset, 1
    )
    shift_parts = lax.dynamic_update_slice_in_dim(
        jnp.zeros((2, full_width), jnp.float32), jnp.stack([shift_first, shift_second]), offset, 1
    )
    total_gain, total_shift, total_w1, total_b1, total_w2 = (
        lax.psum(gain_parts.astype(jnp.bfloat16), "tensor").astype(jnp.float32),
        lax.psum(shift_parts.astype(jnp.bfloat16), "tensor").astype(jnp.float32),
        lax.psum(grad_token_w1.astype(jnp.bfloat16), "tensor").astype(jnp.float32),
        lax.psum(grad_token_b1.astype(jnp.bfloat16), "tensor").astype(jnp.float32),
        lax.psum(grad_token_w2.astype(jnp.bfloat16), "tensor").astype(jnp.float32),
    )
    share_gain, share_shift, share_tw1, share_tb1, share_tw2 = (
        lax.psum_scatter(
            total_gain.astype(jnp.bfloat16), "dp", scatter_dimension=1, tiled=True
        ).astype(jnp.float32),
        lax.psum_scatter(
            total_shift.astype(jnp.bfloat16), "dp", scatter_dimension=1, tiled=True
        ).astype(jnp.float32),
        lax.psum_scatter(
            total_w1.astype(jnp.bfloat16), "dp", scatter_dimension=1, tiled=True
        ).astype(jnp.float32),
        lax.psum_scatter(
            total_b1.astype(jnp.bfloat16), "dp", scatter_dimension=0, tiled=True
        ).astype(jnp.float32),
        lax.psum_scatter(
            total_w2.astype(jnp.bfloat16), "dp", scatter_dimension=0, tiled=True
        ).astype(jnp.float32),
    )
    share_tb2 = lax.psum(grad_token_b2, ("dp", "tensor"))
    return (
        masked,
        pooled,
        grad_input,
        share_gain,
        share_shift,
        share_tw1,
        share_tb1,
        share_tw2,
        share_tb2,
        share_w1,
        share_b1,
        share_w2,
        share_b2,
        example_sq,
    )


def solution(mesh):
    n_dp, n_tensor = mesh.shape["dp"], mesh.shape["tensor"]
    chosen = body
    if (n_dp, n_tensor) == (16, 2):
        chosen = functools.partial(fused_body, n_dp, (4, 2, 2))
    return jax.shard_map(
        chosen,
        mesh=mesh,
        in_specs=(
            P("dp", "tensor", None),
            P("dp", None),
            P(None, "dp"),
            P(None, "dp"),
            P(None, "dp"),
            P("dp"),
            P("dp", None),
            P(),
            P(None, "tensor"),
            P("tensor"),
            P("tensor", None),
            P("tensor"),
            P("dp", "tensor", None),
            P("dp", "tensor"),
        ),
        out_specs=(
            P("dp", "tensor", None),
            P("dp", "tensor"),
            P("dp", "tensor", None),
            P(None, "dp"),
            P(None, "dp"),
            P(None, "dp"),
            P("dp"),
            P("dp", None),
            P(),
            P("dp", "tensor"),
            P(("tensor", "dp")),
            P("tensor", "dp"),
            P(("tensor", "dp")),
            P("dp"),
        ),
        check_vma=False,
    )
```

```python
import functools
import math

import jax
import jax.numpy as jnp
from jax import lax
from jax.experimental import pallas as pl
from jax.experimental.pallas import tpu as pltpu
from jax.sharding import PartitionSpec as P

MESH = pl.DeviceIdType.MESH
EPS = 1e-05
F32 = jnp.float32
BF16 = jnp.bfloat16
VM = pl.BlockSpec(memory_space=pltpu.VMEM)
ANY = pl.BlockSpec(memory_space=pl.ANY)
BLK = 256
VMEM_BYTES = 63 * 2**20


def up(n, m):
    return -(-n // m) * m


def nn(a, b):
    return lax.dot_general(a, b, (((1,), (0,)), ((), ())), preferred_element_type=F32)


def nt(a, b):
    return lax.dot_general(a, b, (((1,), (1,)), ((), ())), preferred_element_type=F32)


def tn(a, b):
    return lax.dot_general(a, b, (((0,), (0,)), ((), ())), preferred_element_type=F32)


def eye(rows, cols):
    r = lax.broadcasted_iota(jnp.int32, (rows, cols), 0)
    c = lax.broadcasted_iota(jnp.int32, (rows, cols), 1)
    return (r == c).astype(F32).astype(BF16)


def gelu_parts(v):
    cdf = 0.5 + 0.5 * lax.erf(v * math.sqrt(0.5))
    return cdf, jnp.exp(-0.5 * (v * v)) * (1.0 / math.sqrt(2.0 * math.pi))


def fold(v):
    return jnp.sum(v.reshape(v.shape[0] // 8, 8, v.shape[1]), 0)


def where_am_i():
    return lax.axis_index("dp"), lax.axis_index("tensor")


def greet_all(dp_size, dp, core):
    barrier = pltpu.get_barrier_semaphore()

    def one(n, c):
        pl.semaphore_signal(
            barrier, inc=1, device_id=(lax.rem(dp + n, dp_size), core), device_id_type=MESH
        )
        return c

    lax.fori_loop(1, dp_size, one, 0)
    pl.semaphore_signal(barrier, inc=1, device_id=(dp, 1 - core), device_id_type=MESH)
    pl.semaphore_wait(barrier, dp_size)


def remote(src, dst, send, recv, device):
    return pltpu.make_async_remote_copy(
        src_ref=src,
        dst_ref=dst,
        send_sem=send,
        recv_sem=recv,
        device_id=device,
        device_id_type=MESH,
    )


ROWS = 16


def row_pieces(pat):
    return [slice(r, min(r + ROWS, pat)) for r in range(0, pat, ROWS)]


def lane_pieces(full):
    return [slice(c, c + 256) for c in range(0, full, 256)]


def across(v, full):
    return jnp.concatenate([v] * (full // 128), axis=1)


def centre(v):
    n = v.shape[1]
    d = v - jnp.sum(v, 1, keepdims=True) * (1.0 / n)
    r = lax.rsqrt(jnp.sum(d * d, 1, keepdims=True) * (1.0 / n) + EPS)
    return d * r, r


def mixer_kernel(
    dims,
    x_hbm,
    go_hbm,
    gp_ref,
    w1_hbm,
    w2_hbm,
    row_ref,
    gain_ref,
    shift_ref,
    tw1_ref,
    tb1_ref,
    tw2_ref,
    keep_ref,
    bo_hbm,
    gi_hbm,
    u0_hbm,
    f_hbm,
    hid_hbm,
    slope_hbm,
    mix_hbm,
    u1_hbm,
    pool_o,
    sq_o,
    red_o,
    gw_o,
    xf,
    gof,
    msg,
    square,
    pack,
    packf,
    tok,
    tmp_w,
    prm,
    keep_t,
    tb2_w,
    norm,
    tw,
    twt,
    st,
    yt,
    w1s,
    w2s,
    bias,
    gh,
    ph,
    gs,
    pb,
    ra,
    r1,
    b2,
    r2,
    b3,
    r3,
    us,
    fs,
    hs,
    ls,
    ms,
    vs,
    cs,
    bos,
    gis,
    sg,
    ob,
    ol,
    tg,
    fg,
    acc_norm,
    acc_tok,
    row_h,
    row_c,
    pool_a,
    pool_r,
    sq_a,
    sq_r,
    msgs,
    msgr,
    msgz,
    msgl,
    red_a,
    red_r,
    tg_s,
    tg_r,
    pair_send,
    pair_recv,
    loc_sem,
    spill,
    in_sem,
    sa,
    rsa,
    s1,
    rs1,
    s2,
    rs2,
    s3,
    rs3,
    out_s,
    out_r,
    out_l,
    tok_s,
    tok_r,
    fin_s,
    fin_r,
):
    n_dp, ni, ch, pat, tp, unit_d, nz, ny, nx = dims
    dp, core = where_am_i()
    x = lax.rem(dp, nx)
    y = lax.rem(dp // nx, ny)
    z = dp // (nx * ny)
    other = (dp, 1 - core)
    x_dev = ((z * ny + y) * nx + (1 - x), core)
    y_dev = ((z * ny + (1 - y)) * nx + x, core)
    full = 2 * ch
    rows_own = full // n_dp
    half = w1s.shape[1] // 2
    n_blk = half // BLK
    toks = ni * tp
    toks_pad = gh.shape[0]
    kp = fs.shape[1]
    my_first = core * ni
    ds = tw.shape[1]
    images = 2 * ni
    here = pl.ds(pl.multiple_of(core * ch, 128), ch)
    there = pl.ds(pl.multiple_of((1 - core) * ch, 128), ch)
    bias_rows = half // ch
    pieces = [slice(r, r + ROWS) for r in range(0, tp, ROWS)]

    ours = pl.ds(my_first, ni)
    theirs = pl.ds((1 - core) * ni, ni)
    pair_copies = [
        remote(a, b, pair_send.at[n], pair_recv.at[n], other)
        for n, (a, b) in enumerate(
            (
                (pack, packf.at[:, here]),
                (x_hbm.at[theirs], xf.at[:, :, here]),
                (go_hbm.at[theirs], gof.at[:, :, here]),
                (w2_hbm, w2s.at[pl.ds(half, half)]),
                (w1_hbm, w1s.at[:, pl.ds(half, half)]),
            )
        )
    ]
    local_copies = [
        pltpu.make_async_copy(a, b, loc_sem.at[n])
        for n, (a, b) in enumerate(
            (
                (x_hbm.at[ours], xf.at[:, :, here]),
                (go_hbm.at[ours], gof.at[:, :, here]),
                (w1_hbm, w1s.at[:, pl.ds(0, half)]),
                (w2_hbm, w2s.at[pl.ds(0, half)]),
            )
        )
    ]

    def weights_copy(n):
        to = lax.rem(dp + n, n_dp)
        return remote(msg, tok.at[dp], tg_s.at[n], tg_r.at[dp], (to, core))

    def weights_arrival(n):
        source = lax.rem(dp + n_dp - n, n_dp)
        return remote(msg, tok.at[source], tg_s.at[n], tg_r.at[source], (source, core))

    for c in local_copies:
        c.start()
    square[...] = jnp.zeros_like(square)
    at = pat - 128
    square[at : at + 1, :unit_d] = tb1_ref[...].astype(F32)
    square[at + 4 : at + 6, :rows_own] = gain_ref[...].astype(F32)
    square[at + 6 : at + 8, :rows_own] = shift_ref[...].astype(F32)
    columns = jnp.transpose(square[...])[:rows_own]
    tmp_w[0, :rows_own, :] = jnp.zeros((rows_own, kp), F32)
    tmp_w[0, :unit_d, :pat] = tw1_ref[...].astype(F32)
    tmp_w[0, unit_d:rows_own, :pat] = tw2_ref[...].astype(F32)
    msg[:, :128] = tmp_w[0, :rows_own, :128].astype(BF16)
    msg[:, 128:] = (tmp_w[0, :rows_own, 128:] + columns).astype(BF16)
    pack[...] = jnp.zeros_like(pack)
    pack[:images, :] = gp_ref[...]
    pack[images : images + 1, :] = row_ref[:, half : half + ch].astype(F32)
    for n in range(bias_rows):
        pack[images + 1 + n : images + 2 + n, :] = row_ref[:, n * ch : (n + 1) * ch].astype(F32)
    greet_all(n_dp, dp, core)

    def send(n, c):
        weights_copy(n).start()
        return c

    lax.fori_loop(1, n_dp, send, 0)
    for c in pair_copies:
        c.start()

    tok[dp] = msg[...]
    packf[:, here] = pack[...]
    keep_t[...] = jnp.zeros_like(keep_t)
    keep_t[:images, :pat] = keep_ref[...].astype(F32)
    keep_t[images : images + 1, :pat] = row_ref[:, half + ch : half + ch + pat].astype(F32)
    turned = jnp.transpose(keep_t[...])
    keep_t[...] = turned
    tb2_w[...] = jnp.broadcast_to(turned[:tp, images : images + 1], (tp, 128))
    zero_rows = jnp.zeros((toks_pad - toks, gh.shape[1]), BF16)
    gh[toks:, :] = zero_rows
    ph[toks:, :] = zero_rows
    st[toks:, :] = zero_rows[:, :full]
    yt[toks:, :] = zero_rows[:, :full]
    for ref in (row_h, row_c, acc_norm, acc_tok, pool_a, sq_a, ol):
        ref[...] = jnp.zeros_like(ref)
    partial = row_pieces(pat)
    last = slice(pat // ROWS * ROWS, tp)
    blank = jnp.zeros((last.stop - last.start, full), BF16)
    for n in range(2):
        us[n, last, :] = blank
        vs[n, last, :] = blank
        ms[n, last, :] = blank
        fs[n, last.start :, :] = jnp.zeros((kp - last.start, full), BF16)
        fs[n, pat : pat + 1, :] = jnp.ones((1, full), BF16)
        hs[n, ds:, :] = jnp.ones((16, full), BF16)
    for c in local_copies[:2]:
        c.wait()
    for c in pair_copies[:3]:
        c.wait_recv()

    def token_rows(i, r):
        return pl.ds(pl.multiple_of(i * tp + r.start, 16), r.stop - r.start)

    def early_step(i, carry):
        number = my_first + i
        count = jnp.sum(keep_ref[pl.ds(number, 1), :].astype(F32), 1, keepdims=True)
        g = packf[pl.ds(number, 1), :] / count
        rows = token_rows(i, last)
        st[rows, :] = blank
        yt[rows, :] = blank
        cs[i, :, last, :] = jnp.zeros((3, tp - last.start, 128), F32)
        for r in partial:
            size = r.stop - r.start
            rows = token_rows(i, r)
            unit, rstd = centre(xf[i, r, :].astype(F32))
            st[rows, :] = unit.astype(BF16)
            cs[i, 0, r, :] = jnp.broadcast_to(rstd, (size, 128))
            lane = lax.broadcasted_iota(jnp.int32, (size, 128), 1)
            k = jnp.sum(jnp.where(lane == number, keep_t[r, :128], 0.0), 1, keepdims=True)
            yt[rows, :] = (k * (gof[i, r, :].astype(F32) + g)).astype(BF16)
            cs[i, 2, r, :] = jnp.broadcast_to(k, (size, 128))
        return carry

    lax.fori_loop(0, ni, early_step, 0)
    local_copies[3].wait()
    for a in range(0, half, BLK):
        ph[:toks, a : a + BLK] = nt(yt[:toks, :], w2s[a : a + BLK, :]).astype(BF16)
    for n in range(bias_rows):
        row = packf[images + 1 + n : images + 2 + n, :]
        swapped = jnp.concatenate([row[:, ch:], row[:, :ch]], axis=1)
        row = jnp.where(core == 0, row, swapped)
        bias[0:1, n * ch : (n + 1) * ch] = row[:, :ch]
        bias[0:1, half + n * ch : half + (n + 1) * ch] = row[:, ch:]

    def arrive_w(n, c):
        weights_arrival(n).wait_recv()
        return c

    lax.fori_loop(1, n_dp, arrive_w, 0)
    lane = lax.broadcasted_iota(jnp.int32, (unit_d, kp), 1)
    for d in range(n_dp):
        block = tok[d].astype(F32)
        tmp_w[0, unit_d * d : unit_d * (d + 1), :] = jnp.where(lane <= pat, block[:unit_d], 0.0)
        tmp_w[1, unit_d * d : unit_d * (d + 1), :] = jnp.where(lane < pat, block[unit_d:], 0.0)
        prm[rows_own * d : rows_own * (d + 1), :] = tok[d, :, 128:]
    r = lax.broadcasted_iota(jnp.int32, (16, 128), 0)
    c = lax.broadcasted_iota(jnp.int32, (16, 128), 1)
    norm[...] = nt(((c - (at + 4) == r) & (r < 4)).astype(F32).astype(BF16), prm[...])
    ident = eye(kp, kp)
    for n in range(2):
        w = tmp_w[n].astype(BF16)
        tw[n] = w
        t = nt(ident, w)
        r = lax.broadcasted_iota(jnp.int32, t.shape, 0)
        twt[n] = jnp.where(r < pat, t, 0.0)[:tp].astype(BF16)

    def saved(i):
        slot = lax.rem(i, 2)
        pairs = (
            (us, u0_hbm),
            (fs, f_hbm),
            (hs, hid_hbm),
            (ls, slope_hbm),
            (vs, u1_hbm),
            (ms, mix_hbm),
        )
        return [
            pltpu.make_async_copy(a.at[slot, pl.ds(0, b.shape[1])], b.at[i], spill.at[slot, n])
            for n, (a, b) in enumerate(pairs)
        ]

    def token_step(i, carry):
        slot = lax.rem(i, 2)

        @pl.when(i >= 2)
        def _():
            for c in saved(i - 2):
                c.wait()

        for r in partial:
            unit = st[token_rows(i, r), :]
            us[slot, r, :] = unit
            f = unit.astype(F32) * norm[0:1, :] + norm[2:3, :]
            fs[slot, r, :] = f.astype(BF16)
        for c in lane_pieces(full):
            pre = nn(tw[0], fs[slot, :, c])
            for a in range(0, ds, 32):
                v = pre[a : a + 32]
                cdf, pdf = gelu_parts(v)
                hs[slot, a : a + 32, c] = (v * cdf).astype(BF16)
                ls[slot, a : a + 32, c] = (cdf + v * pdf).astype(BF16)
            ob[:, c] = nn(twt[1], hs[slot, :ds, c])
        for r in partial:
            v = xf[i, r, :].astype(F32) + (ob[r, :] + across(tb2_w[r, :], full))
            ms[slot, r, :] = v.astype(BF16)
            unit, rstd = centre(v)
            vs[slot, r, :] = unit.astype(BF16)
            st[token_rows(i, r), :] = (unit * norm[1:2, :] + norm[3:4, :]).astype(BF16)
            cs[i, 1, r, :] = jnp.broadcast_to(rstd, (r.stop - r.start, 128))
        for c in saved(i):
            c.start()
        return carry

    lax.fori_loop(0, ni, token_step, 0)
    for i in (ni - 2, ni - 1):
        for c in saved(i):
            c.wait()
    local_copies[2].wait()
    for c in pair_copies[3:]:
        c.wait_recv()

    def image_loads(i, slot):
        pairs = ((u0_hbm, us), (f_hbm, fs), (hid_hbm, hs), (slope_hbm, ls), (u1_hbm, vs))
        return [
            pltpu.make_async_copy(a.at[i], b.at[slot, pl.ds(0, a.shape[1])], in_sem.at[slot, n])
            for n, (a, b) in enumerate(pairs)
        ]

    def late_loads(i, slot):
        return [pltpu.make_async_copy(mix_hbm.at[i], ms.at[slot], in_sem.at[slot, 5])]

    for c in image_loads(0, 0):
        c.start()
    for c in late_loads(0, 0):
        c.start()

    def pair_copy(slot):
        return remote(pb, ra.at[slot], sa.at[0], rsa.at[slot], other)

    def first_copies(j):
        slot = lax.rem(j, 2)
        return (
            remote(
                gs.at[slot, 0, :, :, 1 - x], r1.at[j, 0], s1.at[slot, 0], rs1.at[j, 0], x_dev
            ),
            remote(gs.at[slot, 1, :, 1 - y], r1.at[j, 1], s1.at[slot, 1], rs1.at[j, 1], y_dev),
        )

    def second_copies(j):
        slot = lax.rem(j, 2)
        return (
            remote(b2.at[slot, 0, :, 1 - y], r2.at[j, 0], s2.at[slot, 0], rs2.at[j, 0], y_dev),
            remote(b2.at[slot, 1, :, 1 - x], r2.at[j, 1], s2.at[slot, 1], rs2.at[j, 1], x_dev),
        )

    def third_copies(j):
        slot = lax.rem(j, 2)
        out = []
        for n in range(1, nz):
            to = lax.rem(z + n, nz)
            out.append(
                remote(
                    b3.at[slot, to],
                    r3.at[j, n - 1],
                    s3.at[slot, n - 1],
                    rs3.at[j, n - 1],
                    ((to * ny + y) * nx + x, core),
                )
            )
        return out

    def finish_third(j):
        slot = lax.rem(j, 2)
        for c in third_copies(j):
            c.wait()
        at = pl.ds(pl.multiple_of(j * BLK, BLK), BLK)
        for m in range(2):
            v = b3[slot, z, m].astype(F32)
            for n in range(nz - 1):
                v = v + r3[j, n, m].astype(F32)
            gw_o[m, :, at] = v

    def finish_second(j):
        slot, into = lax.rem(j, 2), lax.rem(j, 2)
        for c in second_copies(j):
            c.wait()
        for m, mine in ((0, y), (1, x)):
            for k in range(nz):
                v = b2[slot, m, k, mine].astype(F32) + r2[j, m, k].astype(F32)
                b3[into, k, m] = v.astype(BF16)
        for c in third_copies(j):
            c.start()

    def finish_first(j):
        slot, into = lax.rem(j, 2), lax.rem(j, 2)
        for c in first_copies(j):
            c.wait()
        for k in range(nz):
            for n in range(2):
                v = gs[slot, 0, k, n, x].astype(F32) + r1[j, 0, k, n].astype(F32)
                b2[into, 0, k, n] = v.astype(BF16)
                v = gs[slot, 1, k, y, n].astype(F32) + r1[j, 1, k, n].astype(F32)
                b2[into, 1, k, n] = v.astype(BF16)
        for c in second_copies(j):
            c.start()

    def hidden_block(side, j):
        col = pl.ds(pl.multiple_of(side * half + j * BLK, BLK), BLK)
        w1 = w1s[:, col]
        w2 = w2s[col, :]
        b_row = bias[0:1, col]
        for i0 in range(0, ni, 2):
            both = slice(i0 * tp, (i0 + 2) * tp)
            pre = nn(st[both, :], w1)
            if side == 1:
                up_grad = nt(yt[both, :], w2)
            for i in (i0, i0 + 1):
                acc = jnp.zeros((8, BLK), F32)
                for a in range(0, tp, 16):
                    r = slice(i * tp + a, i * tp + a + 16)
                    q = slice(r.start - both.start, r.stop - both.start)
                    v = pre[q] + b_row
                    cdf, pdf = gelu_parts(v)
                    gh[r, col] = (v * cdf).astype(BF16)
                    p = up_grad[q] if side == 1 else ph[r, col].astype(F32)
                    p = p * (cdf + v * pdf)
                    ph[r, col] = p.astype(BF16)
                    acc += fold(p)
                row = jnp.sum(acc, 0, keepdims=True)
                row_h[0:1, col] += row
                row_h[1 + i : 2 + i, col] = row
        return tn(st[...], ph[:, col]), tn(yt[...], gh[:, col])

    def due(*work):
        for step, j, exists in work:

            @pl.when(exists)
            def _():
                step(j)

    def split(v, k):
        per = full // nz
        return v[k * per : (k + 1) * per].reshape(ny, nx, rows_own, BLK)

    def block_step(j, carry):
        slot = lax.rem(j, 2)
        for m, v in enumerate(hidden_block(1, j)):
            for k in range(nz):
                pb[m, k] = split(v, k).astype(BF16)
        pair_copy(slot).start()
        due(
            (finish_third, j - 5, j >= 5),
            (finish_first, j - 2, j >= 2),
        )
        grads = hidden_block(0, j)
        pair_copy(slot).wait()
        for m, v in enumerate(grads):
            for k in range(nz):
                gs[slot, m, k] = (split(v, k) + ra[slot, m, k].astype(F32)).astype(BF16)
        for c in first_copies(j):
            c.start()
        due((finish_second, j - 3, j >= 3))
        return carry

    lax.fori_loop(0, n_blk, block_step, 0)

    def out_copies(n, i):
        src, dst = ((bos, bo_hbm), (gis, gi_hbm))[n]
        slot = lax.rem(i, 2)
        to = dst.at[my_first + i]
        return (
            remote(src.at[slot, :, there], to, out_s.at[slot, n], out_r.at[i, n], other),
            pltpu.make_async_copy(src.at[slot, :, here], to, out_l.at[slot, n]),
        )

    def out_start(n, i):
        for c in out_copies(n, i):
            c.start()

    def out_sent(n, i):
        away, local = out_copies(n, i)
        away.wait_send()
        local.wait()

    def out_arrived(n, i):
        src, dst = ((bos, bo_hbm), (gis, gi_hbm))[n]
        remote(
            src.at[0, :, there],
            dst.at[(1 - core) * ni + i],
            out_s.at[0, n],
            out_r.at[i, n],
            other,
        ).wait_recv()

    def store_rows(ref, slot, r, v):
        stop = min(r.stop, pat)
        ref[slot, r.start : stop, :] = v[: stop - r.start].astype(BF16)

    def backward_step(i, carry):
        slot = lax.rem(i, 2)
        due(
            (finish_third, n_blk - 3, i == 4),
            (finish_second, n_blk - 2, i == 4),
            (finish_first, n_blk - 1, i == 2),
        )

        @pl.when(i + 1 < ni)
        def _():
            for c in image_loads(i + 1, 1 - slot):
                c.start()

        for c in image_loads(i, slot):
            c.wait()

        @pl.when(i >= 2)
        def _():
            out_sent(1, i - 2)

        zero8 = jnp.zeros((8, full), F32)
        dy, gain, shift = zero8, zero8, zero8
        for r in pieces:
            e_rows = token_rows(i, r)
            grad = sg[e_rows, :].astype(F32)
            unit = vs[slot, r, :].astype(F32)
            gain += fold(grad * unit)
            shift += fold(grad)
            e = grad * norm[1:2, :]
            m = jnp.sum(e, 1, keepdims=True) * (1.0 / full)
            n = jnp.sum(e * unit, 1, keepdims=True) * (1.0 / full)
            v = yt[e_rows, :].astype(F32)
            dy += fold(v)
            v = v + across(cs[i, 1, r, :], full) * (e - m - unit * n)
            ob[r, :] = v
            ol[r, :] = v.astype(BF16)
        dy = jnp.sum(dy, 0, keepdims=True)
        row_c[0:1, :] += dy
        row_c[pl.ds(1 + i, 1), :] = dy
        acc_norm[1] += gain
        acc_norm[3] += shift
        for c in lane_pieces(full):
            hg = nn(tw[1], ol[:, c])
            for a in range(0, ds, 32):
                r = slice(a, a + 32)
                tg[r, c] = (hg[r] * ls[slot, r, c].astype(F32)).astype(BF16)
            fg[:, c] = nn(twt[0], tg[:, c])
        acc_tok[0, :ds] += nt(tg[...], fs[slot])
        acc_tok[1] += nt(hs[slot], ol[...])
        gain, shift = zero8, zero8
        for r in pieces:
            g = fg[r, :]
            unit = us[slot, r, :].astype(F32)
            gain += fold(g * unit)
            shift += fold(g)
            e = g * norm[0:1, :]
            m = jnp.sum(e, 1, keepdims=True) * (1.0 / full)
            n = jnp.sum(e * unit, 1, keepdims=True) * (1.0 / full)
            v = ob[r, :] + across(cs[i, 0, r, :], full) * (e - m - unit * n)
            store_rows(gis, slot, r, v)
        acc_norm[0] += gain
        acc_norm[2] += shift
        out_start(1, i)
        return carry

    part = toks // 3
    for n in range(3):
        if n == 0:
            finish_third(n_blk - 5)
        if n == 1:
            finish_third(n_blk - 4)
            finish_first(n_blk - 2)
        if n == 2:
            finish_second(n_blk - 3)
        a = n * part
        sg[a : a + part, :] = nt(ph[a : a + part, :], w1s[...]).astype(BF16)
    lax.fori_loop(0, ni, backward_step, 0)
    h_0 = jnp.where(core == 0, row_h[0:1, :half], row_h[0:1, half:])
    h_1 = jnp.where(core == 0, row_h[0:1, half:], row_h[0:1, :half])
    norms = jnp.concatenate([jnp.sum(acc_norm[n], 0, keepdims=True) for n in range(4)], 0)
    norms = jnp.concatenate([norms, jnp.zeros((4, full), F32)], 0)
    per_h = half // n_dp
    per_c = ch // n_dp
    tail = msgs.shape[3] - 2 * unit_d

    def cut(v, start, size):
        n = v.shape[1]
        a = min(start // 128 * 128, n - 256)
        v = v[:, a : a + 256]
        if v.shape[0] == 1:
            v = jnp.broadcast_to(v, (8, 256))
        if start > a:
            v = pltpu.roll(v, 256 - (start - a), 1)
        lane = lax.broadcasted_iota(jnp.int32, v.shape, 1)
        return jnp.where(lane < size, v, 0.0)

    for d in range(n_dp):
        place = (d // (ny * nx), d // nx % ny, d % nx)
        top = jnp.concatenate(
            [
                acc_tok[0, unit_d * d : unit_d * (d + 1), :],
                acc_tok[1, unit_d * d : unit_d * (d + 1), :],
            ],
            axis=0,
        )
        msgs[place + (slice(0, 2 * unit_d),)] = top.astype(BF16)
        extra = jnp.concatenate(
            [
                acc_tok[1, ds : ds + 1, :],
                cut(h_0, per_h * d, per_h)[0:1],
                cut(h_1, per_h * d, per_h)[0:1],
                cut(row_c[0:1, :], per_c * d, per_c)[0:1],
                cut(row_c[0:1, :], ch + per_c * d, per_c)[0:1],
                jnp.zeros((3, kp), F32),
                cut(norms, rows_own * d, rows_own),
            ],
            axis=0,
        )
        msgs[place + (slice(2 * unit_d, None),)] = extra.astype(BF16)

    plane_copies = []
    for n, (ay, ax) in enumerate(((0, 1), (1, 0), (1, 1))):
        to_y = 1 - y if ay else y
        to_x = 1 - x if ax else x
        plane_copies.append(
            remote(
                msgs.at[:, to_y, to_x],
                msgr.at[n],
                tok_s.at[n],
                tok_r.at[n],
                ((z * ny + to_y) * nx + to_x, core),
            )
        )
    line_copies = []
    for n in range(1, nz):
        to_z = lax.rem(z + n, nz)
        line_copies.append(
            remote(
                msgz.at[to_z],
                msgl.at[n - 1],
                tok_s.at[n + 2],
                tok_r.at[n + 2],
                ((to_z * ny + y) * nx + x, core),
            )
        )
    red_copy = remote(red_a, red_r, fin_s.at[2], fin_r.at[2], other)

    def plane_sum():
        for c in plane_copies:
            c.wait()
        for n in range(nz):
            v = msgs[n, y, x].astype(F32)
            for m in range(3):
                v = v + msgr[m, n].astype(F32)
            msgz[n] = v.astype(BF16)
        for c in line_copies:
            c.start()

    def line_sum():
        for c in line_copies:
            c.wait()
        v = msgz[z].astype(F32)
        for n in range(nz - 1):
            v = v + msgl[n].astype(F32)
        red_a[...] = v
        red_copy.start()

    for c in plane_copies:
        c.start()

    def gram_step(i, carry):
        due(
            (finish_third, n_blk - 2, i == 0),
            (finish_third, n_blk - 1, i == 3),
            (lambda j: line_sum(), 0, i == 4),
        )
        r = token_rows(i, slice(0, tp))
        g, p, s, dy = gh[r, :], ph[r, :], st[r, :], yt[r, :]
        both = nt(s, s) * nt(p, p) + nt(g, g) * nt(dy, dy)
        sq = jnp.sum(jnp.sum(both, 0, keepdims=True), 1, keepdims=True)
        rh = row_h[pl.ds(1 + i, 1), :]
        rc = row_c[pl.ds(1 + i, 1), :]
        sq = sq + jnp.sum(rh * rh, 1, keepdims=True) + jnp.sum(rc * rc, 1, keepdims=True)
        lane = lax.broadcasted_iota(jnp.int32, (1, 128), 1)
        sq_a[0:1, :] += jnp.where(lane == my_first + i, sq, 0.0)
        return carry

    def forward_step(i, carry):
        slot = lax.rem(i, 2)

        @pl.when(i + 1 < ni)
        def _():
            for c in late_loads(i + 1, 1 - slot):
                c.start()

        for c in late_loads(i, slot):
            c.wait()

        @pl.when(i >= 2)
        def _():
            out_sent(0, i - 2)

        chan_bias = packf[images : images + 1, :]
        pool = jnp.zeros((8, full), F32)
        kept_sum = jnp.zeros((8, 128), F32)
        for r in pieces:
            kept = cs[i, 2, r, :]
            kept_sum += fold(kept)
            out = sg[token_rows(i, r), :].astype(F32)
            bo = across(kept, full) * (ms[slot, r, :].astype(F32) + (out + chan_bias))
            pool += fold(bo)
            store_rows(bos, slot, r, bo)
        count = jnp.sum(kept_sum, 0, keepdims=True)
        pool_a[pl.ds(my_first + i, 1), :] = jnp.sum(pool, 0, keepdims=True) / across(count, full)
        out_start(0, i)
        return carry

    finish_second(n_blk - 1)
    for a in range(0, toks, part):
        sg[a : a + part, :] = nn(gh[a : a + part, :], w2s[...]).astype(BF16)
    lax.fori_loop(0, ni, forward_step, 0)
    pool_copy = remote(pool_a.at[:, there], pool_r, fin_s.at[0], fin_r.at[0], other)
    pool_copy.start()
    plane_sum()
    lax.fori_loop(0, ni, gram_step, 0)
    sq_copy = remote(sq_a, sq_r, fin_s.at[1], fin_r.at[1], other)
    sq_copy.start()

    def sent_w(n, c):
        weights_copy(n).wait_send()
        return c

    lax.fori_loop(1, n_dp, sent_w, 0)
    for c in pair_copies:
        c.wait_send()
    for n in range(2):
        for i in (ni - 2, ni - 1):
            out_sent(n, i)
        for i in range(ni):
            out_arrived(n, i)
    pool_copy.wait()
    sq_copy.wait()
    pool_o[...] = pool_a[:, here] + pool_r[...]
    sq_o[...] = sq_a[...] + sq_r[...]
    red_copy.wait()
    red_o[...] = red_a[...] + red_r[...]


def mixer(n_dp, grid3, x, go, gp, w1, w2, row, gain, shift, tw1, tb1, tw2, keep):
    images, pat, ch = x.shape
    ni = images // 2
    full = 2 * ch
    half = w1.shape[1]
    unit_d = tw1.shape[0]
    ds = unit_d * n_dp
    tp = up(pat, 16)
    kp = up(pat, 256)
    toks_pad = up(ni * tp, 256)
    n_pack = up(images + 1 + half // ch, 8)
    n_img = up(images, 8)
    nz, ny, nx = grid3
    rows_own = full // n_dp
    n_msg = 2 * unit_d + 16
    n_blk = half // BLK
    sds = jax.ShapeDtypeStruct
    vm = pltpu.VMEM
    dma = pltpu.SemaphoreType.DMA
    part = (nz, ny, nx, rows_own, BLK)
    outs = [
        (sds((images, pat, ch), BF16), ANY),
        (sds((images, pat, ch), BF16), ANY),
        (sds((ni, tp, full), BF16), ANY),
        (sds((ni, kp, full), BF16), ANY),
        (sds((ni, ds, full), BF16), ANY),
        (sds((ni, ds, full), BF16), ANY),
        (sds((ni, tp, full), BF16), ANY),
        (sds((ni, tp, full), BF16), ANY),
        (sds((n_img, ch), F32), VM),
        (sds((8, 128), F32), VM),
        (sds((n_msg, kp), F32), VM),
        (sds((2, rows_own, half), F32), VM),
    ]
    res = pl.pallas_call(
        functools.partial(mixer_kernel, (n_dp, ni, ch, pat, tp, unit_d, nz, ny, nx)),
        out_shape=[o[0] for o in outs],
        in_specs=[ANY, ANY, VM, ANY, ANY] + [VM] * 7,
        out_specs=[o[1] for o in outs],
        scratch_shapes=[
            vm((ni, pat, full), BF16),
            vm((ni, pat, full), BF16),
            vm((2 * unit_d, kp), BF16),
            vm((128, 128), F32),
            vm((n_pack, ch), F32),
            vm((n_pack, full), F32),
            vm((n_dp, 2 * unit_d, kp), BF16),
            vm((2, ds, kp), F32),
            vm((full, 128), BF16),
            vm((kp, kp), F32),
            vm((tp, 128), F32),
            vm((16, full), F32),
            vm((2, ds, kp), BF16),
            vm((2, tp, ds), BF16),
            vm((toks_pad, full), BF16),
            vm((toks_pad, full), BF16),
            vm((full, 2 * half), BF16),
            vm((2 * half, full), BF16),
            vm((8, 2 * half), F32),
            vm((toks_pad, 2 * half), BF16),
            vm((toks_pad, 2 * half), BF16),
            vm((2, 2) + part, BF16),
            vm((2,) + part, BF16),
            vm((2, 2) + part, BF16),
            vm((n_blk, 2, nz, 2, rows_own, BLK), BF16),
            vm((2, 2, nz, 2, rows_own, BLK), BF16),
            vm((n_blk, 2, nz, rows_own, BLK), BF16),
            vm((2, nz, 2, rows_own, BLK), BF16),
            vm((n_blk, nz - 1, 2, rows_own, BLK), BF16),
            vm((2, tp, full), BF16),
            vm((2, kp, full), BF16),
            vm((2, ds + 16, full), BF16),
            vm((2, ds, full), BF16),
            vm((2, tp, full), BF16),
            vm((2, tp, full), BF16),
            vm((ni, 3, tp, 128), F32),
            vm((2, pat, full), BF16),
            vm((2, pat, full), BF16),
            vm((ni * tp, full), BF16),
            vm((tp, full), F32),
            vm((kp, full), BF16),
            vm((ds, full), BF16),
            vm((tp, full), F32),
            vm((4, 8, full), F32),
            vm((2, ds + 16, kp), F32),
            vm((8, 2 * half), F32),
            vm((8, full), F32),
            vm((n_img, full), F32),
            vm((n_img, ch), F32),
            vm((8, 128), F32),
            vm((8, 128), F32),
            vm((nz, ny, nx, n_msg, kp), BF16),
            vm((3, nz, n_msg, kp), BF16),
            vm((nz, n_msg, kp), BF16),
            vm((nz - 1, n_msg, kp), BF16),
            vm((n_msg, kp), F32),
            vm((n_msg, kp), F32),
            dma((n_dp,)),
            dma((n_dp,)),
            dma((5,)),
            dma((5,)),
            dma((4,)),
            dma((2, 6)),
            dma((2, 6)),
            dma((1,)),
            dma((2,)),
            dma((2, 2)),
            dma((n_blk, 2)),
            dma((2, 2)),
            dma((n_blk, 2)),
            dma((2, nz - 1)),
            dma((n_blk, nz - 1)),
            dma((2, 2)),
            dma((ni, 2)),
            dma((2, 2)),
            dma((nz + 2,)),
            dma((nz + 2,)),
            dma((3,)),
            dma((3,)),
        ],
        compiler_params=pltpu.CompilerParams(
            collective_id=0, has_side_effects=True, vmem_limit_bytes=VMEM_BYTES
        ),
        name="mixer",
    )(x, go, gp, w1, w2, row, gain, shift, tw1, tb1, tw2, keep)
    return res[:2] + res[8:]


def finish_kernel(
    dims,
    bo_hbm,
    gi_hbm,
    pool_ref,
    sq_ref,
    red_ref,
    gw_ref,
    bo_out,
    pool_o,
    gi_out,
    gain_o,
    shift_o,
    tw1_o,
    tb1_o,
    tw2_o,
    tb2_o,
    w1_o,
    b1_o,
    w2_o,
    b2_o,
    sq_o,
    narrow,
    broad,
    in_sem,
    out_sem,
):
    pat, unit_d, per_h, per_c = dims
    _, core = where_am_i()
    parts = narrow.shape[1]
    jobs = []
    for n, (src, dst) in enumerate(((bo_hbm, bo_out), (gi_hbm, gi_out))):
        for m in range(parts):
            size = narrow.shape[2]
            rows = pl.ds(m * size, size)
            jobs.append(
                (
                    (n, m),
                    pltpu.make_async_copy(src.at[rows], narrow.at[n, m], in_sem.at[n, m]),
                    pltpu.make_async_copy(broad.at[n, m], dst.at[rows], out_sem.at[n, m]),
                )
            )
    for _, load, _ in jobs:
        load.start()
    for at, load, store in jobs:
        load.wait()
        broad[at] = narrow[at].astype(F32)
        store.start()
    images = pool_o.shape[0]
    pool_o[...] = pool_ref[:images, :]
    sq_o[...] = sq_ref[0:1, :images]
    red = red_ref[...]
    n = 2 * unit_d
    tw1_o[...] = red[:unit_d, :pat]
    tw2_o[...] = red[unit_d:n, :pat]
    gain_o[...] = red[n + 8 : n + 10, :n]
    shift_o[...] = red[n + 10 : n + 12, :n]
    tb1_o[...] = jnp.transpose(red[: up(unit_d, 8), 128:])[pat - 128 : pat - 127, :unit_d]
    tb2_o[...] = red[n : n + 1, :pat]
    w1_o[...] = gw_ref[0]
    w2_o[...] = gw_ref[1]
    b1_o[...] = jnp.where(core == 0, red[n + 1 : n + 2, :per_h], red[n + 2 : n + 3, :per_h])
    b2_o[...] = jnp.where(core == 0, red[n + 3 : n + 4, :per_c], red[n + 4 : n + 5, :per_c])
    for _, _, store in jobs:
        store.wait()


def finish(bo, gi, pool, sq, red, gw, unit_d, per_h, per_c):
    images, pat, ch = bo.shape
    ds = unit_d
    sds = jax.ShapeDtypeStruct
    rows_own, half = gw.shape[1:]
    parts = 6 if images % 6 == 0 else 1
    outs = [
        (images, pat, ch),
        (images, ch),
        (images, pat, ch),
        (2, rows_own),
        (2, rows_own),
        (ds, pat),
        (1, ds),
        (ds, pat),
        (1, pat),
        (rows_own, half),
        (1, per_h),
        (rows_own, half),
        (1, per_c),
        (1, images),
    ]
    res = pl.pallas_call(
        functools.partial(finish_kernel, (pat, unit_d, per_h, per_c)),
        out_shape=[sds(s, F32) for s in outs],
        in_specs=[ANY, ANY, VM, VM, VM, VM],
        out_specs=[ANY if len(s) == 3 else VM for s in outs],
        scratch_shapes=[
            pltpu.VMEM((2, parts, images // parts, pat, ch), BF16),
            pltpu.VMEM((2, parts, images // parts, pat, ch), F32),
            pltpu.SemaphoreType.DMA((2, parts)),
            pltpu.SemaphoreType.DMA((2, parts)),
        ],
        compiler_params=pltpu.CompilerParams(vmem_limit_bytes=VMEM_BYTES),
        name="finish",
    )(bo, gi, pool, sq, red, gw)
    res = [r.reshape(-1) if r.shape[0] == 1 else r for r in res]
    for n in (0, 2):
        res[n] = jnp.swapaxes(res[n], 1, 2)
    for n in (5, 11):
        res[n] = res[n].T
    return tuple(res)


def fused_body(
    n_dp,
    grid3,
    mixer_input,
    keep_mask,
    ln_gain,
    ln_shift,
    token_w1,
    token_b1,
    token_w2,
    token_b2,
    chan_w1,
    chan_b1,
    chan_w2,
    chan_b2,
    grad_out,
    grad_pooled,
):
    images, ch, pat = mixer_input.shape
    unit_d = token_b1.shape[0]
    half = chan_b1.shape[0]
    biases = [chan_b1, chan_b2, token_b2]
    biases = [jnp.pad(b, (0, up(b.shape[0], 128) - b.shape[0])) for b in biases]
    biases = jnp.concatenate(biases).reshape(1, -1)
    bo, gi, pool, sq, red, gw = mixer(
        n_dp,
        grid3,
        jnp.swapaxes(mixer_input, 1, 2),
        jnp.swapaxes(grad_out, 1, 2),
        grad_pooled,
        chan_w1,
        chan_w2,
        biases,
        ln_gain,
        ln_shift,
        token_w1.T,
        token_b1.reshape(1, -1),
        token_w2,
        keep_mask,
    )
    return finish(bo, gi, pool, sq, red, gw, unit_d, half // n_dp, ch // n_dp)


D = 768


epsilon = 1e-05


def gelu_exact(values_in):
    return jax.nn.gelu(values_in, approximate=False)


def gelu_slope(pre_sum, upstream):
    unused, backward = jax.vjp(gelu_exact, pre_sum)
    return backward(upstream)[0]


def channel_sums(first_term, second_term):
    return lax.psum((first_term, second_term), "tensor")


def normalize(values_in, gains, shifts):
    totals, square = channel_sums(jnp.sum(values_in, 1), jnp.sum(values_in * values_in, 1))
    average = totals / D
    spread = square / D - average * average
    scaling = lax.rsqrt(spread + epsilon)[:, None, :]
    unit_part = (values_in - average[:, None, :]) * scaling
    return (unit_part * gains[None, :, None] + shifts[None, :, None], unit_part, scaling)


def normalize_back(upstream, unit_part, scaling, gains):
    scaled = upstream * gains[None, :, None]
    totals, along_unit = channel_sums(jnp.sum(scaled, 1), jnp.sum(scaled * unit_part, 1))
    inner_part = scaled - totals[:, None, :] / D - unit_part * along_unit[:, None, :] / D
    return (scaling * inner_part, jnp.sum(upstream * unit_part, (0, 2)), jnp.sum(upstream, (0, 2)))


def body(
    mixer_input,
    keep_mask,
    ln_gain,
    ln_shift,
    token_w1,
    token_b1,
    token_w2,
    token_b2,
    chan_w1,
    chan_b1,
    chan_w2,
    chan_b2,
    grad_out,
    grad_pooled,
):
    images, channels, patches = mixer_input.shape
    full_width = channels * lax.axis_size("tensor")
    offset = lax.axis_index("tensor") * channels
    gains, shifts, weight_in, bias_in, weight_back = (
        lax.all_gather(ln_gain, "dp", axis=1, tiled=True),
        lax.all_gather(ln_shift, "dp", axis=1, tiled=True),
        lax.all_gather(token_w1, "dp", axis=1, tiled=True),
        lax.all_gather(token_b1, "dp", axis=0, tiled=True),
        lax.all_gather(token_w2, "dp", axis=0, tiled=True),
    )
    gain_own = lax.dynamic_slice_in_dim(gains, offset, channels, 1).astype(jnp.float32)
    shift_own = lax.dynamic_slice_in_dim(shifts, offset, channels, 1).astype(jnp.float32)
    kept = keep_mask.astype(jnp.float32)
    counts = jnp.sum(kept, 1)
    source = mixer_input.astype(jnp.float32)
    normed, unit_first, scale_first = normalize(source, gain_own[0], shift_own[0])
    first_low = normed.astype(jnp.bfloat16)
    token_pre = jnp.einsum(
        "bcp,ph->bch", first_low, weight_in, preferred_element_type=jnp.float32
    ) + bias_in.astype(jnp.float32)
    token_hid = gelu_exact(token_pre).astype(jnp.bfloat16)
    token_out = jnp.einsum(
        "bch,hp->bcp", token_hid, weight_back, preferred_element_type=jnp.float32
    ) + token_b2.astype(jnp.float32)
    mixture = source + token_out
    normed, unit_second, scale_second = normalize(mixture, gain_own[1], shift_own[1])
    second = normed.astype(jnp.bfloat16)
    section = lax.all_gather(second, "tensor", axis=1, tiled=True)
    pre_sum = jnp.einsum("bcp,ch->bhp", section, chan_w1, preferred_element_type=jnp.float32)
    gathered = section
    grams = jnp.einsum("bcp,bcq->bpq", section, section, preferred_element_type=jnp.float32)
    chan_pre = pre_sum
    gram_second = grams
    chan_pre = chan_pre + chan_b1.astype(jnp.float32)[None, :, None]
    chan_hid = gelu_exact(chan_pre).astype(jnp.bfloat16)
    partial_value = jnp.einsum("bhp,hc->bcp", chan_hid, chan_w2, preferred_element_type=jnp.float32)
    chan_out = (
        lax.psum_scatter(
            partial_value.astype(jnp.bfloat16), "tensor", scatter_dimension=1, tiled=True
        ).astype(jnp.float32)
        + chan_b2.astype(jnp.float32)[None, :, None]
    )
    masked = kept[:, None, :] * (mixture + chan_out)
    pooled = jnp.sum(masked, 2) / counts[:, None]
    grad_result = kept[:, None, :] * (
        grad_out.astype(jnp.float32) + grad_pooled[:, :, None] / counts[:, None, None]
    )
    grad_low = grad_result.astype(jnp.bfloat16)
    grad_chan_b2 = jnp.sum(grad_low, (0, 2), dtype=jnp.float32)
    section = lax.all_gather(grad_low, "tensor", axis=1, tiled=True)
    hid_sum = jnp.einsum("bcp,hc->bhp", section, chan_w2, preferred_element_type=jnp.float32)
    column_block = jnp.einsum("bhp,bcp->hc", chan_hid, section, preferred_element_type=jnp.float32)
    grams = jnp.einsum("bcp,bcq->bpq", section, section, preferred_element_type=jnp.float32)
    pre_grad = gelu_slope(chan_pre, hid_sum).astype(jnp.bfloat16)
    grad_chan_b1 = jnp.sum(pre_grad, (0, 2), dtype=jnp.float32)
    grad_chan_w1 = jnp.einsum("bcp,bhp->ch", gathered, pre_grad, preferred_element_type=jnp.float32)
    share_w1, share_b1, share_w2, share_b2 = (
        lax.psum_scatter(
            grad_chan_w1.astype(jnp.bfloat16), "dp", scatter_dimension=0, tiled=True
        ).astype(jnp.float32),
        lax.psum_scatter(
            grad_chan_b1.astype(jnp.bfloat16), "dp", scatter_dimension=0, tiled=True
        ).astype(jnp.float32),
        lax.psum_scatter(
            column_block.astype(jnp.bfloat16), "dp", scatter_dimension=1, tiled=True
        ).astype(jnp.float32),
        lax.psum_scatter(
            grad_chan_b2.astype(jnp.bfloat16), "dp", scatter_dimension=0, tiled=True
        ).astype(jnp.float32),
    )
    second_part = jnp.einsum("bhp,ch->bcp", pre_grad, chan_w1, preferred_element_type=jnp.float32)
    second_grad = lax.psum_scatter(
        second_part.astype(jnp.bfloat16), "tensor", scatter_dimension=1, tiled=True
    ).astype(jnp.float32)
    gram_pre = jnp.einsum("bhp,bhq->bpq", pre_grad, pre_grad, preferred_element_type=jnp.float32)
    gram_hid = jnp.einsum("bhp,bhq->bpq", chan_hid, chan_hid, preferred_element_type=jnp.float32)
    own_terms = jnp.sum(gram_second * gram_pre + gram_hid * grams, (1, 2))
    own_terms = own_terms + jnp.sum(jnp.square(jnp.sum(pre_grad, 2, dtype=jnp.float32)), 1)
    own_terms = own_terms + jnp.sum(jnp.square(jnp.sum(grad_low, 2, dtype=jnp.float32)), 1)
    example_sq = lax.psum(own_terms, "tensor")
    back_second, gain_second, shift_second = normalize_back(
        second_grad, unit_second, scale_second, gain_own[1]
    )
    mixture_grad = grad_result + back_second
    out_low = mixture_grad.astype(jnp.bfloat16)
    grad_token_b2 = jnp.sum(out_low, (0, 1), dtype=jnp.float32)
    token_hid_grad = jnp.einsum(
        "bcp,hp->bch", out_low, weight_back, preferred_element_type=jnp.float32
    )
    grad_token_w2 = jnp.einsum(
        "bch,bcp->hp", token_hid, out_low, preferred_element_type=jnp.float32
    )
    token_pre_grad = gelu_slope(token_pre, token_hid_grad).astype(jnp.bfloat16)
    grad_token_b1 = jnp.sum(token_pre_grad, (0, 1), dtype=jnp.float32)
    grad_token_w1 = jnp.einsum(
        "bcp,bch->ph", first_low, token_pre_grad, preferred_element_type=jnp.float32
    )
    first_grad = jnp.einsum(
        "bch,ph->bcp", token_pre_grad, weight_in, preferred_element_type=jnp.float32
    )
    back_first, gain_first, shift_first = normalize_back(
        first_grad, unit_first, scale_first, gain_own[0]
    )
    grad_input = mixture_grad + back_first
    gain_parts = lax.dynamic_update_slice_in_dim(
        jnp.zeros((2, full_width), jnp.float32), jnp.stack([gain_first, gain_second]), offset, 1
    )
    shift_parts = lax.dynamic_update_slice_in_dim(
        jnp.zeros((2, full_width), jnp.float32), jnp.stack([shift_first, shift_second]), offset, 1
    )
    total_gain, total_shift, total_w1, total_b1, total_w2 = (
        lax.psum(gain_parts.astype(jnp.bfloat16), "tensor").astype(jnp.float32),
        lax.psum(shift_parts.astype(jnp.bfloat16), "tensor").astype(jnp.float32),
        lax.psum(grad_token_w1.astype(jnp.bfloat16), "tensor").astype(jnp.float32),
        lax.psum(grad_token_b1.astype(jnp.bfloat16), "tensor").astype(jnp.float32),
        lax.psum(grad_token_w2.astype(jnp.bfloat16), "tensor").astype(jnp.float32),
    )
    share_gain, share_shift, share_tw1, share_tb1, share_tw2 = (
        lax.psum_scatter(
            total_gain.astype(jnp.bfloat16), "dp", scatter_dimension=1, tiled=True
        ).astype(jnp.float32),
        lax.psum_scatter(
            total_shift.astype(jnp.bfloat16), "dp", scatter_dimension=1, tiled=True
        ).astype(jnp.float32),
        lax.psum_scatter(
            total_w1.astype(jnp.bfloat16), "dp", scatter_dimension=1, tiled=True
        ).astype(jnp.float32),
        lax.psum_scatter(
            total_b1.astype(jnp.bfloat16), "dp", scatter_dimension=0, tiled=True
        ).astype(jnp.float32),
        lax.psum_scatter(
            total_w2.astype(jnp.bfloat16), "dp", scatter_dimension=0, tiled=True
        ).astype(jnp.float32),
    )
    share_tb2 = lax.psum(grad_token_b2, ("dp", "tensor"))
    return (
        masked,
        pooled,
        grad_input,
        share_gain,
        share_shift,
        share_tw1,
        share_tb1,
        share_tw2,
        share_tb2,
        share_w1,
        share_b1,
        share_w2,
        share_b2,
        example_sq,
    )


def solution(mesh):
    n_dp, n_tensor = mesh.shape["dp"], mesh.shape["tensor"]
    chosen = body
    if (n_dp, n_tensor) == (16, 2):
        chosen = functools.partial(fused_body, n_dp, (4, 2, 2))
    return jax.shard_map(
        chosen,
        mesh=mesh,
        in_specs=(
            P("dp", "tensor", None),
            P("dp", None),
            P(None, "dp"),
            P(None, "dp"),
            P(None, "dp"),
            P("dp"),
            P("dp", None),
            P(),
            P(None, "tensor"),
            P("tensor"),
            P("tensor", None),
            P("tensor"),
            P("dp", "tensor", None),
            P("dp", "tensor"),
        ),
        out_specs=(
            P("dp", "tensor", None),
            P("dp", "tensor"),
            P("dp", "tensor", None),
            P(None, "dp"),
            P(None, "dp"),
            P(None, "dp"),
            P("dp"),
            P("dp", None),
            P(),
            P("dp", "tensor"),
            P(("tensor", "dp")),
            P("tensor", "dp"),
            P(("tensor", "dp")),
            P("dp"),
        ),
        check_vma=False,
    )
```

```python
import functools
import math

import jax
import jax.numpy as jnp
from jax import lax
from jax.experimental import pallas as pl
from jax.experimental.pallas import tpu as pltpu
from jax.sharding import PartitionSpec as P

MESH = pl.DeviceIdType.MESH
EPS = 1e-05
F32 = jnp.float32
BF16 = jnp.bfloat16
VM = pl.BlockSpec(memory_space=pltpu.VMEM)
ANY = pl.BlockSpec(memory_space=pl.ANY)
BLK = 256
VMEM_BYTES = 63 * 2**20


def up(n, m):
    return -(-n // m) * m


def nn(a, b):
    return lax.dot_general(a, b, (((1,), (0,)), ((), ())), preferred_element_type=F32)


def nt(a, b):
    return lax.dot_general(a, b, (((1,), (1,)), ((), ())), preferred_element_type=F32)


def tn(a, b):
    return lax.dot_general(a, b, (((0,), (0,)), ((), ())), preferred_element_type=F32)


def eye(rows, cols):
    r = lax.broadcasted_iota(jnp.int32, (rows, cols), 0)
    c = lax.broadcasted_iota(jnp.int32, (rows, cols), 1)
    return (r == c).astype(F32).astype(BF16)


def gelu_parts(v):
    cdf = 0.5 + 0.5 * lax.erf(v * math.sqrt(0.5))
    return cdf, jnp.exp(-0.5 * (v * v)) * (1.0 / math.sqrt(2.0 * math.pi))


def fold(v):
    return jnp.sum(v.reshape(v.shape[0] // 8, 8, v.shape[1]), 0)


def where_am_i():
    return lax.axis_index("dp"), lax.axis_index("tensor")


def greet_all(dp_size, dp, core):
    barrier = pltpu.get_barrier_semaphore()

    def one(n, c):
        pl.semaphore_signal(
            barrier, inc=1, device_id=(lax.rem(dp + n, dp_size), core), device_id_type=MESH
        )
        return c

    lax.fori_loop(1, dp_size, one, 0)
    pl.semaphore_signal(barrier, inc=1, device_id=(dp, 1 - core), device_id_type=MESH)
    pl.semaphore_wait(barrier, dp_size)


def remote(src, dst, send, recv, device):
    return pltpu.make_async_remote_copy(
        src_ref=src,
        dst_ref=dst,
        send_sem=send,
        recv_sem=recv,
        device_id=device,
        device_id_type=MESH,
    )


ROWS = 16


def row_pieces(pat):
    return [slice(r, min(r + ROWS, pat)) for r in range(0, pat, ROWS)]


def lane_pieces(full):
    return [slice(c, c + 256) for c in range(0, full, 256)]


def across(v, full):
    return jnp.concatenate([v] * (full // 128), axis=1)


def centre(v):
    n = v.shape[1]
    d = v - jnp.sum(v, 1, keepdims=True) * (1.0 / n)
    r = lax.rsqrt(jnp.sum(d * d, 1, keepdims=True) * (1.0 / n) + EPS)
    return d * r, r


def mixer_kernel(
    dims,
    x_hbm,
    go_hbm,
    gp_ref,
    w1_hbm,
    w2_hbm,
    b1_ref,
    cb2_ref,
    gain_ref,
    shift_ref,
    tw1_ref,
    tb1_ref,
    tw2_ref,
    tb2_ref,
    keep_ref,
    bo_hbm,
    gi_hbm,
    u0_hbm,
    f_hbm,
    hid_hbm,
    slope_hbm,
    mix_hbm,
    u1_hbm,
    pool_o,
    sq_o,
    red_o,
    gw_o,
    xf,
    gof,
    msg,
    square,
    pack,
    packf,
    tok,
    tmp_w,
    prm,
    keep_t,
    tb2_w,
    norm,
    tw,
    twt,
    st,
    yt,
    w1s,
    w2s,
    bias,
    gh,
    ph,
    gs,
    pb,
    ra,
    r1,
    b2,
    r2,
    b3,
    r3,
    us,
    fs,
    hs,
    ls,
    ms,
    vs,
    cs,
    bos,
    gis,
    sg,
    ob,
    ol,
    tg,
    fg,
    acc_norm,
    acc_tok,
    row_h,
    row_c,
    pool_a,
    pool_r,
    sq_a,
    sq_r,
    msgs,
    msgr,
    msgz,
    msgl,
    red_a,
    red_r,
    tg_s,
    tg_r,
    pair_send,
    pair_recv,
    loc_sem,
    spill,
    in_sem,
    sa,
    rsa,
    s1,
    rs1,
    s2,
    rs2,
    s3,
    rs3,
    out_s,
    out_r,
    out_l,
    tok_s,
    tok_r,
    fin_s,
    fin_r,
):
    n_dp, ni, ch, pat, tp, unit_d, nz, ny, nx = dims
    dp, core = where_am_i()
    x = lax.rem(dp, nx)
    y = lax.rem(dp // nx, ny)
    z = dp // (nx * ny)
    other = (dp, 1 - core)
    x_dev = ((z * ny + y) * nx + (1 - x), core)
    y_dev = ((z * ny + (1 - y)) * nx + x, core)
    full = 2 * ch
    rows_own = full // n_dp
    half = w1s.shape[1] // 2
    n_blk = half // BLK
    toks = ni * tp
    toks_pad = gh.shape[0]
    kp = fs.shape[1]
    my_first = core * ni
    ds = tw.shape[1]
    images = 2 * ni
    here = pl.ds(pl.multiple_of(core * ch, 128), ch)
    there = pl.ds(pl.multiple_of((1 - core) * ch, 128), ch)
    bias_rows = half // ch
    pieces = [slice(r, r + ROWS) for r in range(0, tp, ROWS)]

    ours = pl.ds(my_first, ni)
    theirs = pl.ds((1 - core) * ni, ni)
    pair_copies = [
        remote(a, b, pair_send.at[n], pair_recv.at[n], other)
        for n, (a, b) in enumerate(
            (
                (pack, packf.at[:, here]),
                (x_hbm.at[theirs], xf.at[:, :, here]),
                (go_hbm.at[theirs], gof.at[:, :, here]),
                (w2_hbm, w2s.at[pl.ds(half, half)]),
                (w1_hbm, w1s.at[:, pl.ds(half, half)]),
            )
        )
    ]
    local_copies = [
        pltpu.make_async_copy(a, b, loc_sem.at[n])
        for n, (a, b) in enumerate(
            (
                (x_hbm.at[ours], xf.at[:, :, here]),
                (go_hbm.at[ours], gof.at[:, :, here]),
                (w1_hbm, w1s.at[:, pl.ds(0, half)]),
                (w2_hbm, w2s.at[pl.ds(0, half)]),
            )
        )
    ]

    def weights_copy(n):
        to = lax.rem(dp + n, n_dp)
        return remote(msg, tok.at[dp], tg_s.at[n], tg_r.at[dp], (to, core))

    def weights_arrival(n):
        source = lax.rem(dp + n_dp - n, n_dp)
        return remote(msg, tok.at[source], tg_s.at[n], tg_r.at[source], (source, core))

    for c in local_copies:
        c.start()
    square[...] = jnp.zeros_like(square)
    at = pat - 128
    square[at : at + 1, :unit_d] = tb1_ref[...].astype(F32)
    square[at + 4 : at + 6, :rows_own] = gain_ref[...].astype(F32)
    square[at + 6 : at + 8, :rows_own] = shift_ref[...].astype(F32)
    columns = jnp.transpose(square[...])[:rows_own]
    tmp_w[0, :rows_own, :] = jnp.zeros((rows_own, kp), F32)
    tmp_w[0, :unit_d, :pat] = tw1_ref[...].astype(F32)
    tmp_w[0, unit_d:rows_own, :pat] = tw2_ref[...].astype(F32)
    msg[:, :128] = tmp_w[0, :rows_own, :128].astype(BF16)
    msg[:, 128:] = (tmp_w[0, :rows_own, 128:] + columns).astype(BF16)
    pack[...] = jnp.zeros_like(pack)
    pack[:images, :] = gp_ref[...]
    pack[images : images + 1, :] = cb2_ref[...].astype(F32).reshape(1, ch)
    b1_row = b1_ref[...].astype(F32).reshape(1, half)
    for n in range(bias_rows):
        pack[images + 1 + n : images + 2 + n, :] = b1_row[:, n * ch : (n + 1) * ch]
    greet_all(n_dp, dp, core)

    def send(n, c):
        weights_copy(n).start()
        return c

    lax.fori_loop(1, n_dp, send, 0)
    for c in pair_copies:
        c.start()

    tok[dp] = msg[...]
    packf[:, here] = pack[...]
    keep_t[...] = jnp.zeros_like(keep_t)
    keep_t[:images, :pat] = keep_ref[...].astype(F32)
    keep_t[images : images + 1, :pat] = tb2_ref[...].astype(F32).reshape(1, pat)
    turned = jnp.transpose(keep_t[...])
    keep_t[...] = turned
    tb2_w[...] = jnp.broadcast_to(turned[:tp, images : images + 1], (tp, 128))
    zero_rows = jnp.zeros((toks_pad - toks, gh.shape[1]), BF16)
    gh[toks:, :] = zero_rows
    ph[toks:, :] = zero_rows
    st[toks:, :] = zero_rows[:, :full]
    yt[toks:, :] = zero_rows[:, :full]
    for ref in (row_h, row_c, acc_norm, acc_tok, pool_a, sq_a, ol):
        ref[...] = jnp.zeros_like(ref)
    partial = row_pieces(pat)
    last = slice(pat // ROWS * ROWS, tp)
    blank = jnp.zeros((last.stop - last.start, full), BF16)
    for n in range(2):
        us[n, last, :] = blank
        vs[n, last, :] = blank
        ms[n, last, :] = blank
        fs[n, last.start :, :] = jnp.zeros((kp - last.start, full), BF16)
        fs[n, pat : pat + 1, :] = jnp.ones((1, full), BF16)
        hs[n, ds:, :] = jnp.ones((16, full), BF16)
    for c in local_copies[:2]:
        c.wait()
    for c in pair_copies[:3]:
        c.wait_recv()

    def token_rows(i, r):
        return pl.ds(pl.multiple_of(i * tp + r.start, 16), r.stop - r.start)

    def early_step(i, carry):
        number = my_first + i
        count = jnp.sum(keep_ref[pl.ds(number, 1), :].astype(F32), 1, keepdims=True)
        g = packf[pl.ds(number, 1), :] / count
        rows = token_rows(i, last)
        st[rows, :] = blank
        yt[rows, :] = blank
        cs[i, :, last, :] = jnp.zeros((3, tp - last.start, 128), F32)
        for r in partial:
            size = r.stop - r.start
            rows = token_rows(i, r)
            unit, rstd = centre(xf[i, r, :].astype(F32))
            st[rows, :] = unit.astype(BF16)
            cs[i, 0, r, :] = jnp.broadcast_to(rstd, (size, 128))
            lane = lax.broadcasted_iota(jnp.int32, (size, 128), 1)
            k = jnp.sum(jnp.where(lane == number, keep_t[r, :128], 0.0), 1, keepdims=True)
            yt[rows, :] = (k * (gof[i, r, :].astype(F32) + g)).astype(BF16)
            cs[i, 2, r, :] = jnp.broadcast_to(k, (size, 128))
        return carry

    lax.fori_loop(0, ni, early_step, 0)
    local_copies[3].wait()
    for a in range(0, half, BLK):
        ph[:toks, a : a + BLK] = nt(yt[:toks, :], w2s[a : a + BLK, :]).astype(BF16)
    for n in range(bias_rows):
        row = packf[images + 1 + n : images + 2 + n, :]
        swapped = jnp.concatenate([row[:, ch:], row[:, :ch]], axis=1)
        row = jnp.where(core == 0, row, swapped)
        bias[0:1, n * ch : (n + 1) * ch] = row[:, :ch]
        bias[0:1, half + n * ch : half + (n + 1) * ch] = row[:, ch:]

    def arrive_w(n, c):
        weights_arrival(n).wait_recv()
        return c

    lax.fori_loop(1, n_dp, arrive_w, 0)
    lane = lax.broadcasted_iota(jnp.int32, (unit_d, kp), 1)
    for d in range(n_dp):
        block = tok[d].astype(F32)
        tmp_w[0, unit_d * d : unit_d * (d + 1), :] = jnp.where(lane <= pat, block[:unit_d], 0.0)
        tmp_w[1, unit_d * d : unit_d * (d + 1), :] = jnp.where(lane < pat, block[unit_d:], 0.0)
        prm[rows_own * d : rows_own * (d + 1), :] = tok[d, :, 128:]
    r = lax.broadcasted_iota(jnp.int32, (16, 128), 0)
    c = lax.broadcasted_iota(jnp.int32, (16, 128), 1)
    norm[...] = nt(((c - (at + 4) == r) & (r < 4)).astype(F32).astype(BF16), prm[...])
    ident = eye(kp, kp)
    for n in range(2):
        w = tmp_w[n].astype(BF16)
        tw[n] = w
        t = nt(ident, w)
        r = lax.broadcasted_iota(jnp.int32, t.shape, 0)
        twt[n] = jnp.where(r < pat, t, 0.0)[:tp].astype(BF16)

    def saved(i):
        slot = lax.rem(i, 2)
        pairs = (
            (us, u0_hbm),
            (fs, f_hbm),
            (hs, hid_hbm),
            (ls, slope_hbm),
            (vs, u1_hbm),
            (ms, mix_hbm),
        )
        return [
            pltpu.make_async_copy(a.at[slot, pl.ds(0, b.shape[1])], b.at[i], spill.at[slot, n])
            for n, (a, b) in enumerate(pairs)
        ]

    def token_step(i, carry):
        slot = lax.rem(i, 2)

        @pl.when(i >= 2)
        def _():
            for c in saved(i - 2):
                c.wait()

        for r in partial:
            unit = st[token_rows(i, r), :]
            us[slot, r, :] = unit
            f = unit.astype(F32) * norm[0:1, :] + norm[2:3, :]
            fs[slot, r, :] = f.astype(BF16)
        for c in lane_pieces(full):
            pre = nn(tw[0], fs[slot, :, c])
            for a in range(0, ds, 32):
                v = pre[a : a + 32]
                cdf, pdf = gelu_parts(v)
                hs[slot, a : a + 32, c] = (v * cdf).astype(BF16)
                ls[slot, a : a + 32, c] = (cdf + v * pdf).astype(BF16)
            ob[:, c] = nn(twt[1], hs[slot, :ds, c])
        for r in partial:
            v = xf[i, r, :].astype(F32) + (ob[r, :] + across(tb2_w[r, :], full))
            ms[slot, r, :] = v.astype(BF16)
            unit, rstd = centre(v)
            vs[slot, r, :] = unit.astype(BF16)
            st[token_rows(i, r), :] = (unit * norm[1:2, :] + norm[3:4, :]).astype(BF16)
            cs[i, 1, r, :] = jnp.broadcast_to(rstd, (r.stop - r.start, 128))
        for c in saved(i):
            c.start()
        return carry

    lax.fori_loop(0, ni, token_step, 0)
    for i in (ni - 2, ni - 1):
        for c in saved(i):
            c.wait()
    local_copies[2].wait()
    for c in pair_copies[3:]:
        c.wait_recv()

    def image_loads(i, slot):
        pairs = ((u0_hbm, us), (f_hbm, fs), (hid_hbm, hs), (slope_hbm, ls), (u1_hbm, vs))
        return [
            pltpu.make_async_copy(a.at[i], b.at[slot, pl.ds(0, a.shape[1])], in_sem.at[slot, n])
            for n, (a, b) in enumerate(pairs)
        ]

    def late_loads(i, slot):
        return [pltpu.make_async_copy(mix_hbm.at[i], ms.at[slot], in_sem.at[slot, 5])]

    for c in image_loads(0, 0):
        c.start()
    for c in late_loads(0, 0):
        c.start()

    def pair_copy(slot):
        return remote(pb, ra.at[slot], sa.at[0], rsa.at[slot], other)

    def first_copies(j):
        slot = lax.rem(j, 2)
        return (
            remote(
                gs.at[slot, 0, :, :, 1 - x], r1.at[j, 0], s1.at[slot, 0], rs1.at[j, 0], x_dev
            ),
            remote(gs.at[slot, 1, :, 1 - y], r1.at[j, 1], s1.at[slot, 1], rs1.at[j, 1], y_dev),
        )

    def second_copies(j):
        slot = lax.rem(j, 2)
        return (
            remote(b2.at[slot, 0, :, 1 - y], r2.at[j, 0], s2.at[slot, 0], rs2.at[j, 0], y_dev),
            remote(b2.at[slot, 1, :, 1 - x], r2.at[j, 1], s2.at[slot, 1], rs2.at[j, 1], x_dev),
        )

    def third_copies(j):
        slot = lax.rem(j, 2)
        out = []
        for n in range(1, nz):
            to = lax.rem(z + n, nz)
            out.append(
                remote(
                    b3.at[slot, to],
                    r3.at[j, n - 1],
                    s3.at[slot, n - 1],
                    rs3.at[j, n - 1],
                    ((to * ny + y) * nx + x, core),
                )
            )
        return out

    def finish_third(j):
        slot = lax.rem(j, 2)
        for c in third_copies(j):
            c.wait()
        at = pl.ds(pl.multiple_of(j * BLK, BLK), BLK)
        for m in range(2):
            v = b3[slot, z, m].astype(F32)
            for n in range(nz - 1):
                v = v + r3[j, n, m].astype(F32)
            gw_o[m, :, at] = v

    def finish_second(j):
        slot, into = lax.rem(j, 2), lax.rem(j, 2)
        for c in second_copies(j):
            c.wait()
        for m, mine in ((0, y), (1, x)):
            for k in range(nz):
                v = b2[slot, m, k, mine].astype(F32) + r2[j, m, k].astype(F32)
                b3[into, k, m] = v.astype(BF16)
        for c in third_copies(j):
            c.start()

    def finish_first(j):
        slot, into = lax.rem(j, 2), lax.rem(j, 2)
        for c in first_copies(j):
            c.wait()
        for k in range(nz):
            for n in range(2):
                v = gs[slot, 0, k, n, x].astype(F32) + r1[j, 0, k, n].astype(F32)
                b2[into, 0, k, n] = v.astype(BF16)
                v = gs[slot, 1, k, y, n].astype(F32) + r1[j, 1, k, n].astype(F32)
                b2[into, 1, k, n] = v.astype(BF16)
        for c in second_copies(j):
            c.start()

    def hidden_block(side, j):
        col = pl.ds(pl.multiple_of(side * half + j * BLK, BLK), BLK)
        w1 = w1s[:, col]
        w2 = w2s[col, :]
        b_row = bias[0:1, col]
        for i0 in range(0, ni, 2):
            both = slice(i0 * tp, (i0 + 2) * tp)
            pre = nn(st[both, :], w1)
            if side == 1:
                up_grad = nt(yt[both, :], w2)
            for i in (i0, i0 + 1):
                acc = jnp.zeros((8, BLK), F32)
                for a in range(0, tp, 16):
                    r = slice(i * tp + a, i * tp + a + 16)
                    q = slice(r.start - both.start, r.stop - both.start)
                    v = pre[q] + b_row
                    cdf, pdf = gelu_parts(v)
                    gh[r, col] = (v * cdf).astype(BF16)
                    p = up_grad[q] if side == 1 else ph[r, col].astype(F32)
                    p = p * (cdf + v * pdf)
                    ph[r, col] = p.astype(BF16)
                    acc += fold(p)
                row = jnp.sum(acc, 0, keepdims=True)
                row_h[0:1, col] += row
                row_h[1 + i : 2 + i, col] = row
        return tn(st[...], ph[:, col]), tn(yt[...], gh[:, col])

    def due(*work):
        for step, j, exists in work:

            @pl.when(exists)
            def _():
                step(j)

    def split(v, k):
        per = full // nz
        return v[k * per : (k + 1) * per].reshape(ny, nx, rows_own, BLK)

    def block_step(j, carry):
        slot = lax.rem(j, 2)
        for m, v in enumerate(hidden_block(1, j)):
            for k in range(nz):
                pb[m, k] = split(v, k).astype(BF16)
        pair_copy(slot).start()
        due(
            (finish_third, j - 5, j >= 5),
            (finish_first, j - 2, j >= 2),
        )
        grads = hidden_block(0, j)
        pair_copy(slot).wait()
        for m, v in enumerate(grads):
            for k in range(nz):
                gs[slot, m, k] = (split(v, k) + ra[slot, m, k].astype(F32)).astype(BF16)
        for c in first_copies(j):
            c.start()
        due((finish_second, j - 3, j >= 3))
        return carry

    lax.fori_loop(0, n_blk, block_step, 0)

    def out_copies(n, i):
        src, dst = ((bos, bo_hbm), (gis, gi_hbm))[n]
        slot = lax.rem(i, 2)
        to = dst.at[my_first + i]
        return (
            remote(src.at[slot, :, there], to, out_s.at[slot, n], out_r.at[i, n], other),
            pltpu.make_async_copy(src.at[slot, :, here], to, out_l.at[slot, n]),
        )

    def out_start(n, i):
        for c in out_copies(n, i):
            c.start()

    def out_sent(n, i):
        away, local = out_copies(n, i)
        away.wait_send()
        local.wait()

    def out_arrived(n, i):
        src, dst = ((bos, bo_hbm), (gis, gi_hbm))[n]
        remote(
            src.at[0, :, there],
            dst.at[(1 - core) * ni + i],
            out_s.at[0, n],
            out_r.at[i, n],
            other,
        ).wait_recv()

    def store_rows(ref, slot, r, v):
        stop = min(r.stop, pat)
        ref[slot, r.start : stop, :] = v[: stop - r.start].astype(BF16)

    def backward_step(i, carry):
        slot = lax.rem(i, 2)
        due(
            (finish_third, n_blk - 3, i == 5),
            (finish_second, n_blk - 3, i == 0),
            (finish_second, n_blk - 2, i == 5),
            (finish_first, n_blk - 1, i == 3),
        )

        @pl.when(i + 1 < ni)
        def _():
            for c in image_loads(i + 1, 1 - slot):
                c.start()

        for c in image_loads(i, slot):
            c.wait()

        @pl.when(i >= 2)
        def _():
            out_sent(1, i - 2)

        zero8 = jnp.zeros((8, full), F32)
        dy, gain, shift = zero8, zero8, zero8
        for r in pieces:
            e_rows = token_rows(i, r)
            grad = sg[e_rows, :].astype(F32)
            unit = vs[slot, r, :].astype(F32)
            gain += fold(grad * unit)
            shift += fold(grad)
            e = grad * norm[1:2, :]
            m = jnp.sum(e, 1, keepdims=True) * (1.0 / full)
            n = jnp.sum(e * unit, 1, keepdims=True) * (1.0 / full)
            v = yt[e_rows, :].astype(F32)
            dy += fold(v)
            v = v + across(cs[i, 1, r, :], full) * (e - m - unit * n)
            ob[r, :] = v
            ol[r, :] = v.astype(BF16)
        dy = jnp.sum(dy, 0, keepdims=True)
        row_c[0:1, :] += dy
        row_c[pl.ds(1 + i, 1), :] = dy
        acc_norm[1] += gain
        acc_norm[3] += shift
        hg = nn(tw[1], ol[...])
        acc_tok[1] += nt(hs[slot], ol[...])
        for a in range(0, ds, 16):
            r = slice(a, a + 16)
            tg[r, :] = (hg[r] * ls[slot, r, :].astype(F32)).astype(BF16)
        acc_tok[0, :ds] += nt(tg[...], fs[slot])
        fg[...] = nn(twt[0], tg[...])
        gain, shift = zero8, zero8
        for r in pieces:
            g = fg[r, :]
            unit = us[slot, r, :].astype(F32)
            gain += fold(g * unit)
            shift += fold(g)
            e = g * norm[0:1, :]
            m = jnp.sum(e, 1, keepdims=True) * (1.0 / full)
            n = jnp.sum(e * unit, 1, keepdims=True) * (1.0 / full)
            v = ob[r, :] + across(cs[i, 0, r, :], full) * (e - m - unit * n)
            store_rows(gis, slot, r, v)
        acc_norm[0] += gain
        acc_norm[2] += shift
        out_start(1, i)
        return carry

    part = toks // 3
    for n in range(3):
        if n == 1:
            finish_third(n_blk - 5)
        if n == 2:
            finish_third(n_blk - 4)
            finish_first(n_blk - 2)
        a = n * part
        sg[a : a + part, :] = nt(ph[a : a + part, :], w1s[...]).astype(BF16)
    lax.fori_loop(0, ni, backward_step, 0)
    h_0 = jnp.where(core == 0, row_h[0:1, :half], row_h[0:1, half:])
    h_1 = jnp.where(core == 0, row_h[0:1, half:], row_h[0:1, :half])
    norms = jnp.concatenate([jnp.sum(acc_norm[n], 0, keepdims=True) for n in range(4)], 0)
    norms = jnp.concatenate([norms, jnp.zeros((4, full), F32)], 0)
    per_h = half // n_dp
    per_c = ch // n_dp
    tail = msgs.shape[3] - 2 * unit_d

    def cut(v, start, size):
        n = v.shape[1]
        a = min(start // 128 * 128, n - 256)
        v = v[:, a : a + 256]
        if v.shape[0] == 1:
            v = jnp.broadcast_to(v, (8, 256))
        if start > a:
            v = pltpu.roll(v, 256 - (start - a), 1)
        lane = lax.broadcasted_iota(jnp.int32, v.shape, 1)
        return jnp.where(lane < size, v, 0.0)

    for d in range(n_dp):
        place = (d // (ny * nx), d // nx % ny, d % nx)
        top = jnp.concatenate(
            [
                acc_tok[0, unit_d * d : unit_d * (d + 1), :],
                acc_tok[1, unit_d * d : unit_d * (d + 1), :],
            ],
            axis=0,
        )
        msgs[place + (slice(0, 2 * unit_d),)] = top.astype(BF16)
        extra = jnp.concatenate(
            [
                acc_tok[1, ds : ds + 1, :],
                cut(h_0, per_h * d, per_h)[0:1],
                cut(h_1, per_h * d, per_h)[0:1],
                cut(row_c[0:1, :], per_c * d, per_c)[0:1],
                cut(row_c[0:1, :], ch + per_c * d, per_c)[0:1],
                jnp.zeros((3, kp), F32),
                cut(norms, rows_own * d, rows_own),
            ],
            axis=0,
        )
        msgs[place + (slice(2 * unit_d, None),)] = extra.astype(BF16)

    plane_copies = []
    for n, (ay, ax) in enumerate(((0, 1), (1, 0), (1, 1))):
        to_y = 1 - y if ay else y
        to_x = 1 - x if ax else x
        plane_copies.append(
            remote(
                msgs.at[:, to_y, to_x],
                msgr.at[n],
                tok_s.at[n],
                tok_r.at[n],
                ((z * ny + to_y) * nx + to_x, core),
            )
        )
    line_copies = []
    for n in range(1, nz):
        to_z = lax.rem(z + n, nz)
        line_copies.append(
            remote(
                msgz.at[to_z],
                msgl.at[n - 1],
                tok_s.at[n + 2],
                tok_r.at[n + 2],
                ((to_z * ny + y) * nx + x, core),
            )
        )
    red_copy = remote(red_a, red_r, fin_s.at[2], fin_r.at[2], other)

    def plane_sum():
        for c in plane_copies:
            c.wait()
        for n in range(nz):
            v = msgs[n, y, x].astype(F32)
            for m in range(3):
                v = v + msgr[m, n].astype(F32)
            msgz[n] = v.astype(BF16)
        for c in line_copies:
            c.start()

    def line_sum():
        for c in line_copies:
            c.wait()
        v = msgz[z].astype(F32)
        for n in range(nz - 1):
            v = v + msgl[n].astype(F32)
        red_a[...] = v
        red_copy.start()

    for c in plane_copies:
        c.start()

    def gram_step(i, carry):
        due(
            (finish_third, n_blk - 2, i == 0),
            (finish_third, n_blk - 1, i == 3),
            (lambda j: line_sum(), 0, i == 4),
        )
        r = token_rows(i, slice(0, tp))
        g, p, s, dy = gh[r, :], ph[r, :], st[r, :], yt[r, :]
        both = nt(s, s) * nt(p, p) + nt(g, g) * nt(dy, dy)
        sq = jnp.sum(jnp.sum(both, 0, keepdims=True), 1, keepdims=True)
        rh = row_h[pl.ds(1 + i, 1), :]
        rc = row_c[pl.ds(1 + i, 1), :]
        sq = sq + jnp.sum(rh * rh, 1, keepdims=True) + jnp.sum(rc * rc, 1, keepdims=True)
        lane = lax.broadcasted_iota(jnp.int32, (1, 128), 1)
        sq_a[0:1, :] += jnp.where(lane == my_first + i, sq, 0.0)
        return carry

    def forward_step(i, carry):
        slot = lax.rem(i, 2)

        @pl.when(i + 1 < ni)
        def _():
            for c in late_loads(i + 1, 1 - slot):
                c.start()

        for c in late_loads(i, slot):
            c.wait()

        @pl.when(i >= 2)
        def _():
            out_sent(0, i - 2)

        chan_bias = packf[images : images + 1, :]
        pool = jnp.zeros((8, full), F32)
        kept_sum = jnp.zeros((8, 128), F32)
        for r in pieces:
            kept = cs[i, 2, r, :]
            kept_sum += fold(kept)
            out = sg[token_rows(i, r), :].astype(F32)
            bo = across(kept, full) * (ms[slot, r, :].astype(F32) + (out + chan_bias))
            pool += fold(bo)
            store_rows(bos, slot, r, bo)
        count = jnp.sum(kept_sum, 0, keepdims=True)
        pool_a[pl.ds(my_first + i, 1), :] = jnp.sum(pool, 0, keepdims=True) / across(count, full)
        out_start(0, i)
        return carry

    finish_second(n_blk - 1)
    for a in range(0, toks, part):
        sg[a : a + part, :] = nn(gh[a : a + part, :], w2s[...]).astype(BF16)
    lax.fori_loop(0, ni, forward_step, 0)
    pool_copy = remote(pool_a.at[:, there], pool_r, fin_s.at[0], fin_r.at[0], other)
    pool_copy.start()
    plane_sum()
    lax.fori_loop(0, ni, gram_step, 0)
    sq_copy = remote(sq_a, sq_r, fin_s.at[1], fin_r.at[1], other)
    sq_copy.start()

    def sent_w(n, c):
        weights_copy(n).wait_send()
        return c

    lax.fori_loop(1, n_dp, sent_w, 0)
    for c in pair_copies:
        c.wait_send()
    for n in range(2):
        for i in (ni - 2, ni - 1):
            out_sent(n, i)
        for i in range(ni):
            out_arrived(n, i)
    pool_copy.wait()
    sq_copy.wait()
    pool_o[...] = pool_a[:, here] + pool_r[...]
    sq_o[...] = sq_a[...] + sq_r[...]
    red_copy.wait()
    red_o[...] = red_a[...] + red_r[...]


def mixer(n_dp, grid3, x, go, gp, w1, w2, b1, cb2, gain, shift, tw1, tb1, tw2, tb2, keep):
    images, pat, ch = x.shape
    ni = images // 2
    full = 2 * ch
    half = w1.shape[1]
    unit_d = tw1.shape[0]
    ds = unit_d * n_dp
    tp = up(pat, 16)
    kp = up(pat, 256)
    toks_pad = up(ni * tp, 256)
    n_pack = up(images + 1 + half // ch, 8)
    n_img = up(images, 8)
    nz, ny, nx = grid3
    rows_own = full // n_dp
    n_msg = 2 * unit_d + 16
    n_blk = half // BLK
    sds = jax.ShapeDtypeStruct
    vm = pltpu.VMEM
    dma = pltpu.SemaphoreType.DMA
    part = (nz, ny, nx, rows_own, BLK)
    outs = [
        (sds((images, pat, ch), BF16), ANY),
        (sds((images, pat, ch), BF16), ANY),
        (sds((ni, tp, full), BF16), ANY),
        (sds((ni, kp, full), BF16), ANY),
        (sds((ni, ds, full), BF16), ANY),
        (sds((ni, ds, full), BF16), ANY),
        (sds((ni, tp, full), BF16), ANY),
        (sds((ni, tp, full), BF16), ANY),
        (sds((n_img, ch), F32), VM),
        (sds((8, 128), F32), VM),
        (sds((n_msg, kp), F32), VM),
        (sds((2, rows_own, half), F32), VM),
    ]
    res = pl.pallas_call(
        functools.partial(mixer_kernel, (n_dp, ni, ch, pat, tp, unit_d, nz, ny, nx)),
        out_shape=[o[0] for o in outs],
        in_specs=[ANY, ANY, VM, ANY, ANY] + [VM] * 9,
        out_specs=[o[1] for o in outs],
        scratch_shapes=[
            vm((ni, pat, full), BF16),
            vm((ni, pat, full), BF16),
            vm((2 * unit_d, kp), BF16),
            vm((128, 128), F32),
            vm((n_pack, ch), F32),
            vm((n_pack, full), F32),
            vm((n_dp, 2 * unit_d, kp), BF16),
            vm((2, ds, kp), F32),
            vm((full, 128), BF16),
            vm((kp, kp), F32),
            vm((tp, 128), F32),
            vm((16, full), F32),
            vm((2, ds, kp), BF16),
            vm((2, tp, ds), BF16),
            vm((toks_pad, full), BF16),
            vm((toks_pad, full), BF16),
            vm((full, 2 * half), BF16),
            vm((2 * half, full), BF16),
            vm((8, 2 * half), F32),
            vm((toks_pad, 2 * half), BF16),
            vm((toks_pad, 2 * half), BF16),
            vm((2, 2) + part, BF16),
            vm((2,) + part, BF16),
            vm((2, 2) + part, BF16),
            vm((n_blk, 2, nz, 2, rows_own, BLK), BF16),
            vm((2, 2, nz, 2, rows_own, BLK), BF16),
            vm((n_blk, 2, nz, rows_own, BLK), BF16),
            vm((2, nz, 2, rows_own, BLK), BF16),
            vm((n_blk, nz - 1, 2, rows_own, BLK), BF16),
            vm((2, tp, full), BF16),
            vm((2, kp, full), BF16),
            vm((2, ds + 16, full), BF16),
            vm((2, ds, full), BF16),
            vm((2, tp, full), BF16),
            vm((2, tp, full), BF16),
            vm((ni, 3, tp, 128), F32),
            vm((2, pat, full), BF16),
            vm((2, pat, full), BF16),
            vm((ni * tp, full), BF16),
            vm((tp, full), F32),
            vm((kp, full), BF16),
            vm((ds, full), BF16),
            vm((tp, full), F32),
            vm((4, 8, full), F32),
            vm((2, ds + 16, kp), F32),
            vm((8, 2 * half), F32),
            vm((8, full), F32),
            vm((n_img, full), F32),
            vm((n_img, ch), F32),
            vm((8, 128), F32),
            vm((8, 128), F32),
            vm((nz, ny, nx, n_msg, kp), BF16),
            vm((3, nz, n_msg, kp), BF16),
            vm((nz, n_msg, kp), BF16),
            vm((nz - 1, n_msg, kp), BF16),
            vm((n_msg, kp), F32),
            vm((n_msg, kp), F32),
            dma((n_dp,)),
            dma((n_dp,)),
            dma((5,)),
            dma((5,)),
            dma((4,)),
            dma((2, 6)),
            dma((2, 6)),
            dma((1,)),
            dma((2,)),
            dma((2, 2)),
            dma((n_blk, 2)),
            dma((2, 2)),
            dma((n_blk, 2)),
            dma((2, nz - 1)),
            dma((n_blk, nz - 1)),
            dma((2, 2)),
            dma((ni, 2)),
            dma((2, 2)),
            dma((nz + 2,)),
            dma((nz + 2,)),
            dma((3,)),
            dma((3,)),
        ],
        compiler_params=pltpu.CompilerParams(
            collective_id=0, has_side_effects=True, vmem_limit_bytes=VMEM_BYTES
        ),
        name="mixer",
    )(x, go, gp, w1, w2, b1, cb2, gain, shift, tw1, tb1, tw2, tb2, keep)
    return res[:2] + res[8:]


def finish_kernel(
    dims,
    bo_hbm,
    gi_hbm,
    pool_ref,
    sq_ref,
    red_ref,
    gw_hbm,
    bo_out,
    pool_o,
    gi_out,
    gain_o,
    shift_o,
    tw1_o,
    tb1_o,
    tw2_o,
    tb2_o,
    w1_out,
    b1_o,
    w2_out,
    b2_o,
    sq_o,
    narrow,
    broad,
    gw,
    in_sem,
    out_sem,
    gw_sem,
):
    pat, unit_d, per_h, per_c = dims
    _, core = where_am_i()
    parts = narrow.shape[1]
    jobs = []
    for n, (src, dst) in enumerate(((bo_hbm, bo_out), (gi_hbm, gi_out))):
        for m in range(parts):
            size = narrow.shape[2]
            rows = pl.ds(m * size, size)
            jobs.append(
                (
                    (n, m),
                    pltpu.make_async_copy(src.at[rows], narrow.at[n, m], in_sem.at[n, m]),
                    pltpu.make_async_copy(broad.at[n, m], dst.at[rows], out_sem.at[n, m]),
                )
            )
    load_w = pltpu.make_async_copy(gw_hbm, gw, gw_sem.at[0])
    store_w = [
        pltpu.make_async_copy(gw.at[n], dst, gw_sem.at[1 + n])
        for n, dst in enumerate((w1_out, w2_out))
    ]
    for _, load, _ in jobs:
        load.start()
    load_w.start()
    for at, load, store in jobs:
        load.wait()
        broad[at] = narrow[at].astype(F32)
        store.start()
    load_w.wait()
    for store in store_w:
        store.start()
    images = pool_o.shape[0]
    pool_o[...] = pool_ref[:images, :]
    sq_o[...] = sq_ref[0:1, :images]
    red = red_ref[...]
    n = 2 * unit_d
    tw1_o[...] = red[:unit_d, :pat]
    tw2_o[...] = red[unit_d:n, :pat]
    gain_o[...] = red[n + 8 : n + 10, :n]
    shift_o[...] = red[n + 10 : n + 12, :n]
    tb1_o[...] = jnp.transpose(red[: up(unit_d, 8), 128:])[pat - 128 : pat - 127, :unit_d]
    tb2_o[...] = red[n : n + 1, :pat]
    b1_o[...] = jnp.where(core == 0, red[n + 1 : n + 2, :per_h], red[n + 2 : n + 3, :per_h])
    b2_o[...] = jnp.where(core == 0, red[n + 3 : n + 4, :per_c], red[n + 4 : n + 5, :per_c])
    for _, _, store in jobs:
        store.wait()
    for store in store_w:
        store.wait()


def finish(bo, gi, pool, sq, red, gw, unit_d, per_h, per_c):
    images, pat, ch = bo.shape
    ds = unit_d
    sds = jax.ShapeDtypeStruct
    rows_own, half = gw.shape[1:]
    parts = 6 if images % 6 == 0 else 1
    outs = [
        (images, pat, ch),
        (images, ch),
        (images, pat, ch),
        (2, rows_own),
        (2, rows_own),
        (ds, pat),
        (1, ds),
        (ds, pat),
        (1, pat),
        (rows_own, half),
        (1, per_h),
        (rows_own, half),
        (1, per_c),
        (1, images),
    ]
    res = pl.pallas_call(
        functools.partial(finish_kernel, (pat, unit_d, per_h, per_c)),
        out_shape=[sds(s, F32) for s in outs],
        in_specs=[ANY, ANY, VM, VM, VM, ANY],
        out_specs=[ANY if n in (0, 2, 9, 11) else VM for n in range(len(outs))],
        scratch_shapes=[
            pltpu.VMEM((2, parts, images // parts, pat, ch), BF16),
            pltpu.VMEM((2, parts, images // parts, pat, ch), F32),
            pltpu.VMEM(gw.shape, F32),
            pltpu.SemaphoreType.DMA((2, parts)),
            pltpu.SemaphoreType.DMA((2, parts)),
            pltpu.SemaphoreType.DMA((3,)),
        ],
        compiler_params=pltpu.CompilerParams(vmem_limit_bytes=VMEM_BYTES),
        name="finish",
    )(bo, gi, pool, sq, red, gw)
    res = [r.reshape(-1) if r.shape[0] == 1 else r for r in res]
    for n in (0, 2):
        res[n] = jnp.swapaxes(res[n], 1, 2)
    for n in (5, 11):
        res[n] = res[n].T
    return tuple(res)


def fused_body(
    n_dp,
    grid3,
    mixer_input,
    keep_mask,
    ln_gain,
    ln_shift,
    token_w1,
    token_b1,
    token_w2,
    token_b2,
    chan_w1,
    chan_b1,
    chan_w2,
    chan_b2,
    grad_out,
    grad_pooled,
):
    images, ch, pat = mixer_input.shape
    unit_d = token_b1.shape[0]
    half = chan_b1.shape[0]
    bo, gi, pool, sq, red, gw = mixer(
        n_dp,
        grid3,
        jnp.swapaxes(mixer_input, 1, 2),
        jnp.swapaxes(grad_out, 1, 2),
        grad_pooled,
        chan_w1,
        chan_w2,
        chan_b1,
        chan_b2,
        ln_gain,
        ln_shift,
        token_w1.T,
        token_b1.reshape(1, -1),
        token_w2,
        token_b2,
        keep_mask,
    )
    return finish(bo, gi, pool, sq, red, gw, unit_d, half // n_dp, ch // n_dp)


D = 768


epsilon = 1e-05


def gelu_exact(values_in):
    return jax.nn.gelu(values_in, approximate=False)


def gelu_slope(pre_sum, upstream):
    unused, backward = jax.vjp(gelu_exact, pre_sum)
    return backward(upstream)[0]


def channel_sums(first_term, second_term):
    return lax.psum((first_term, second_term), "tensor")


def normalize(values_in, gains, shifts):
    totals, square = channel_sums(jnp.sum(values_in, 1), jnp.sum(values_in * values_in, 1))
    average = totals / D
    spread = square / D - average * average
    scaling = lax.rsqrt(spread + epsilon)[:, None, :]
    unit_part = (values_in - average[:, None, :]) * scaling
    return (unit_part * gains[None, :, None] + shifts[None, :, None], unit_part, scaling)


def normalize_back(upstream, unit_part, scaling, gains):
    scaled = upstream * gains[None, :, None]
    totals, along_unit = channel_sums(jnp.sum(scaled, 1), jnp.sum(scaled * unit_part, 1))
    inner_part = scaled - totals[:, None, :] / D - unit_part * along_unit[:, None, :] / D
    return (scaling * inner_part, jnp.sum(upstream * unit_part, (0, 2)), jnp.sum(upstream, (0, 2)))


def body(
    mixer_input,
    keep_mask,
    ln_gain,
    ln_shift,
    token_w1,
    token_b1,
    token_w2,
    token_b2,
    chan_w1,
    chan_b1,
    chan_w2,
    chan_b2,
    grad_out,
    grad_pooled,
):
    images, channels, patches = mixer_input.shape
    full_width = channels * lax.axis_size("tensor")
    offset = lax.axis_index("tensor") * channels
    gains, shifts, weight_in, bias_in, weight_back = (
        lax.all_gather(ln_gain, "dp", axis=1, tiled=True),
        lax.all_gather(ln_shift, "dp", axis=1, tiled=True),
        lax.all_gather(token_w1, "dp", axis=1, tiled=True),
        lax.all_gather(token_b1, "dp", axis=0, tiled=True),
        lax.all_gather(token_w2, "dp", axis=0, tiled=True),
    )
    gain_own = lax.dynamic_slice_in_dim(gains, offset, channels, 1).astype(jnp.float32)
    shift_own = lax.dynamic_slice_in_dim(shifts, offset, channels, 1).astype(jnp.float32)
    kept = keep_mask.astype(jnp.float32)
    counts = jnp.sum(kept, 1)
    source = mixer_input.astype(jnp.float32)
    normed, unit_first, scale_first = normalize(source, gain_own[0], shift_own[0])
    first_low = normed.astype(jnp.bfloat16)
    token_pre = jnp.einsum(
        "bcp,ph->bch", first_low, weight_in, preferred_element_type=jnp.float32
    ) + bias_in.astype(jnp.float32)
    token_hid = gelu_exact(token_pre).astype(jnp.bfloat16)
    token_out = jnp.einsum(
        "bch,hp->bcp", token_hid, weight_back, preferred_element_type=jnp.float32
    ) + token_b2.astype(jnp.float32)
    mixture = source + token_out
    normed, unit_second, scale_second = normalize(mixture, gain_own[1], shift_own[1])
    second = normed.astype(jnp.bfloat16)
    section = lax.all_gather(second, "tensor", axis=1, tiled=True)
    pre_sum = jnp.einsum("bcp,ch->bhp", section, chan_w1, preferred_element_type=jnp.float32)
    gathered = section
    grams = jnp.einsum("bcp,bcq->bpq", section, section, preferred_element_type=jnp.float32)
    chan_pre = pre_sum
    gram_second = grams
    chan_pre = chan_pre + chan_b1.astype(jnp.float32)[None, :, None]
    chan_hid = gelu_exact(chan_pre).astype(jnp.bfloat16)
    partial_value = jnp.einsum("bhp,hc->bcp", chan_hid, chan_w2, preferred_element_type=jnp.float32)
    chan_out = (
        lax.psum_scatter(
            partial_value.astype(jnp.bfloat16), "tensor", scatter_dimension=1, tiled=True
        ).astype(jnp.float32)
        + chan_b2.astype(jnp.float32)[None, :, None]
    )
    masked = kept[:, None, :] * (mixture + chan_out)
    pooled = jnp.sum(masked, 2) / counts[:, None]
    grad_result = kept[:, None, :] * (
        grad_out.astype(jnp.float32) + grad_pooled[:, :, None] / counts[:, None, None]
    )
    grad_low = grad_result.astype(jnp.bfloat16)
    grad_chan_b2 = jnp.sum(grad_low, (0, 2), dtype=jnp.float32)
    section = lax.all_gather(grad_low, "tensor", axis=1, tiled=True)
    hid_sum = jnp.einsum("bcp,hc->bhp", section, chan_w2, preferred_element_type=jnp.float32)
    column_block = jnp.einsum("bhp,bcp->hc", chan_hid, section, preferred_element_type=jnp.float32)
    grams = jnp.einsum("bcp,bcq->bpq", section, section, preferred_element_type=jnp.float32)
    pre_grad = gelu_slope(chan_pre, hid_sum).astype(jnp.bfloat16)
    grad_chan_b1 = jnp.sum(pre_grad, (0, 2), dtype=jnp.float32)
    grad_chan_w1 = jnp.einsum("bcp,bhp->ch", gathered, pre_grad, preferred_element_type=jnp.float32)
    share_w1, share_b1, share_w2, share_b2 = (
        lax.psum_scatter(
            grad_chan_w1.astype(jnp.bfloat16), "dp", scatter_dimension=0, tiled=True
        ).astype(jnp.float32),
        lax.psum_scatter(
            grad_chan_b1.astype(jnp.bfloat16), "dp", scatter_dimension=0, tiled=True
        ).astype(jnp.float32),
        lax.psum_scatter(
            column_block.astype(jnp.bfloat16), "dp", scatter_dimension=1, tiled=True
        ).astype(jnp.float32),
        lax.psum_scatter(
            grad_chan_b2.astype(jnp.bfloat16), "dp", scatter_dimension=0, tiled=True
        ).astype(jnp.float32),
    )
    second_part = jnp.einsum("bhp,ch->bcp", pre_grad, chan_w1, preferred_element_type=jnp.float32)
    second_grad = lax.psum_scatter(
        second_part.astype(jnp.bfloat16), "tensor", scatter_dimension=1, tiled=True
    ).astype(jnp.float32)
    gram_pre = jnp.einsum("bhp,bhq->bpq", pre_grad, pre_grad, preferred_element_type=jnp.float32)
    gram_hid = jnp.einsum("bhp,bhq->bpq", chan_hid, chan_hid, preferred_element_type=jnp.float32)
    own_terms = jnp.sum(gram_second * gram_pre + gram_hid * grams, (1, 2))
    own_terms = own_terms + jnp.sum(jnp.square(jnp.sum(pre_grad, 2, dtype=jnp.float32)), 1)
    own_terms = own_terms + jnp.sum(jnp.square(jnp.sum(grad_low, 2, dtype=jnp.float32)), 1)
    example_sq = lax.psum(own_terms, "tensor")
    back_second, gain_second, shift_second = normalize_back(
        second_grad, unit_second, scale_second, gain_own[1]
    )
    mixture_grad = grad_result + back_second
    out_low = mixture_grad.astype(jnp.bfloat16)
    grad_token_b2 = jnp.sum(out_low, (0, 1), dtype=jnp.float32)
    token_hid_grad = jnp.einsum(
        "bcp,hp->bch", out_low, weight_back, preferred_element_type=jnp.float32
    )
    grad_token_w2 = jnp.einsum(
        "bch,bcp->hp", token_hid, out_low, preferred_element_type=jnp.float32
    )
    token_pre_grad = gelu_slope(token_pre, token_hid_grad).astype(jnp.bfloat16)
    grad_token_b1 = jnp.sum(token_pre_grad, (0, 1), dtype=jnp.float32)
    grad_token_w1 = jnp.einsum(
        "bcp,bch->ph", first_low, token_pre_grad, preferred_element_type=jnp.float32
    )
    first_grad = jnp.einsum(
        "bch,ph->bcp", token_pre_grad, weight_in, preferred_element_type=jnp.float32
    )
    back_first, gain_first, shift_first = normalize_back(
        first_grad, unit_first, scale_first, gain_own[0]
    )
    grad_input = mixture_grad + back_first
    gain_parts = lax.dynamic_update_slice_in_dim(
        jnp.zeros((2, full_width), jnp.float32), jnp.stack([gain_first, gain_second]), offset, 1
    )
    shift_parts = lax.dynamic_update_slice_in_dim(
        jnp.zeros((2, full_width), jnp.float32), jnp.stack([shift_first, shift_second]), offset, 1
    )
    total_gain, total_shift, total_w1, total_b1, total_w2 = (
        lax.psum(gain_parts.astype(jnp.bfloat16), "tensor").astype(jnp.float32),
        lax.psum(shift_parts.astype(jnp.bfloat16), "tensor").astype(jnp.float32),
        lax.psum(grad_token_w1.astype(jnp.bfloat16), "tensor").astype(jnp.float32),
        lax.psum(grad_token_b1.astype(jnp.bfloat16), "tensor").astype(jnp.float32),
        lax.psum(grad_token_w2.astype(jnp.bfloat16), "tensor").astype(jnp.float32),
    )
    share_gain, share_shift, share_tw1, share_tb1, share_tw2 = (
        lax.psum_scatter(
            total_gain.astype(jnp.bfloat16), "dp", scatter_dimension=1, tiled=True
        ).astype(jnp.float32),
        lax.psum_scatter(
            total_shift.astype(jnp.bfloat16), "dp", scatter_dimension=1, tiled=True
        ).astype(jnp.float32),
        lax.psum_scatter(
            total_w1.astype(jnp.bfloat16), "dp", scatter_dimension=1, tiled=True
        ).astype(jnp.float32),
        lax.psum_scatter(
            total_b1.astype(jnp.bfloat16), "dp", scatter_dimension=0, tiled=True
        ).astype(jnp.float32),
        lax.psum_scatter(
            total_w2.astype(jnp.bfloat16), "dp", scatter_dimension=0, tiled=True
        ).astype(jnp.float32),
    )
    share_tb2 = lax.psum(grad_token_b2, ("dp", "tensor"))
    return (
        masked,
        pooled,
        grad_input,
        share_gain,
        share_shift,
        share_tw1,
        share_tb1,
        share_tw2,
        share_tb2,
        share_w1,
        share_b1,
        share_w2,
        share_b2,
        example_sq,
    )


def solution(mesh):
    n_dp, n_tensor = mesh.shape["dp"], mesh.shape["tensor"]
    chosen = body
    if (n_dp, n_tensor) == (16, 2):
        chosen = functools.partial(fused_body, n_dp, (4, 2, 2))
    return jax.shard_map(
        chosen,
        mesh=mesh,
        in_specs=(
            P("dp", "tensor", None),
            P("dp", None),
            P(None, "dp"),
            P(None, "dp"),
            P(None, "dp"),
            P("dp"),
            P("dp", None),
            P(),
            P(None, "tensor"),
            P("tensor"),
            P("tensor", None),
            P("tensor"),
            P("dp", "tensor", None),
            P("dp", "tensor"),
        ),
        out_specs=(
            P("dp", "tensor", None),
            P("dp", "tensor"),
            P("dp", "tensor", None),
            P(None, "dp"),
            P(None, "dp"),
            P(None, "dp"),
            P("dp"),
            P("dp", None),
            P(),
            P("dp", "tensor"),
            P(("tensor", "dp")),
            P("tensor", "dp"),
            P(("tensor", "dp")),
            P("dp"),
        ),
        check_vma=False,
    )
```
